32 devices in a mesh: batch: 8 (over y, x, core), chan: 4 (over z).
Axes of the slice: x: 2, y: 2, z: 4, core: 2. Of those that a mesh axis runs over, the one named last changes fastest.
Arguments:
- tokens: bfloat16 [32768, 768], P(('batch', 'chan')), may hold values from -6 to 6
- w_in: bfloat16 [768, 768], P(None, 'chan'), may hold values from -0.21875 to 0.21875
- w_forget: bfloat16 [768, 384], P(None, 'chan'), may hold values from -0.21875 to 0.21875
- b_forget: float32 [384], P('chan'), may hold values from 2.5 to 10
- rotation: float32 [384], P('chan'), may hold values from -3.140625 to 3.140625
- w_outgate: bfloat16 [768, 768], P(None, 'chan'), may hold values from -0.21875 to 0.21875
- gn_gain: float32 [768], P('chan'), may hold values from 0.5 to 1.5
- w_out: bfloat16 [768, 768], P('chan'), may hold values from -0.21875 to 0.21875
- rms_gain: float32 [768], replicated, may hold values from 0.5 to 1.5
- w_gate: bfloat16 [768, 1536], P(None, 'chan'), may hold values from -0.21875 to 0.21875
- w_up: bfloat16 [768, 1536], P(None, 'chan'), may hold values from -0.21875 to 0.21875
- w_down: bfloat16 [1536, 768], P('chan'), may hold values from -0.15625 to 0.15625
- cotangent: bfloat16 [32768, 768], P(('batch', 'chan')), may hold values from -6 to 6
- buckets: int32 [8], P('batch'), may hold values from 1024 to 4096, as said below
- lengths: int32 [8, 4], P('batch'), may hold values from 0 to 4096, as said below
Outputs:
- block_out: bfloat16 [32768, 768], P(('batch', 'chan'))
- grad_tokens: float32 [32768, 768], P(('batch', 'chan'))
- grad_w_in: float32 [768, 768], P(None, 'chan')
- grad_w_forget: float32 [768, 384], P(None, 'chan')
- grad_b_forget: float32 [384], P('chan')
- grad_rotation: float32 [384], P('chan')
- grad_w_outgate: float32 [768, 768], P(None, 'chan')
- grad_gn_gain: float32 [768], P('chan')
- grad_w_out: float32 [768, 768], P('chan')
- grad_rms_gain: float32 [768], P('chan')
- grad_w_gate: float32 [768, 1536], P(None, 'chan')
- grad_w_up: float32 [768, 1536], P(None, 'chan')
- grad_w_down: float32 [1536, 768], P('chan')
The draws below stay inside these ranges and needn't reach their ends.
Inputs may be any that keep to these rules, and one draw needn't show every extreme that they name: `buckets`: each group's bucket is 4096, 2048 or 1024, and the group holds 4096 // bucket sequences; the first group's bucket is 4096. `lengths`: slot j of a group is the true length of its sequence j; the group's first sequence fills its bucket, the others are longer than half the bucket and at most the bucket; slots past the group's sequences are 0.
All inputs are finite; a program needn't handle non-finite values.
Results may differ from the reference program's by a relative error of at most 0.015.
Values may be sent and summed in bfloat16 or wider, within the bound.
A program may use at most 256 MiB of HBM per device.

```python
import jax
import jax.numpy as jnp
from jax import lax

D = 768
C = 384
FF = 1536
HEAD_CH = 32
SLOTS = 4
GROUP_TOK = 4096
GROUPS = 8
TOKENS = 32768


def bucket_plan(key):
    level_pick = jax.random.randint(key, (GROUPS,), 0, 3)
    level_pick = jnp.where(jnp.arange(GROUPS) == 0, 0, level_pick)
    seq_count = jnp.left_shift(jnp.ones((GROUPS,), jnp.int32), level_pick)
    return (GROUP_TOK // seq_count, seq_count)


def draw_buckets(key, part):
    bucket_sizes, seq_count = bucket_plan(key)
    return bucket_sizes.astype(jnp.int32)


def draw_lengths(key, part):
    bucket_sizes, seq_count = bucket_plan(key)
    key = jax.random.fold_in(key, 23)
    half_bucket = bucket_sizes // 2
    offsets = jax.random.randint(key, (GROUPS, SLOTS), 0, 1 << 20) % half_bucket[:, None]
    slot_ids = jnp.arange(SLOTS)[None, :]
    lengths_out = jnp.where(slot_ids == 0, bucket_sizes[:, None], half_bucket[:, None] + 1 + offsets)
    return jnp.where(slot_ids < seq_count[:, None], lengths_out, 0).astype(jnp.int32)


def shard_levels(stream_key, extent, pieces, smallest, top_value):
    def one(dim, blocks):
        draws = jax.random.uniform(jax.random.fold_in(jax.random.fold_in(stream_key, 6), dim), (blocks,), jnp.float32, smallest / len(pieces), top_value / len(pieces))
        return jnp.repeat(jnp.exp(draws), extent[dim] // blocks).reshape((-1,) + (1,) * (len(extent) - dim - 1))

    factor_of = one(*pieces[0])
    for cut in pieces[1:]:
        factor_of = factor_of * one(*cut)
    return factor_of


def noise(key, dims, deviation, bound, cuts=(), kind=jnp.bfloat16):
    drawn = deviation * jax.random.normal(key, dims, jnp.float32)
    if cuts:
        drawn = drawn * shard_levels(key, dims, cuts, -0.22, 0.18)
    return jnp.clip(drawn, -bound, bound).astype(kind)


def setup_inputs(seed: int = 0) -> dict:
    arg_keys = jax.random.split(jax.random.key(seed), 16)
    tokens = noise(arg_keys[0], (TOKENS, D), 1.0, 6.0, ((0, 32),))
    w_in = noise(arg_keys[1], (D, 2 * C), D ** -0.5, 0.21875, ((1, 4),))
    w_forget = noise(arg_keys[2], (D, C), D ** -0.5, 0.21875, ((1, 4),))
    b_forget = jnp.clip(2.5 + 7.5 * jax.random.uniform(arg_keys[3], (C,), jnp.float32) ** shard_levels(arg_keys[3], (C,), ((0, 4),), -0.2, 0.2), 2.5, 10.0)
    rotation = jnp.clip(jax.random.uniform(arg_keys[4], (C,), jnp.float32, -3.140625, 3.140625), -3.140625, 3.140625)
    w_outgate = noise(arg_keys[5], (D, 2 * C), D ** -0.5, 0.21875, ((1, 4),))
    gn_gain = jnp.clip(1.0 + 0.1 * jax.random.normal(arg_keys[6], (2 * C,), jnp.float32), 0.5, 1.5)
    w_out = noise(arg_keys[7], (2 * C, D), (2 * C) ** -0.5, 0.21875, ((0, 4),))
    rms_gain = jnp.clip(1.0 + 0.1 * jax.random.normal(arg_keys[8], (D,), jnp.float32), 0.5, 1.5)
    w_gate = noise(arg_keys[9], (D, FF), D ** -0.5, 0.21875, ((1, 4),))
    w_up = noise(arg_keys[10], (D, FF), D ** -0.5, 0.21875, ((1, 4),))
    w_down = noise(arg_keys[11], (FF, D), FF ** -0.5, 0.15625, ((0, 4),))
    cotangent = noise(arg_keys[12], (TOKENS, D), 1.0, 6.0, ((0, 32),))
    buckets = draw_buckets(jax.random.fold_in(arg_keys[15], 71), 0)
    lengths = draw_lengths(jax.random.fold_in(arg_keys[15], 71), 0)
    return dict(tokens=tokens, w_in=w_in, w_forget=w_forget, b_forget=b_forget, rotation=rotation, w_outgate=w_outgate, gn_gain=gn_gain, w_out=w_out, rms_gain=rms_gain, w_gate=w_gate, w_up=w_up, w_down=w_down, cotangent=cotangent, buckets=buckets, lengths=lengths)


@jax.custom_vjp
def low(v):
    return lax.optimization_barrier(v.astype(jnp.bfloat16)).astype(jnp.float32)

@jax.custom_vjp
def low_back(v):
    return v

def low_keep(v):
    return (low(v), None)

def low_pass(kept, grad):
    return (grad,)

def back_keep(v):
    return (v, None)

def back_low(kept, grad):
    return (low(grad),)
low.defvjp(low_keep, low_pass)
low_back.defvjp(back_keep, back_low)

def matmul(left, right):
    return jnp.dot(left, right, precision=lax.Precision.HIGHEST)

def recurrence(rho_r, rho_i, push_r, push_i):

    def combine(former, latter):
        return (latter[0] * former[0] - latter[1] * former[1], latter[0] * former[1] + latter[1] * former[0], latter[0] * former[2] - latter[1] * former[3] + latter[2], latter[0] * former[3] + latter[1] * former[2] + latter[3])
    scanned = lax.associative_scan(combine, (rho_r, rho_i, push_r, push_i), axis=0)
    return (scanned[2], scanned[3])

def mixer_core(proj_in, proj_f, proj_g, b_forget, rotation, gn_gain, starts):
    row_count = proj_in.shape[0]
    head_count = proj_in.shape[1] // (2 * HEAD_CH)
    values_in = jax.nn.silu(proj_in).reshape(row_count, head_count, 2, HEAD_CH)
    real_in = values_in[:, :, 0, :].reshape(row_count, head_count * HEAD_CH)
    imag_in = values_in[:, :, 1, :].reshape(row_count, head_count * HEAD_CH)
    forget = jax.nn.sigmoid(proj_f + b_forget)
    keep_rate = forget * (1.0 - starts)[:, None]
    state_r, state_i = recurrence(keep_rate * jnp.cos(rotation), keep_rate * jnp.sin(rotation), (1.0 - forget) * real_in, (1.0 - forget) * imag_in)
    stacked = jnp.stack([state_r.reshape(row_count, head_count, HEAD_CH), state_i.reshape(row_count, head_count, HEAD_CH)], axis=2)
    stacked = stacked.reshape(row_count, head_count, 2 * HEAD_CH)
    gated = jax.nn.silu(proj_g).reshape(row_count, head_count, 2 * HEAD_CH) * stacked
    group_mean = lax.optimization_barrier(jnp.mean(gated, axis=-1, keepdims=True))
    centred = gated - group_mean
    variance = lax.optimization_barrier(jnp.mean(centred * centred, axis=-1, keepdims=True))
    normed = centred * lax.rsqrt(variance + 1e-05)
    return normed.reshape(row_count, head_count * 2 * HEAD_CH) * gn_gain

def row_flags(positions, bucket, seq_lengths):
    slot_index = positions // bucket
    offset = positions - slot_index * bucket
    slot_ids = jnp.arange(seq_lengths.shape[0], dtype=jnp.int32)
    onehot = slot_index[:, None] == slot_ids[None, :]
    live_limit = lax.optimization_barrier(jnp.sum(jnp.where(onehot, seq_lengths[None, :], 0), axis=1))
    return ((offset == 0).astype(jnp.float32), (offset < live_limit).astype(jnp.float32))

def forward(tokens_f, weights_f, starts):
    w_in, w_forget, b_forget, rotation, w_outgate, gn_gain, w_out, rms_gain, w_gate, w_up, w_down = weights_f
    proj_in = low_back(matmul(tokens_f, w_in))
    proj_f = low_back(matmul(tokens_f, w_forget))
    proj_g = low_back(matmul(tokens_f, w_outgate))
    norm_mix = mixer_core(proj_in, proj_f, proj_g, b_forget, rotation, gn_gain, starts)
    mixed = low_back(matmul(low(norm_mix), w_out))
    residual = tokens_f + mixed
    ffn_in = low(residual * lax.rsqrt(lax.optimization_barrier(jnp.mean(residual * residual, axis=-1, keepdims=True)) + 1e-06) * rms_gain)
    gate_act = low_back(matmul(ffn_in, w_gate))
    up_act = low_back(matmul(ffn_in, w_up))
    hidden = low(jax.nn.silu(gate_act) * up_act)
    return residual + matmul(hidden, w_down)

def reference(tokens, w_in, w_forget, b_forget, rotation, w_outgate, gn_gain, w_out, rms_gain, w_gate, w_up, w_down, cotangent, buckets, lengths):
    params = tuple((weight_arg.astype(jnp.float32) for weight_arg in (w_in, w_forget, b_forget, rotation, w_outgate, gn_gain, w_out, rms_gain, w_gate, w_up, w_down)))
    positions = jnp.arange(GROUP_TOK, dtype=jnp.int32)

    def group_step(totals, group_item):
        token_rows, cot_rows, bucket, seq_lengths = group_item
        starts, live_rows = row_flags(positions, bucket, seq_lengths)

        def forward_fn(tokens_f, *weights_f):
            return forward(tokens_f, weights_f, starts)
        out_rows, backward = jax.vjp(forward_fn, token_rows.astype(jnp.float32), *params)
        gradients = backward(cot_rows.astype(jnp.float32) * live_rows[:, None])
        totals = tuple((accum + new_term for accum, new_term in zip(totals, gradients[1:])))
        return (totals, (out_rows.astype(jnp.bfloat16), gradients[0]))
    zeros_init = tuple((jnp.zeros(weight_arg.shape, jnp.float32) for weight_arg in params))
    totals, (out_rows, grad_rows) = lax.scan(group_step, zeros_init, (tokens.reshape(GROUPS, GROUP_TOK, D), cotangent.reshape(GROUPS, GROUP_TOK, D), buckets, lengths))
    return (out_rows.reshape(TOKENS, D), grad_rows.reshape(TOKENS, D), totals[0], totals[1], totals[2], totals[3], totals[4], totals[5], totals[6], totals[7], totals[8], totals[9], totals[10])
```

```python
import functools

import jax
import jax.numpy as jnp
from jax import lax
from jax.experimental import pallas as pl
from jax.experimental.pallas import tpu as pltpu
from jax.sharding import PartitionSpec as P

MESH = pl.DeviceIdType.MESH
BF = jnp.bfloat16
F32 = jnp.float32
HEAD_CH = 32
SEGS = 16
TM = 256
MT0, WO0, WG0, WD0, PIECE = 0, 512, 704, 1472, 1856
PAD0 = 480


def dot(left, right, left_dim, right_dim):
    return lax.dot_general(
        left, right, (((left_dim,), (right_dim,)), ((), ())), preferred_element_type=F32
    )


def rows_of(tile, size):
    return pl.ds(pl.multiple_of(tile * size, size), size)


def sigmoid(v):
    return 1.0 / (1.0 + jnp.exp(-v))


def get(ref, rows, first, count):
    return jnp.concatenate([ref[first + k, rows, :] for k in range(count)], axis=1)


def put(ref, rows, first, v):
    for k in range(v.shape[1] // 128):
        ref[first + k, rows, :] = v[:, 128 * k : 128 * (k + 1)]


def fold_rows(v):
    return jnp.sum(v.reshape(v.shape[0] // 8, 8, v.shape[1]), axis=0)


def main_kernel(
    w_hbm, tok_hbm, cot_hbm, par_ref, rms_ref, bucket_ref, len_ref,
    g_hbm, gtok_hbm, out_hbm,
    w, tok, sd, pv, om, pg, ws, xh, rstd, res, fin, mix, out, dff, hid, dgu, dm, dp,
    ones, parx, carx, carb, seg, sgrad, seg_prod,
    load_sem, store_sem, par_send, par_recv, car_send, car_recv, cab_send, cab_recv,
):
    n_chan, n_rows = 4, tok.shape[0]
    width = tok.shape[1]
    half = width // 2
    lt = half // 128
    n_tiles = n_rows // TM
    seg_len = n_rows // SEGS
    b = lax.axis_index("batch")
    c = lax.axis_index("chan")
    peers = [lax.rem(c + j, n_chan) for j in range(1, n_chan)]

    loads = [
        pltpu.make_async_copy(tok_hbm, tok, load_sem.at[0]),
        pltpu.make_async_copy(w_hbm, w, load_sem.at[1]),
        pltpu.make_async_copy(cot_hbm, sd, load_sem.at[2]),
    ]
    for load in loads:
        load.start()

    barrier = pltpu.get_barrier_semaphore()
    for peer in peers:
        pl.semaphore_signal(barrier, inc=1, device_id=(b, peer), device_id_type=MESH)
    pl.semaphore_wait(barrier, n_chan - 1)

    def exchange(ref, send_sem, recv_sem):
        copies = [
            pltpu.make_async_remote_copy(
                ref.at[c], ref.at[c], send_sem.at[j], recv_sem.at[j],
                device_id=(b, peer), device_id_type=MESH,
            )
            for j, peer in enumerate(peers)
        ]
        return copies

    parx[c] = par_ref[...]
    par_copies = exchange(parx, par_send, par_recv)
    for copy in par_copies:
        copy.start()
    lane_r = lax.broadcasted_iota(jnp.int32, (half, half), 0) // HEAD_CH
    lane_c = lax.broadcasted_iota(jnp.int32, (half, half), 1) // HEAD_CH
    ones[...] = jnp.where(lane_r == lane_c, 1.0 / (2 * HEAD_CH), 0.0).astype(BF)
    sgrad[...] = jnp.zeros_like(sgrad)

    def head_mean(v):
        high = v.astype(BF)
        low = (v - high.astype(F32)).astype(BF)
        return dot(high, ones[...], 1, 0) + dot(low, ones[...], 1, 0)

    bucket = bucket_ref[0]
    base = c * n_rows
    offset = jnp.bitwise_and(base, bucket - 1)
    slot_limit = len_ref[0, 0]
    for k in range(1, len_ref.shape[1]):
        slot_limit = jnp.where(base >= k * bucket, len_ref[0, k], slot_limit)
    live_rows = slot_limit - offset
    not_start = jnp.where(offset == 0, 0.0, 1.0).astype(F32)

    for copy in par_copies:
        copy.wait()
    par = parx[0] + parx[1] + parx[2] + parx[3]
    bias = par[0:1, :]
    cos1, sin1 = par[1:2, :], par[2:3, :]
    gain_r, gain_i = par[3:4, :], par[4:5, :]
    rms_gain = rms_ref[...]
    cos16 = jnp.broadcast_to(cos1, (SEGS, half))
    sin16 = jnp.broadcast_to(sin1, (SEGS, half))

    def power(count):
        rr, ri = cos1, sin1
        while count > 1:
            rr, ri = rr * rr - ri * ri, 2.0 * rr * ri
            count //= 2
        return rr, ri

    seg_cos, seg_sin = power(seg_len)
    all_cos, all_sin = power(n_rows)

    loads[0].wait()
    loads[1].wait()

    def section(k):
        return jnp.concatenate(
            [w[cc, 96 * k : 96 * k + 96, :] for cc in range(n_chan)], axis=0
        )

    def out_rows(k):
        return jnp.concatenate(
            [w[cc, WO0 + 96 * k : WO0 + 96 * k + 96, :] for cc in range(n_chan)], axis=0
        )

    @pl.loop(0, n_tiles)
    def _(i):
        rows = rows_of(i, TM)
        x = tok[rows, :]
        for k in range(2):
            pre = dot(x, section(k), 1, 1)
            pv[rows, k * half : (k + 1) * half] = pre
            put(out, rows, k * lt, pre * sigmoid(pre))
        put(om, rows, 0, 1.0 / (1.0 + jnp.exp(dot(x, section(2), 1, 1) + bias)))

    def strided(t):
        return pl.ds(t, SEGS, stride=seg_len)

    def first(t, carry):
        sr, si, prod = carry
        o = get(om, strided(t), 0, lt)
        f = 1.0 - o
        vr = get(out, strided(t), 0, lt)
        vi = get(out, strided(t), lt, lt)
        tr = cos16 * sr - sin16 * si
        ti = sin16 * sr + cos16 * si
        return f * tr + o * vr, f * ti + o * vi, prod * f

    zero = jnp.zeros((SEGS, half), F32)
    end_r, end_i, prod = lax.fori_loop(
        0, seg_len, first, (zero, zero, jnp.ones((SEGS, half), F32)), unroll=4
    )
    seg[0] = end_r
    seg[1] = end_i
    seg_prod[...] = prod

    def fold_forward(cr, ci, keep):
        total = jnp.ones((1, half), F32)
        for s in range(SEGS):
            if keep:
                seg[2, s : s + 1, :] = cr
                seg[3, s : s + 1, :] = ci
            p = seg_prod[s : s + 1, :]
            ar, ai = p * seg_cos, p * seg_sin
            cr, ci = (
                ar * cr - ai * ci + seg[0, s : s + 1, :],
                ar * ci + ai * cr + seg[1, s : s + 1, :],
            )
            total = total * p
        return cr, ci, total

    zrow = jnp.zeros((1, half), F32)
    er, ei, total = fold_forward(zrow, zrow, False)
    carx[c, 0:1, :] = er
    carx[c, 1:2, :] = ei
    carx[c, 2:3, :] = total * all_cos * not_start
    carx[c, 3:4, :] = total * all_sin * not_start
    car_copies = exchange(carx, car_send, car_recv)
    for copy in car_copies:
        copy.start()

    @pl.loop(0, n_tiles)
    def _(i):
        rows = rows_of(i, TM)
        x = tok[rows, :]
        for k in range(2):
            pg[rows, k * half : (k + 1) * half] = dot(x, section(3 + k), 1, 1)

    for copy in car_copies:
        copy.wait()
    cr, ci = zrow, zrow
    for k in range(n_chan - 1):
        ar, ai = carx[k, 2:3, :], carx[k, 3:4, :]
        nr = ar * cr - ai * ci + carx[k, 0:1, :]
        ni = ar * ci + ai * cr + carx[k, 1:2, :]
        cr = jnp.where(k < c, nr, cr)
        ci = jnp.where(k < c, ni, ci)
    fold_forward(cr * not_start, ci * not_start, True)

    def second(t, carry):
        sr, si = carry
        o = get(om, strided(t), 0, lt)
        f = 1.0 - o
        vr = get(out, strided(t), 0, lt)
        vi = get(out, strided(t), lt, lt)
        tr = cos16 * sr - sin16 * si
        ti = sin16 * sr + cos16 * si
        put(ws, strided(t), 0, tr)
        put(ws, strided(t), lt, ti)
        return f * tr + o * vr, f * ti + o * vi

    lax.fori_loop(0, seg_len, second, (seg[2], seg[3]), unroll=4)

    @pl.loop(0, n_tiles)
    def _(i):
        rows = rows_of(i, TM)
        o = get(om, rows, 0, lt)
        f = 1.0 - o
        gr, gi = pg[rows, :half], pg[rows, half:]
        yr = gr * sigmoid(gr) * (f * get(ws, rows, 0, lt) + o * get(out, rows, 0, lt))
        yi = gi * sigmoid(gi) * (f * get(ws, rows, lt, lt) + o * get(out, rows, lt, lt))
        mean = head_mean(yr + yi)
        yr, yi = yr - mean, yi - mean
        inv = lax.rsqrt(head_mean(yr * yr + yi * yi) + 1e-5)
        yr, yi = yr * inv, yi * inv
        rstd[rows, :] = inv
        xh[rows, :half] = yr
        xh[rows, half:] = yi
        lr, li = (yr * gain_r).astype(BF), (yi * gain_i).astype(BF)
        mix[rows, :half] = lr
        mix[rows, half:] = li
        r = tok[rows, :].astype(F32) + (
            dot(lr, out_rows(0), 1, 0) + dot(li, out_rows(1), 1, 0)
        )
        res[rows, :] = r
        put(out, rows, 0, r)
        rinv = lax.rsqrt(jnp.mean(r * r, axis=1, keepdims=True) + 1e-6)
        fin[rows, :] = (r * rinv * rms_gain).astype(BF)
        dff[rows, :] = jnp.zeros((TM, width), F32)

    loads[2].wait()

    @pl.loop(0, n_tiles)
    def _(i):
        rows = rows_of(i, TM)
        place = lax.broadcasted_iota(jnp.int32, (TM, 1), 0) + i * TM
        live = jnp.where(place < live_rows, 1.0, 0.0)
        sd[rows, :] = (sd[rows, :].astype(F32) * live).astype(BF)

    hw = hid.shape[1]

    @pl.loop(0, n_chan)
    def _(j):
        cc = lax.rem(c + j, n_chan)

        @pl.loop(0, n_tiles)
        def _(i):
            rows = rows_of(i, TM)
            gate_up = dot(fin[rows, :], w[cc, WG0:WD0, :], 1, 1)
            d_hid = dot(sd[rows, :], w[cc, WD0:PIECE, :], 1, 1)
            gate, up = gate_up[:, :hw], gate_up[:, hw:]
            sig = sigmoid(gate)
            act = gate * sig
            h = (act * up).astype(BF)
            hid[rows, :] = h
            dg = (d_hid * up * (sig + act * (1.0 - sig))).astype(BF)
            du = (d_hid * act).astype(BF)
            dgu[rows, :hw] = dg
            dgu[rows, hw:] = du
            put(out, rows, 0, get(out, rows, 0, 2 * lt) + dot(h, w[cc, WD0:PIECE, :], 1, 0))
            dff[rows, :] += dot(dgu[rows, :], w[cc, WG0:WD0, :], 1, 0)

        for k in range(2):
            w[cc, WG0 + hw * k : WG0 + hw * (k + 1), :] = dot(
                dgu[:, hw * k : hw * (k + 1)], fin[...], 0, 0
            ).astype(BF)
        w[cc, WD0:PIECE, :] = dot(hid[...], sd[...], 0, 0).astype(BF)

    @pl.loop(0, n_tiles)
    def _(i):
        rows = rows_of(i, TM)
        fin[rows, :] = get(out, rows, 0, 2 * lt).astype(BF)
        r = res[rows, :]
        rinv = lax.rsqrt(jnp.mean(r * r, axis=1, keepdims=True) + 1e-6)
        rhat = r * rinv
        d = dff[rows, :]
        sgrad[2] += fold_rows(d * rhat)
        t = d * rms_gain
        dres = sd[rows, :].astype(F32) + rinv * (
            t - rhat * jnp.mean(t * rhat, axis=1, keepdims=True)
        )
        dff[rows, :] = dres
        low = dres.astype(BF)
        dm[rows, :] = low
        dr = dot(low, out_rows(0), 1, 1)
        di = dot(low, out_rows(1), 1, 1)
        xr, xi = xh[rows, :half], xh[rows, half:]
        sgrad[1, :, :half] += fold_rows(dr * xr)
        sgrad[1, :, half:] += fold_rows(di * xi)
        dr, di = dr * gain_r, di * gain_i
        m1 = head_mean(dr + di)
        m2 = head_mean(dr * xr + di * xi)
        inv = rstd[rows, :]
        dr = inv * (dr - m1 - xr * m2)
        di = inv * (di - m1 - xi * m2)
        o = get(om, rows, 0, lt)
        f = 1.0 - o
        for k, dy in ((0, dr), (1, di)):
            cols = slice(k * half, (k + 1) * half)
            pre = pv[rows, cols]
            state = f * get(ws, rows, k * lt, lt) + o * (pre * sigmoid(pre))
            g = pg[rows, cols]
            sig = sigmoid(g)
            act = g * sig
            dp[rows, (3 + k) * half : (4 + k) * half] = (
                dy * state * (sig + act * (1.0 - sig))
            ).astype(BF)
            put(out, rows, k * lt, dy * act)

    out_copy = pltpu.make_async_copy(fin, out_hbm, store_sem.at[0])
    out_copy.start()

    def first_back(k, carry):
        qr, qi = carry
        t = seg_len - 1 - k
        f = 1.0 - get(om, strided(t), 0, lt)
        lr = get(out, strided(t), 0, lt) + qr
        li = get(out, strided(t), lt, lt) + qi
        return f * (cos16 * lr + sin16 * li), f * (cos16 * li - sin16 * lr)

    qr, qi = lax.fori_loop(0, seg_len, first_back, (zero, zero), unroll=4)
    seg[0] = qr
    seg[1] = qi

    def fold_back(cr, ci, keep):
        for s in range(SEGS - 1, -1, -1):
            if keep:
                seg[2, s : s + 1, :] = cr
                seg[3, s : s + 1, :] = ci
            p = seg_prod[s : s + 1, :]
            ar, ai = p * seg_cos, -(p * seg_sin)
            cr, ci = (
                ar * cr - ai * ci + seg[0, s : s + 1, :],
                ar * ci + ai * cr + seg[1, s : s + 1, :],
            )
        return cr, ci

    er, ei = fold_back(zrow, zrow, False)
    carb[c, 0:1, :] = er * not_start
    carb[c, 1:2, :] = ei * not_start
    car_copies = exchange(carb, cab_send, cab_recv)
    for copy in car_copies:
        copy.start()

    for k in range(2):
        grad = dot(mix[:, k * half : (k + 1) * half], dm[...], 0, 0).astype(BF)
        for cc in range(n_chan):
            w[cc, WO0 + 96 * k : WO0 + 96 * k + 96, :] = grad[96 * cc : 96 * cc + 96, :]

    for copy in car_copies:
        copy.wait()
    cr, ci = zrow, zrow
    for k in range(n_chan - 1, 0, -1):
        ar, ai = carx[k, 2:3, :], -carx[k, 3:4, :]
        nr = ar * cr - ai * ci + carb[k, 0:1, :]
        ni = ar * ci + ai * cr + carb[k, 1:2, :]
        cr = jnp.where(k > c, nr, cr)
        ci = jnp.where(k > c, ni, ci)
    fold_back(cr, ci, True)

    def second_back(k, carry):
        qr, qi = carry
        t = seg_len - 1 - k
        f = 1.0 - get(om, strided(t), 0, lt)
        lr = get(out, strided(t), 0, lt) + qr
        li = get(out, strided(t), lt, lt) + qi
        put(out, strided(t), 0, lr)
        put(out, strided(t), lt, li)
        return f * (cos16 * lr + sin16 * li), f * (cos16 * li - sin16 * lr)

    lax.fori_loop(0, seg_len, second_back, (seg[2], seg[3]), unroll=4)

    @pl.loop(0, n_tiles)
    def _(i):
        rows = rows_of(i, TM)
        o = get(om, rows, 0, lt)
        f = 1.0 - o
        df = jnp.zeros((TM, half), F32)
        for k in range(2):
            cols = slice(k * half, (k + 1) * half)
            pre = pv[rows, cols]
            sig = sigmoid(pre)
            act = pre * sig
            lam = get(out, rows, k * lt, lt)
            df += lam * (get(ws, rows, k * lt, lt) - act)
            dp[rows, cols] = (o * lam * (sig + act * (1.0 - sig))).astype(BF)
        dx = df * f * o
        dp[rows, 2 * half : 3 * half] = dx.astype(BF)
        sgrad[0, :, :half] += fold_rows(dx)
        sgrad[0, :, half:] += fold_rows(
            f
            * (
                get(out, rows, lt, lt) * get(ws, rows, 0, lt)
                - get(out, rows, 0, lt) * get(ws, rows, lt, lt)
            )
        )
        acc = dff[rows, :]
        for k in range(5):
            acc += dot(dp[rows, k * half : (k + 1) * half], section(k), 1, 0)
        dff[rows, :] = acc

    gtok_copy = pltpu.make_async_copy(dff, gtok_hbm, store_sem.at[1])
    gtok_copy.start()

    small = jnp.concatenate(
        [jnp.sum(sgrad[k], axis=0, keepdims=True) for k in range(3)]
        + [jnp.zeros((13, width), F32)],
        axis=0,
    ).astype(BF)
    for cc in range(n_chan):
        w[cc, PAD0 : PAD0 + 16, :] = small
        w[cc, PAD0 + 16 : WO0, :] = jnp.zeros((16, width), BF)
    for k in range(5):
        grad = dot(dp[:, k * half : (k + 1) * half], tok[...], 0, 0).astype(BF)
        for cc in range(n_chan):
            w[cc, 96 * k : 96 * k + 96, :] = grad[96 * cc : 96 * cc + 96, :]

    g_copy = pltpu.make_async_copy(w, g_hbm, store_sem.at[2])
    g_copy.start()
    for copy in (out_copy, gtok_copy, g_copy):
        copy.wait()


def main_call(w_all, tokens, cotangent, params, rms, bucket, lengths):
    rows, width = tokens.shape
    half = width // 2
    n_chan = w_all.shape[0]
    hw = (WD0 - WG0) // 2
    any_spec = pl.BlockSpec(memory_space=pl.ANY)
    vmem = pl.BlockSpec(memory_space=pltpu.VMEM)
    smem = pl.BlockSpec(memory_space=pltpu.SMEM)
    full32 = pltpu.VMEM((rows, width), F32)
    half32 = pltpu.VMEM((rows, half), F32)
    tiles32 = pltpu.VMEM((width // 128, rows, 128), F32)
    full16 = pltpu.VMEM((rows, width), BF)
    return pl.pallas_call(
        main_kernel,
        out_shape=[
            jax.ShapeDtypeStruct(w_all.shape, BF),
            jax.ShapeDtypeStruct((rows, width), F32),
            jax.ShapeDtypeStruct((rows, width), BF),
        ],
        in_specs=[any_spec, any_spec, any_spec, vmem, vmem, smem, smem],
        out_specs=[any_spec] * 3,
        scratch_shapes=[
            pltpu.VMEM(w_all.shape, BF),
            full16, full16, full32, pltpu.VMEM((half // 128, rows, 128), F32), full32, tiles32,
            full32, half32, full32, full16, full16, tiles32, full32,
            pltpu.VMEM((rows, hw), BF), pltpu.VMEM((rows, 2 * hw), BF),
            full16, pltpu.VMEM((rows, 5 * half), BF),
            pltpu.VMEM((half, half), BF),
            pltpu.VMEM((n_chan, 8, half), F32),
            pltpu.VMEM((n_chan, 8, half), F32),
            pltpu.VMEM((n_chan, 8, half), F32),
            pltpu.VMEM((4, SEGS, half), F32),
            pltpu.VMEM((3, 8, width), F32),
            pltpu.VMEM((SEGS, half), F32),
            pltpu.SemaphoreType.DMA((3,)),
            pltpu.SemaphoreType.DMA((3,)),
        ]
        + [pltpu.SemaphoreType.DMA((n_chan - 1,))] * 6,
        compiler_params=pltpu.CompilerParams(
            collective_id=0, has_side_effects=True, vmem_limit_bytes=60 * 2**20
        ),
        cost_estimate=pl.CostEstimate(
            flops=34 * 10**9, bytes_accessed=3 * 10**7, transcendentals=0
        ),
        name="block",
    )(w_all, tokens, cotangent, params, rms, bucket, lengths)


def split_parts(v):
    heads = v.shape[1] // (2 * HEAD_CH)
    return v.T.reshape(heads, 2, HEAD_CH, -1).swapaxes(0, 1).reshape(v.shape[1], -1)


def join_parts(v):
    heads = v.shape[0] // (2 * HEAD_CH)
    return v.reshape(2, heads, HEAD_CH, -1).swapaxes(0, 1).reshape(v.shape[0], -1)


def local(
    tokens, w_in, w_forget, b_forget, rotation, w_outgate, gn_gain, w_out, rms_gain,
    w_gate, w_up, w_down, cotangent, buckets, lengths,
):
    width = tokens.shape[1]
    half = width // 2
    chan = lax.axis_index("chan")
    nch = b_forget.shape[0]
    piece = jnp.concatenate(
        [
            split_parts(w_in), w_forget.T, split_parts(w_outgate),
            jnp.zeros((WO0 - PAD0, width), BF),
            w_out.reshape(-1, 2, HEAD_CH, width).swapaxes(0, 1).reshape(-1, width),
            w_gate.T, w_up.T, w_down,
        ],
        axis=0,
    )
    gains = gn_gain.reshape(-1, 2, HEAD_CH).swapaxes(0, 1).reshape(2, nch)
    params = jnp.concatenate(
        [
            b_forget[None], jnp.cos(rotation)[None], jnp.sin(rotation)[None], gains,
            jnp.zeros((3, nch), F32),
        ],
        axis=0,
    )
    params = lax.dynamic_update_slice(jnp.zeros((8, half), F32), params, (0, chan * nch))
    w_all = lax.all_gather(piece, "chan", axis=0, tiled=False)
    g, grad_tokens, block_out = main_call(
        w_all, tokens, cotangent, params, rms_gain[None], buckets, lengths
    )
    g = lax.psum_scatter(g, "chan", scatter_dimension=0, tiled=False)
    g = lax.psum(g, "batch").astype(F32)
    grad_w_in = join_parts(g[:192]).T
    grad_w_forget = g[192:288].T
    grad_w_outgate = join_parts(g[288:480]).T
    grad_w_out = join_parts(g[WO0:WG0])
    hw = (WD0 - WG0) // 2
    grad_w_gate = g[WG0 : WG0 + hw].T
    grad_w_up = g[WG0 + hw : WD0].T
    grad_w_down = g[WD0:PIECE]
    own = lax.dynamic_slice(g[PAD0 : PAD0 + 2].reshape(4, half), (0, chan * nch), (4, nch))
    grad_b, grad_rot = own[0], own[1]
    grad_gn = join_parts(own[2:4].reshape(2 * nch, 1))[:, 0]
    grad_rms = lax.dynamic_slice(g[PAD0 + 2], (chan * 2 * nch,), (2 * nch,))
    return (
        block_out, grad_tokens, grad_w_in, grad_w_forget, grad_b, grad_rot, grad_w_outgate,
        grad_gn, grad_w_out, grad_rms, grad_w_gate, grad_w_up, grad_w_down,
    )


def solution(mesh):
    both = P(("batch", "chan"), None)
    cols, rows, vec = P(None, "chan"), P("chan", None), P("chan")
    return jax.shard_map(
        local,
        mesh=mesh,
        in_specs=(
            both, cols, cols, vec, vec, cols, vec, rows, P(), cols, cols, rows, both,
            P("batch"), P("batch", None),
        ),
        out_specs=(
            both, both, cols, cols, vec, vec, cols, vec, rows, vec, cols, cols, rows,
        ),
        check_vma=False,
    )
```

```python
import functools

import jax
import jax.numpy as jnp
from jax import lax
from jax.experimental import pallas as pl
from jax.experimental.pallas import tpu as pltpu
from jax.sharding import PartitionSpec as P

MESH = pl.DeviceIdType.MESH
BF = jnp.bfloat16
F32 = jnp.float32
HEAD_CH = 32
SEGS = 16
TM = 256
PAD0, MA0, WO0, WG0, WD0, PIECE = 288, 320, 512, 704, 1472, 1856
SECTION = (0, 96, 192, 320, 416)


def dot(left, right, left_dim, right_dim):
    return lax.dot_general(
        left, right, (((left_dim,), (right_dim,)), ((), ())), preferred_element_type=F32
    )


def rows_of(tile, size):
    return pl.ds(pl.multiple_of(tile * size, size), size)


def sigmoid(v):
    return 1.0 / (1.0 + jnp.exp(-v))


def get(ref, rows, first, count):
    return jnp.concatenate([ref[first + k, rows, :] for k in range(count)], axis=1)


def put(ref, rows, first, v):
    for k in range(v.shape[1] // 128):
        ref[first + k, rows, :] = v[:, 128 * k : 128 * (k + 1)]


def fold_rows(v):
    return jnp.sum(v.reshape(v.shape[0] // 8, 8, v.shape[1]), axis=0)


def main_kernel(
    n_batch, n_chan,
    piece_hbm, tok_hbm, cot_hbm, par_ref, rms_ref, bucket_ref, len_ref,
    g_hbm, gtok_hbm, out_hbm,
    w, tok, sd, pv, om, pg, ws, xh, rstd, res, fin, mix, out, dff, hid, dgu, dm, dp,
    ones, parx, carx, carb, seg, sgrad, seg_prod,
    rb0, rb1, rb2, zbf, zba, zbb, mixf, extra,
    load_sem, store_sem, par_send, par_recv, car_send, car_recv, cab_send, cab_recv,
    ag_send, ag_recv, rs_send, rs_recv, fin_send, fin_recv, ex_send, ex_recv,
):
    n_rows, width = tok.shape
    half = width // 2
    lt = half // 128
    n_tiles = n_rows // TM
    seg_len = n_rows // SEGS
    b = lax.axis_index("batch")
    c = lax.axis_index("chan")
    peers = [lax.rem(c + j, n_chan) for j in range(1, n_chan)]
    core = lax.rem(b, 2)
    quarter = lax.rem(b // 2, 4)
    x_bit, y_bit = lax.rem(quarter, 2), quarter // 2

    def flip(bit):
        here = b
        for k in range(n_batch.bit_length()):
            if bit >> k & 1:
                here = here + (1 << k) - (2 << k) * lax.rem(b // (1 << k), 2)
        return here

    core_dev, x_dev, y_dev, diag_dev = ((flip(bit), c) for bit in (1, 2, 4, 6))
    extra_devs = [(flip(1 << k), c) for k in range(3, n_batch.bit_length() - 1)]
    mine = pl.ds(pl.multiple_of(core * half, 128), half)
    theirs = pl.ds(pl.multiple_of((1 - core) * half, 128), half)

    def span(start, size):
        return pl.ds(pl.multiple_of(start, 16), size)

    def remote(src, dst, send_sem, recv_sem, device):
        return pltpu.make_async_remote_copy(
            src, dst, send_sem, recv_sem, device_id=device, device_id_type=MESH
        )

    loads = [
        pltpu.make_async_copy(piece_hbm, w.at[c], load_sem.at[0]),
        pltpu.make_async_copy(tok_hbm, tok, load_sem.at[1]),
        pltpu.make_async_copy(cot_hbm, sd, load_sem.at[2]),
    ]
    for load in loads:
        load.start()

    barrier = pltpu.get_barrier_semaphore()
    talk = [core_dev, x_dev, y_dev, diag_dev] + extra_devs + [(b, peer) for peer in peers]
    for device in talk:
        pl.semaphore_signal(barrier, inc=1, device_id=device, device_id_type=MESH)
    pl.semaphore_wait(barrier, len(talk))

    def exchange(ref, send_sem, recv_sem):
        copies = [
            remote(ref.at[c], ref.at[c], send_sem.at[j], recv_sem.at[j], (b, peer))
            for j, peer in enumerate(peers)
        ]
        return copies

    class Gather:
        def __init__(self, unit, j, first, count):
            self.j, self.first, self.count = j, first, count
            self.src = lax.rem(c + j, n_chan)
            self.send, self.recv = ag_send.at[unit], ag_recv.at[unit]
            self.sent = []

        def rows(self, part, start=0, size=None):
            size = self.count // 4 if size is None else size
            return span(self.first + part * (self.count // 4) + start, size)

        def copy(self, k, chan, rows, device):
            ref = w.at[chan, rows, mine]
            return remote(ref, ref, self.send.at[k], self.recv.at[k], device)

        def start(self, copies):
            for copy in copies:
                copy.start()
            self.sent += copies

        def along(self):
            peer = lax.rem(c + n_chan - self.j, n_chan)
            self.z = self.copy(0, c, self.rows(quarter), (b, peer))
            self.start([self.z])

        def along_free(self):
            self.z.wait_send()
            self.sent.remove(self.z)

        def plane(self):
            self.z.wait_recv()
            rows = self.rows(quarter)
            self.p1 = [
                self.copy(1, self.src, rows, x_dev),
                self.copy(2, self.src, rows, y_dev),
            ]
            self.c1 = self.copy(3, self.src, rows, core_dev)
            self.start(self.p1 + [self.c1])

        def turn(self):
            for copy in self.p1:
                copy.wait_recv()
            from_x = y_bit * 2 + 1 - x_bit
            from_y = (1 - y_bit) * 2 + x_bit
            cut = self.count // 4 // 32 * 16
            rest = self.count // 4 - cut
            self.p2 = [
                self.copy(4, self.src, self.rows(from_x, 0, cut), y_dev),
                self.copy(5, self.src, self.rows(from_y, cut, rest), x_dev),
            ]
            self.c2 = [
                self.copy(6, self.src, self.rows(from_x), core_dev),
                self.copy(7, self.src, self.rows(from_y), core_dev),
            ]
            self.start(self.p2 + self.c2)

        def cross(self):
            for copy in self.p2:
                copy.wait_recv()
            self.c3 = self.copy(8, self.src, self.rows(3 - quarter), core_dev)
            self.start([self.c3])

        def ready(self):
            for copy in [self.c1] + self.c2 + [self.c3]:
                copy.wait_recv()

        def free(self):
            for copy in self.sent:
                copy.wait_send()

    gather_a = [Gather(j - 1, j, 0, MA0) for j in range(1, n_chan)]
    gather_b = [Gather(2 + j, j, MA0, WG0 - MA0) for j in range(1, n_chan)]
    gather_f = [Gather(5 + j, j, WG0, PIECE - WG0) for j in range(1, n_chan)]

    class Reduce:
        def __init__(self, chunk, chans, first, count, store_first, slots):
            self.chans, self.first, self.count = chans, first, count
            self.send, self.recv = rs_send.at[chunk], rs_recv.at[chunk]
            self.store_first = store_first
            self.n = len(chans)
            self.q = count // 4
            self.cut = self.q // 32 * 16
            self.buf = [buf.at[chunk % 2] for buf in (rb0, rb1, rb2)]
            self.slots = slots
            self.k = 0
            self.sent = []

        def rows(self, part, start, size):
            return span(self.store_first + part * self.q + start, size)

        def copy(self, src, dst, device):
            copy = remote(src, dst, self.send.at[self.k], self.recv.at[self.k], device)
            self.k += 1
            self.sent.append(copy)
            copy.start()
            return copy

        def add(self, chan, rows, buf, size):
            step = size if size <= 144 else 128
            for start in range(0, size, step):
                n = min(step, size - start)
                at = span(rows.start + start, n)
                w[chan, at, mine] = (
                    w[chan, at, mine].astype(F32) + buf[start : start + n, :].astype(F32)
                ).astype(BF)

        def to_core(self):
            self.s0 = []
            for i, chan in enumerate(self.chans):
                part = self.buf[0].at[i * self.count : (i + 1) * self.count, :]
                self.s0.append(
                    (chan, part, self.copy(
                        w.at[chan, self.store_first : self.store_first + self.count, theirs],
                        part, core_dev,
                    ))
                )

        def to_plane(self):
            for chan, part, copy in self.s0:
                copy.wait_recv()
                self.add(chan, pl.ds(self.store_first, self.count), part, self.count)
            self.s1 = []
            at = 0
            rest = self.q - self.cut
            for chan in self.chans:
                for k in range(2):
                    give, keep = k * 2 + 1 - x_bit, k * 2 + x_bit
                    buf = self.buf[1].at[at : at + self.cut, :]
                    at += self.cut
                    self.s1.append((chan, self.rows(keep, 0, self.cut), buf, self.cut, self.copy(
                        w.at[chan, self.rows(give, 0, self.cut), mine], buf, x_dev)))
                for k in range(2):
                    give, keep = (1 - y_bit) * 2 + k, y_bit * 2 + k
                    buf = self.buf[1].at[at : at + rest, :]
                    at += rest
                    self.s1.append((chan, self.rows(keep, self.cut, rest), buf, rest, self.copy(
                        w.at[chan, self.rows(give, self.cut, rest), mine], buf, y_dev)))

        def turn(self):
            for chan, rows, buf, size, copy in self.s1:
                copy.wait_recv()
                self.add(chan, rows, buf, size)
            self.s2 = []
            at = 0
            rest = self.q - self.cut
            for chan in self.chans:
                give = (1 - y_bit) * 2 + x_bit
                buf = self.buf[2].at[at : at + self.cut, :]
                at += self.cut
                self.s2.append((chan, self.rows(quarter, 0, self.cut), buf, self.cut, self.copy(
                    w.at[chan, self.rows(give, 0, self.cut), mine], buf, y_dev)))
                give = y_bit * 2 + 1 - x_bit
                buf = self.buf[2].at[at : at + rest, :]
                at += rest
                self.s2.append((chan, self.rows(quarter, self.cut, rest), buf, rest, self.copy(
                    w.at[chan, self.rows(give, self.cut, rest), mine], buf, x_dev)))

        def along(self, distances):
            for chan, rows, buf, size, copy in self.s2:
                copy.wait_recv()
                self.add(chan, rows, buf, size)
            self.s3 = []
            for chan, j in zip(self.chans, distances, strict=True):
                if j:
                    self.s3.append(self.copy(
                        w.at[chan, self.rows(quarter, 0, self.q), mine],
                        self.slots.at[j - 1], (b, chan)))

        def free(self):
            for copy in self.sent:
                copy.wait_send()

    class Spread:
        def __init__(self, chunk, store_first, count, slots, recvs, dest, dest_first, ex_at):
            self.first, self.q, self.count = store_first, count // 4, count
            self.slots, self.recvs, self.dest, self.at = slots, recvs, dest, dest_first
            self.send, self.recv = fin_send.at[chunk], fin_recv.at[chunk]
            self.ex = ex_send.at[chunk], ex_recv.at[chunk]
            self.ex_at = ex_at

        def total(self):
            for copy in self.recvs:
                copy.wait_recv()
            here = span(self.first + quarter * self.q, self.q)
            v = w[c, here, mine].astype(F32)
            for j in range(n_chan - 1):
                v = v + self.slots[j].astype(F32)
            at = span(self.at + quarter * self.q, self.q)
            self.dest[at, mine] = v.astype(BF)
            for k, device in enumerate(extra_devs):
                buf = extra.at[k, self.ex_at : self.ex_at + self.q, :]
                copy = remote(
                    self.dest.at[at, mine], buf, self.ex[0].at[k], self.ex[1].at[k], device
                )
                copy.start()
                copy.wait()
                v = self.dest[at, mine].astype(F32) + buf[...].astype(F32)
                self.dest[at, mine] = v.astype(BF)
            ref = self.dest.at[at, mine]
            self.copies = [
                remote(ref, ref, self.send.at[k], self.recv.at[k], device)
                for k, device in enumerate((x_dev, y_dev, diag_dev))
            ]
            for copy in self.copies:
                copy.start()

        def cross(self):
            for copy in self.copies:
                copy.wait_recv()
            ref = self.dest.at[self.at : self.at + self.count, mine]
            self.last = remote(ref, ref, self.send.at[3], self.recv.at[3], core_dev)
            self.last.start()

        def done(self):
            self.last.wait_recv()
            for copy in self.copies + [self.last]:
                copy.wait_send()

    loads[0].wait()
    for g in gather_a + gather_b:
        g.along()
    parx[c] = par_ref[...]
    par_copies = exchange(parx, par_send, par_recv)
    for copy in par_copies:
        copy.start()
    lane_r = lax.broadcasted_iota(jnp.int32, (half, half), 0) // HEAD_CH
    lane_c = lax.broadcasted_iota(jnp.int32, (half, half), 1) // HEAD_CH
    ones[...] = jnp.where(lane_r == lane_c, 1.0 / (2 * HEAD_CH), 0.0).astype(BF)
    sgrad[...] = jnp.zeros_like(sgrad)

    def head_mean(v):
        high = v.astype(BF)
        low = (v - high.astype(F32)).astype(BF)
        return dot(high, ones[...], 1, 0) + dot(low, ones[...], 1, 0)

    bucket = bucket_ref[0]
    base = c * n_rows
    offset = jnp.bitwise_and(base, bucket - 1)
    slot_limit = len_ref[0, 0]
    for k in range(1, len_ref.shape[1]):
        slot_limit = jnp.where(base >= k * bucket, len_ref[0, k], slot_limit)
    live_rows = slot_limit - offset
    not_start = jnp.where(offset == 0, 0.0, 1.0).astype(F32)

    for copy in par_copies:
        copy.wait()
    par = parx[0] + parx[1] + parx[2] + parx[3]
    bias = par[0:1, :]
    cos1, sin1 = par[1:2, :], par[2:3, :]
    gain_r, gain_i = par[3:4, :], par[4:5, :]
    rms_gain = rms_ref[...]
    cos16 = jnp.broadcast_to(cos1, (SEGS, half))
    sin16 = jnp.broadcast_to(sin1, (SEGS, half))

    def power(count):
        rr, ri = cos1, sin1
        while count > 1:
            rr, ri = rr * rr - ri * ri, 2.0 * rr * ri
            count //= 2
        return rr, ri

    seg_cos, seg_sin = power(seg_len)
    all_cos, all_sin = power(n_rows)

    def section(k):
        return jnp.concatenate(
            [w[cc, SECTION[k] : SECTION[k] + 96, :] for cc in range(n_chan)], axis=0
        )

    def out_rows(k):
        return jnp.concatenate(
            [w[cc, WO0 + 96 * k : WO0 + 96 * k + 96, :] for cc in range(n_chan)], axis=0
        )

    for g in gather_a:
        g.plane()
    for g in gather_b:
        g.plane()
    gather_f[0].along()
    for g in gather_a:
        g.turn()
    for g in gather_b:
        g.turn()
    for g in gather_a:
        g.cross()
    for g in gather_a:
        g.ready()
    loads[1].wait()

    @pl.loop(0, n_tiles)
    def _(i):
        rows = rows_of(i, TM)
        x = tok[rows, :]
        for k in range(2):
            pre = dot(x, section(k), 1, 1)
            pv[rows, k * half : (k + 1) * half] = pre
            put(out, rows, k * lt, pre * sigmoid(pre))
        put(om, rows, 0, 1.0 / (1.0 + jnp.exp(dot(x, section(2), 1, 1) + bias)))

    for g in gather_b:
        g.cross()
    gather_f[1].along()

    def strided(t):
        return pl.ds(t, SEGS, stride=seg_len)

    def first(t, carry):
        sr, si, prod = carry
        o = get(om, strided(t), 0, lt)
        f = 1.0 - o
        vr = get(out, strided(t), 0, lt)
        vi = get(out, strided(t), lt, lt)
        tr = cos16 * sr - sin16 * si
        ti = sin16 * sr + cos16 * si
        return f * tr + o * vr, f * ti + o * vi, prod * f

    zero = jnp.zeros((SEGS, half), F32)
    end_r, end_i, prod = lax.fori_loop(
        0, seg_len, first, (zero, zero, jnp.ones((SEGS, half), F32)), unroll=4
    )
    seg[0] = end_r
    seg[1] = end_i
    seg_prod[...] = prod

    def fold_forward(cr, ci, keep):
        total = jnp.ones((1, half), F32)
        for s in range(SEGS):
            if keep:
                seg[2, s : s + 1, :] = cr
                seg[3, s : s + 1, :] = ci
            p = seg_prod[s : s + 1, :]
            ar, ai = p * seg_cos, p * seg_sin
            cr, ci = (
                ar * cr - ai * ci + seg[0, s : s + 1, :],
                ar * ci + ai * cr + seg[1, s : s + 1, :],
            )
            total = total * p
        return cr, ci, total

    zrow = jnp.zeros((1, half), F32)
    er, ei, total = fold_forward(zrow, zrow, False)
    carx[c, 0:1, :] = er
    carx[c, 1:2, :] = ei
    carx[c, 2:3, :] = total * all_cos * not_start
    carx[c, 3:4, :] = total * all_sin * not_start
    car_copies = exchange(carx, car_send, car_recv)
    for copy in car_copies:
        copy.start()
    for g in gather_b:
        g.ready()
    gather_f[0].plane()
    gather_f[2].along()

    @pl.loop(0, n_tiles)
    def _(i):
        rows = rows_of(i, TM)
        x = tok[rows, :]
        for k in range(2):
            pg[rows, k * half : (k + 1) * half] = dot(x, section(3 + k), 1, 1)

    for copy in car_copies:
        copy.wait()
    cr, ci = zrow, zrow
    for k in range(n_chan - 1):
        ar, ai = carx[k, 2:3, :], carx[k, 3:4, :]
        nr = ar * cr - ai * ci + carx[k, 0:1, :]
        ni = ar * ci + ai * cr + carx[k, 1:2, :]
        cr = jnp.where(k < c, nr, cr)
        ci = jnp.where(k < c, ni, ci)
    fold_forward(cr * not_start, ci * not_start, True)

    def second(t, carry):
        sr, si = carry
        o = get(om, strided(t), 0, lt)
        f = 1.0 - o
        vr = get(out, strided(t), 0, lt)
        vi = get(out, strided(t), lt, lt)
        tr = cos16 * sr - sin16 * si
        ti = sin16 * sr + cos16 * si
        put(ws, strided(t), 0, tr)
        put(ws, strided(t), lt, ti)
        return f * tr + o * vr, f * ti + o * vi

    lax.fori_loop(0, seg_len, second, (seg[2], seg[3]), unroll=4)

    gather_f[0].turn()
    gather_f[1].plane()

    @pl.loop(0, n_tiles)
    def _(i):
        rows = rows_of(i, TM)
        o = get(om, rows, 0, lt)
        f = 1.0 - o
        gr, gi = pg[rows, :half], pg[rows, half:]
        yr = gr * sigmoid(gr) * (f * get(ws, rows, 0, lt) + o * get(out, rows, 0, lt))
        yi = gi * sigmoid(gi) * (f * get(ws, rows, lt, lt) + o * get(out, rows, lt, lt))
        mean = head_mean(yr + yi)
        yr, yi = yr - mean, yi - mean
        inv = lax.rsqrt(head_mean(yr * yr + yi * yi) + 1e-5)
        yr, yi = yr * inv, yi * inv
        rstd[rows, :] = inv
        xh[rows, :half] = yr
        xh[rows, half:] = yi
        lr, li = (yr * gain_r).astype(BF), (yi * gain_i).astype(BF)
        mix[rows, :half] = lr
        mix[rows, half:] = li
        r = tok[rows, :].astype(F32) + (
            dot(lr, out_rows(0), 1, 0) + dot(li, out_rows(1), 1, 0)
        )
        res[rows, :] = r
        put(out, rows, 0, r)
        rinv = lax.rsqrt(jnp.mean(r * r, axis=1, keepdims=True) + 1e-6)
        fin[rows, :] = (r * rinv * rms_gain).astype(BF)
        dff[rows, :] = jnp.zeros((TM, width), F32)

    loads[2].wait()
    gather_f[0].cross()
    gather_f[1].turn()
    gather_f[2].plane()

    @pl.loop(0, n_tiles)
    def _(i):
        rows = rows_of(i, TM)
        place = lax.broadcasted_iota(jnp.int32, (TM, 1), 0) + i * TM
        live = jnp.where(place < live_rows, 1.0, 0.0)
        sd[rows, :] = (sd[rows, :].astype(F32) * live).astype(BF)

    hw = hid.shape[1]

    reduce_f = [
        Reduce(j, [lax.rem(c + j, n_chan)], WG0, PIECE - WG0, WG0, zbf) for j in range(n_chan)
    ]
    for j in range(n_chan):
        cc = lax.rem(c + j, n_chan)

        def feed(i, cc=cc):
            rows = rows_of(i, TM)
            gate_up = dot(fin[rows, :], w[cc, WG0:WD0, :], 1, 1)
            d_hid = dot(sd[rows, :], w[cc, WD0:PIECE, :], 1, 1)
            gate, up = gate_up[:, :hw], gate_up[:, hw:]
            sig = sigmoid(gate)
            act = gate * sig
            h = (act * up).astype(BF)
            hid[rows, :] = h
            dg = (d_hid * up * (sig + act * (1.0 - sig))).astype(BF)
            du = (d_hid * act).astype(BF)
            dgu[rows, :hw] = dg
            dgu[rows, hw:] = du
            put(out, rows, 0, get(out, rows, 0, 2 * lt) + dot(h, w[cc, WD0:PIECE, :], 1, 0))
            dff[rows, :] += dot(dgu[rows, :], w[cc, WG0:WD0, :], 1, 0)

        if j:
            gather_f[j - 1].ready()
        pl.loop(0, n_tiles // 2)(feed)
        if j:
            reduce_f[j - 1].to_plane()
        elif j == 0:
            gather_f[1].cross()
            gather_f[2].turn()
        pl.loop(n_tiles // 2, n_tiles)(feed)
        if j:
            reduce_f[j - 1].turn()
            gather_f[j - 1].free()
        else:
            gather_f[2].cross()
            for g in gather_f:
                g.along_free()
        for k in range(2):
            w[cc, WG0 + hw * k : WG0 + hw * (k + 1), :] = dot(
                dgu[:n_rows, hw * k : hw * (k + 1)], fin[...], 0, 0
            ).astype(BF)
        if j:
            reduce_f[j - 1].along([j - 1])
        w[cc, WD0:PIECE, :] = dot(hid[...], sd[...], 0, 0).astype(BF)
        reduce_f[j].to_core()

    @pl.loop(0, n_tiles)
    def _(i):
        rows = rows_of(i, TM)
        fin[rows, :] = get(out, rows, 0, 2 * lt).astype(BF)
        r = res[rows, :]
        rinv = lax.rsqrt(jnp.mean(r * r, axis=1, keepdims=True) + 1e-6)
        rhat = r * rinv
        d = dff[rows, :]
        sgrad[2] += fold_rows(d * rhat)
        t = d * rms_gain
        dres = sd[rows, :].astype(F32) + rinv * (
            t - rhat * jnp.mean(t * rhat, axis=1, keepdims=True)
        )
        dff[rows, :] = dres
        low = dres.astype(BF)
        dm[rows, :] = low
        dr = dot(low, out_rows(0), 1, 1)
        di = dot(low, out_rows(1), 1, 1)
        xr, xi = xh[rows, :half], xh[rows, half:]
        sgrad[1, :, :half] += fold_rows(dr * xr)
        sgrad[1, :, half:] += fold_rows(di * xi)
        dr, di = dr * gain_r, di * gain_i
        m1 = head_mean(dr + di)
        m2 = head_mean(dr * xr + di * xi)
        inv = rstd[rows, :]
        dr = inv * (dr - m1 - xr * m2)
        di = inv * (di - m1 - xi * m2)
        o = get(om, rows, 0, lt)
        f = 1.0 - o
        for k, dy in ((0, dr), (1, di)):
            cols = slice(k * half, (k + 1) * half)
            pre = pv[rows, cols]
            state = f * get(ws, rows, k * lt, lt) + o * (pre * sigmoid(pre))
            g = pg[rows, cols]
            sig = sigmoid(g)
            act = g * sig
            dp[rows, (3 + k) * half : (4 + k) * half] = (
                dy * state * (sig + act * (1.0 - sig))
            ).astype(BF)
            put(out, rows, k * lt, dy * act)
        acc = dff[rows, :]
        for k in range(3, 5):
            acc += dot(dp[rows, k * half : (k + 1) * half], section(k), 1, 0)
        dff[rows, :] = acc

    out_copy = pltpu.make_async_copy(fin, out_hbm, store_sem.at[0])
    out_copy.start()
    reduce_f[-1].to_plane()

    for g in gather_a + gather_b:
        g.free()
    for k in range(4):
        left = mix[:, k * half : (k + 1) * half] if k < 2 else dp[:, (k + 1) * half : (k + 2) * half]
        grad = dot(left, dm[...] if k < 2 else tok[...], 0, 0).astype(BF)
        to = WO0 + 96 * k if k < 2 else SECTION[k + 1]
        for cc in range(n_chan):
            w[cc, to : to + 96, :] = grad[96 * cc : 96 * cc + 96, :]
    reduce_f[-1].turn()
    ring = [lax.rem(c + j, n_chan) for j in range(n_chan)]
    reduce_a = Reduce(n_chan, ring, MA0, WG0 - MA0, MA0, zba)
    reduce_a.to_core()

    def first_back(k, carry):
        qr, qi = carry
        t = seg_len - 1 - k
        f = 1.0 - get(om, strided(t), 0, lt)
        lr = get(out, strided(t), 0, lt) + qr
        li = get(out, strided(t), lt, lt) + qi
        return f * (cos16 * lr + sin16 * li), f * (cos16 * li - sin16 * lr)

    qr, qi = lax.fori_loop(0, seg_len, first_back, (zero, zero), unroll=4)
    seg[0] = qr
    seg[1] = qi

    def fold_back(cr, ci, keep):
        for s in range(SEGS - 1, -1, -1):
            if keep:
                seg[2, s : s + 1, :] = cr
                seg[3, s : s + 1, :] = ci
            p = seg_prod[s : s + 1, :]
            ar, ai = p * seg_cos, -(p * seg_sin)
            cr, ci = (
                ar * cr - ai * ci + seg[0, s : s + 1, :],
                ar * ci + ai * cr + seg[1, s : s + 1, :],
            )
        return cr, ci

    er, ei = fold_back(zrow, zrow, False)
    carb[c, 0:1, :] = er * not_start
    carb[c, 1:2, :] = ei * not_start
    car_copies = exchange(carb, cab_send, cab_recv)
    for copy in car_copies:
        copy.start()

    reduce_f[-1].along([n_chan - 1])
    reduce_a.to_plane()

    for copy in car_copies:
        copy.wait()
    cr, ci = zrow, zrow
    for k in range(n_chan - 1, 0, -1):
        ar, ai = carx[k, 2:3, :], -carx[k, 3:4, :]
        nr = ar * cr - ai * ci + carb[k, 0:1, :]
        ni = ar * ci + ai * cr + carb[k, 1:2, :]
        cr = jnp.where(k > c, nr, cr)
        ci = jnp.where(k > c, ni, ci)
    fold_back(cr, ci, True)

    def second_back(k, carry):
        qr, qi = carry
        t = seg_len - 1 - k
        f = 1.0 - get(om, strided(t), 0, lt)
        lr = get(out, strided(t), 0, lt) + qr
        li = get(out, strided(t), lt, lt) + qi
        put(out, strided(t), 0, lr)
        put(out, strided(t), lt, li)
        return f * (cos16 * lr + sin16 * li), f * (cos16 * li - sin16 * lr)

    lax.fori_loop(0, seg_len, second_back, (seg[2], seg[3]), unroll=4)
    spread_f = Spread(
        0, WG0, PIECE - WG0, zbf, [copy for r in reduce_f for copy in r.s3], dgu, 0, 0
    )
    spread_f.total()
    reduce_a.turn()

    @pl.loop(0, n_tiles)
    def _(i):
        rows = rows_of(i, TM)
        o = get(om, rows, 0, lt)
        f = 1.0 - o
        df = jnp.zeros((TM, half), F32)
        for k in range(2):
            cols = slice(k * half, (k + 1) * half)
            pre = pv[rows, cols]
            sig = sigmoid(pre)
            act = pre * sig
            lam = get(out, rows, k * lt, lt)
            df += lam * (get(ws, rows, k * lt, lt) - act)
            dp[rows, cols] = (o * lam * (sig + act * (1.0 - sig))).astype(BF)
        dx = df * f * o
        dp[rows, 2 * half : 3 * half] = dx.astype(BF)
        sgrad[0, :, :half] += fold_rows(dx)
        sgrad[0, :, half:] += fold_rows(
            f
            * (
                get(out, rows, lt, lt) * get(ws, rows, 0, lt)
                - get(out, rows, 0, lt) * get(ws, rows, lt, lt)
            )
        )

    spread_f.cross()
    reduce_a.along(range(n_chan))
    for r in reduce_f:
        r.free()
    small = jnp.concatenate(
        [jnp.sum(sgrad[k], axis=0, keepdims=True) for k in range(3)]
        + [jnp.zeros((29, width), F32)],
        axis=0,
    ).astype(BF)
    for cc in range(n_chan):
        w[cc, WG0 + PAD0 : WG0 + MA0, :] = small
    for k in range(3):
        grad = dot(dp[:, k * half : (k + 1) * half], tok[...], 0, 0).astype(BF)
        for cc in range(n_chan):
            w[cc, WG0 + 96 * k : WG0 + 96 * k + 96, :] = grad[96 * cc : 96 * cc + 96, :]
    reduce_b = Reduce(n_chan + 1, ring, 0, MA0, WG0, zbb)
    reduce_b.to_core()
    spread_f.done()
    g_copies = [pltpu.make_async_copy(
        dgu, g_hbm.at[WG0:PIECE, :], store_sem.at[2]
    )]
    g_copies[0].start()

    def d_tokens(i):
        rows = rows_of(i, TM)
        acc = dff[rows, :]
        for k in range(3):
            acc += dot(dp[rows, k * half : (k + 1) * half], section(k), 1, 0)
        dff[rows, :] = acc

    pl.loop(0, n_tiles // 2)(d_tokens)
    reduce_b.to_plane()
    pl.loop(n_tiles // 2, n_tiles)(d_tokens)
    gtok_copy = pltpu.make_async_copy(dff, gtok_hbm, store_sem.at[1])
    gtok_copy.start()
    spread_a = Spread(1, MA0, WG0 - MA0, zba, reduce_a.s3, mixf, MA0, (PIECE - WG0) // 4)
    spread_a.total()
    reduce_b.turn()
    spread_a.cross()
    reduce_b.along(range(n_chan))
    spread_a.done()
    spread_b = Spread(2, WG0, MA0, zbb, reduce_b.s3, mixf, 0, (PIECE - MA0) // 4)
    spread_b.total()
    spread_b.cross()
    spread_b.done()
    g_copies.append(pltpu.make_async_copy(mixf, g_hbm.at[:WG0, :], store_sem.at[3]))
    g_copies[1].start()
    reduce_a.free()
    reduce_b.free()
    for copy in [out_copy, gtok_copy] + g_copies:
        copy.wait()


def main_call(piece, tokens, cotangent, params, rms, bucket, lengths):
    rows, width = tokens.shape
    half = width // 2
    n_chan, n_batch = lax.axis_size("chan"), lax.axis_size("batch")
    n_extra = max(1, n_batch.bit_length() - 4)
    w_shape = (n_chan,) + piece.shape
    hw = (WD0 - WG0) // 2
    any_spec = pl.BlockSpec(memory_space=pl.ANY)
    vmem = pl.BlockSpec(memory_space=pltpu.VMEM)
    smem = pl.BlockSpec(memory_space=pltpu.SMEM)
    full32 = pltpu.VMEM((rows, width), F32)
    half32 = pltpu.VMEM((rows, half), F32)
    tiles32 = pltpu.VMEM((width // 128, rows, 128), F32)
    full16 = pltpu.VMEM((rows, width), BF)
    return pl.pallas_call(
        functools.partial(main_kernel, n_batch, n_chan),
        out_shape=[
            jax.ShapeDtypeStruct(piece.shape, BF),
            jax.ShapeDtypeStruct((rows, width), F32),
            jax.ShapeDtypeStruct((rows, width), BF),
        ],
        in_specs=[any_spec, any_spec, any_spec, vmem, vmem, smem, smem],
        out_specs=[any_spec] * 3,
        scratch_shapes=[
            pltpu.VMEM(w_shape, BF),
            full16, full16, full32, pltpu.VMEM((half // 128, rows, 128), F32), full32, tiles32,
            full32, half32, full32, full16, full16, tiles32, full32,
            pltpu.VMEM((rows, hw), BF), pltpu.VMEM((PIECE - WG0, 2 * hw), BF),
            full16, pltpu.VMEM((rows, 5 * half), BF),
            pltpu.VMEM((half, half), BF),
            pltpu.VMEM((n_chan, 8, half), F32),
            pltpu.VMEM((n_chan, 8, half), F32),
            pltpu.VMEM((n_chan, 8, half), F32),
            pltpu.VMEM((4, SEGS, half), F32),
            pltpu.VMEM((3, 8, width), F32),
            pltpu.VMEM((SEGS, half), F32),
            pltpu.VMEM((2, n_chan * (WG0 - MA0), half), BF),
            pltpu.VMEM((2, n_chan * (WG0 - MA0) // 2, half), BF),
            pltpu.VMEM((2, n_chan * (WG0 - MA0) // 4, half), BF),
            pltpu.VMEM((n_chan - 1, (PIECE - WG0) // 4, half), BF),
            pltpu.VMEM((n_chan - 1, (WG0 - MA0) // 4, half), BF),
            pltpu.VMEM((n_chan - 1, MA0 // 4, half), BF),
            pltpu.VMEM((WG0, width), BF),
            pltpu.VMEM((n_extra, PIECE // 4, half) if n_batch > 8 else (1, 16, 128), BF),
            pltpu.SemaphoreType.DMA((3,)),
            pltpu.SemaphoreType.DMA((4,)),
        ]
        + [pltpu.SemaphoreType.DMA((n_chan - 1,))] * 6
        + [pltpu.SemaphoreType.DMA((3 * (n_chan - 1), 9))] * 2
        + [pltpu.SemaphoreType.DMA((n_chan + 2, 8 * n_chan))] * 2
        + [pltpu.SemaphoreType.DMA((3, 4))] * 2
        + [pltpu.SemaphoreType.DMA((3, n_extra))] * 2,
        compiler_params=pltpu.CompilerParams(
            collective_id=0, has_side_effects=True, vmem_limit_bytes=60 * 2**20
        ),
        cost_estimate=pl.CostEstimate(
            flops=34 * 10**9, bytes_accessed=3 * 10**7, transcendentals=0
        ),
        name="block",
    )(piece, tokens, cotangent, params, rms, bucket, lengths)


def split_parts(v):
    heads = v.shape[1] // (2 * HEAD_CH)
    return v.T.reshape(heads, 2, HEAD_CH, -1).swapaxes(0, 1).reshape(v.shape[1], -1)


def join_parts(v):
    heads = v.shape[0] // (2 * HEAD_CH)
    return v.reshape(2, heads, HEAD_CH, -1).swapaxes(0, 1).reshape(v.shape[0], -1)


def local(
    tokens, w_in, w_forget, b_forget, rotation, w_outgate, gn_gain, w_out, rms_gain,
    w_gate, w_up, w_down, cotangent, buckets, lengths,
):
    width = tokens.shape[1]
    half = width // 2
    chan = lax.axis_index("chan")
    nch = b_forget.shape[0]
    piece = jnp.concatenate(
        [
            split_parts(w_in), w_forget.T, jnp.zeros((MA0 - PAD0, width), BF),
            split_parts(w_outgate),
            w_out.reshape(-1, 2, HEAD_CH, width).swapaxes(0, 1).reshape(-1, width),
            w_gate.T, w_up.T, w_down,
        ],
        axis=0,
    )
    gains = gn_gain.reshape(-1, 2, HEAD_CH).swapaxes(0, 1).reshape(2, nch)
    params = jnp.concatenate(
        [
            b_forget[None], jnp.cos(rotation)[None], jnp.sin(rotation)[None], gains,
            jnp.zeros((3, nch), F32),
        ],
        axis=0,
    )
    params = lax.dynamic_update_slice(jnp.zeros((8, half), F32), params, (0, chan * nch))
    g, grad_tokens, block_out = main_call(
        piece, tokens, cotangent, params, rms_gain[None], buckets, lengths
    )
    g = g.astype(F32)
    grad_w_in = join_parts(g[:192]).T
    grad_w_forget = g[192:288].T
    grad_w_outgate = join_parts(g[MA0:WO0]).T
    grad_w_out = join_parts(g[WO0:WG0])
    hw = (WD0 - WG0) // 2
    grad_w_gate = g[WG0 : WG0 + hw].T
    grad_w_up = g[WG0 + hw : WD0].T
    grad_w_down = g[WD0:PIECE]
    own = lax.dynamic_slice(g[PAD0 : PAD0 + 2].reshape(4, half), (0, chan * nch), (4, nch))
    grad_b, grad_rot = own[0], own[1]
    grad_gn = join_parts(own[2:4].reshape(2 * nch, 1))[:, 0]
    grad_rms = lax.dynamic_slice(g[PAD0 + 2], (chan * 2 * nch,), (2 * nch,))
    return (
        block_out, grad_tokens, grad_w_in, grad_w_forget, grad_b, grad_rot, grad_w_outgate,
        grad_gn, grad_w_out, grad_rms, grad_w_gate, grad_w_up, grad_w_down,
    )


def solution(mesh):
    both = P(("batch", "chan"), None)
    cols, rows, vec = P(None, "chan"), P("chan", None), P("chan")
    return jax.shard_map(
        local,
        mesh=mesh,
        in_specs=(
            both, cols, cols, vec, vec, cols, vec, rows, P(), cols, cols, rows, both,
            P("batch"), P("batch", None),
        ),
        out_specs=(
            both, both, cols, cols, vec, vec, cols, vec, rows, vec, cols, cols, rows,
        ),
        check_vma=False,
    )
```

```python
import functools

import jax
import jax.numpy as jnp
from jax import lax
from jax.experimental import pallas as pl
from jax.experimental.pallas import tpu as pltpu
from jax.sharding import PartitionSpec as P

MESH = pl.DeviceIdType.MESH
BF = jnp.bfloat16
F32 = jnp.float32
HEAD_CH = 32
SEGS = 16
TM = SEGS * SEGS
PAD0, MA0, WO0, WG0, WD0, PIECE = 288, 320, 512, 704, 1472, 1856
SECTION = (0, 96, 192, 320, 416)


def dot(left, right, left_dim, right_dim):
    return lax.dot_general(
        left, right, (((left_dim,), (right_dim,)), ((), ())), preferred_element_type=F32
    )


def rows_of(tile, size):
    return pl.ds(pl.multiple_of(tile * size, size), size)


def sigmoid(v):
    return 0.5 * jnp.tanh(0.5 * v) + 0.5


def tiles(count, body, steps=None):
    @pl.loop(0, count)
    def _(i):
        for at, calls in (steps or {}).items():

            @pl.when(i == at)
            def _(calls=calls):
                for call in calls:
                    call()

        body(i)


def get(ref, rows, first, count):
    return jnp.concatenate([ref[first + k, rows, :] for k in range(count)], axis=1)


def put(ref, rows, first, v):
    for k in range(v.shape[1] // 128):
        ref[first + k, rows, :] = v[:, 128 * k : 128 * (k + 1)]


def fold_rows(v):
    return jnp.sum(v.reshape(v.shape[0] // 8, 8, v.shape[1]), axis=0)


def main_kernel(
    n_batch, n_chan,
    win_hbm, wf_hbm, wg_hbm, wout_hbm, wgate_hbm, wup_hbm, wdown_hbm, tok_hbm, cot_hbm,
    bias_ref, rot_ref, gn_ref, rms_ref, bucket_ref, len_ref,
    g_hbm, gtok_hbm, out_hbm,
    w, tok, sd, pv, om, pg, ws, xh, rstd, res, fin, mix, out, dff, hid, dgu, dm, dp,
    ones, swap, parx, carx, carb, seg, sgrad, seg_prod,
    rb0, rb1, rb2, zbf, zba, zbb, mixf, extra,
    par_own,
    load_sem, store_sem, par_send, par_recv, car_send, car_recv, cab_send, cab_recv,
    ag_send, ag_recv, rs_send, rs_recv, fin_send, fin_recv, ex_send, ex_recv,
):
    n_rows, width = tok.shape
    half = width // 2
    lt = half // 128
    n_tiles = n_rows // TM
    seg_len = n_rows // SEGS
    b = lax.axis_index("batch")
    c = lax.axis_index("chan")
    peers = [lax.rem(c + j, n_chan) for j in range(1, n_chan)]
    core = lax.rem(b, 2)
    quarter = lax.rem(b // 2, 4)
    x_bit, y_bit = lax.rem(quarter, 2), quarter // 2

    def flip(bit):
        here = b
        for k in range(n_batch.bit_length()):
            if bit >> k & 1:
                here = here + (1 << k) - (2 << k) * lax.rem(b // (1 << k), 2)
        return here

    core_dev, x_dev, y_dev, diag_dev = ((flip(bit), c) for bit in (1, 2, 4, 6))
    extra_devs = [(flip(1 << k), c) for k in range(3, n_batch.bit_length() - 1)]
    mine = pl.ds(pl.multiple_of(core * half, 128), half)
    theirs = pl.ds(pl.multiple_of((1 - core) * half, 128), half)

    def span(start, size):
        return pl.ds(pl.multiple_of(start, 16), size)

    def remote(src, dst, send_sem, recv_sem, device):
        return pltpu.make_async_remote_copy(
            src, dst, send_sem, recv_sem, device_id=device, device_id_type=MESH
        )

    nch = bias_ref.shape[1]
    heads = nch // HEAD_CH

    def load(src, dst, k):
        copy = pltpu.make_async_copy(src, dst, load_sem.at[k])
        copy.start()
        return copy

    def load_heads(src, first, at):
        return [
            load(
                src.at[HEAD_CH * (2 * hh + part) : HEAD_CH * (2 * hh + part + 1), :],
                w.at[c, pl.ds(first + nch * part + HEAD_CH * hh, HEAD_CH), :],
                at + 2 * hh + part,
            )
            for hh in range(heads)
            for part in range(2)
        ]

    load_first = load_heads(win_hbm, 0, 6) + [load(wf_hbm, w.at[c, pl.ds(2 * nch, nch), :], 0)]
    load_second = load_heads(wg_hbm, MA0, 6 + 2 * heads) + load_heads(wout_hbm, WO0, 6 + 4 * heads)
    load_gate = load(wgate_hbm, hid.at[:width, :], 1)
    load_up = load(wup_hbm, dgu.at[:width, : hid.shape[1]], 2)
    load_down = load(wdown_hbm, w.at[c, WD0:PIECE, :], 3)
    load_tok = load(tok_hbm, fin, 4)
    load_cot = load(cot_hbm, dm.at[:n_rows, :], 5)

    barrier = pltpu.get_barrier_semaphore()
    talk = [core_dev, x_dev, y_dev, diag_dev] + extra_devs + [(b, peer) for peer in peers]
    for device in talk:
        pl.semaphore_signal(barrier, inc=1, device_id=device, device_id_type=MESH)

    w[c, PAD0:MA0, :] = jnp.zeros((MA0 - PAD0, width), BF)
    par_own[...] = jnp.zeros_like(par_own)
    par_own[0:1, :nch] = bias_ref[...]
    par_own[1:2, :nch] = jnp.cos(rot_ref[...])
    par_own[2:3, :nch] = jnp.sin(rot_ref[...])
    for hh in range(heads):
        for part in range(2):
            at = HEAD_CH * (2 * hh + part)
            par_own[3 + part : 4 + part, HEAD_CH * hh : HEAD_CH * (hh + 1)] = gn_ref[
                :, at : at + HEAD_CH
            ]
    parx[c] = pltpu.roll(par_own[...], c * nch, 1)
    pl.semaphore_wait(barrier, len(talk))

    def exchange(ref, send_sem, recv_sem):
        copies = [
            remote(ref.at[c], ref.at[c], send_sem.at[j], recv_sem.at[j], (b, peer))
            for j, peer in enumerate(peers)
        ]
        return copies

    class Gather:
        def __init__(self, unit, j, first, count, turns):
            self.first, self.count, self.turns = first, count, turns
            src = lax.rem(c + j, n_chan)
            peer = lax.rem(c + n_chan - j, n_chan)
            send, recv = ag_send.at[unit], ag_recv.at[unit]

            def copy(k, chan, rows, device):
                ref = w.at[chan, rows, mine]
                return remote(ref, ref, send.at[k], recv.at[k], device)

            from_x = y_bit * 2 + 1 - x_bit
            from_y = (1 - y_bit) * 2 + x_bit
            own = self.rows(quarter)
            self.z = copy(0, c, own, (b, peer))
            self.p1 = [copy(1, src, own, x_dev), copy(2, src, own, y_dev)]
            self.c1 = copy(3, src, own, core_dev)
            if turns:
                cut = count // 4 // 32 * 16
                rest = count // 4 - cut
                self.p2 = [
                    copy(4, src, self.rows(from_x, 0, cut), y_dev),
                    copy(5, src, self.rows(from_y, cut, rest), x_dev),
                ]
            else:
                self.p2 = [copy(4, src, own, diag_dev)]
            self.c2 = [copy(6, src, self.rows(from_x), core_dev),
                       copy(7, src, self.rows(from_y), core_dev)]
            self.c3 = copy(8, src, self.rows(3 - quarter), core_dev)

        def rows(self, part, start=0, size=None):
            size = self.count // 4 if size is None else size
            return span(self.first + part * (self.count // 4) + start, size)

        def along(self):
            self.z.start()

        def plane(self):
            self.z.wait_recv()
            for copy in self.p1 + [self.c1] + ([] if self.turns else self.p2):
                copy.start()

        def turn(self):
            for copy in self.p1:
                copy.wait_recv()
            for copy in (self.p2 if self.turns else []) + self.c2:
                copy.start()

        def cross(self):
            for copy in self.p2:
                copy.wait_recv()
            self.c3.start()

        def ready(self):
            for copy in [self.c1] + self.c2 + [self.c3]:
                copy.wait_recv()

        def along_free(self):
            self.z.wait_send()

        def free(self):
            for copy in self.p1 + self.p2 + [self.c1] + self.c2 + [self.c3]:
                copy.wait_send()

    gather_a = [Gather(j - 1, j, 0, MA0, False) for j in range(1, n_chan)]
    gather_b = [Gather(2 + j, j, MA0, WG0 - MA0, True) for j in range(1, n_chan)]
    gather_f = [Gather(5 + j, j, WG0, PIECE - WG0, True) for j in range(1, n_chan)]

    def in_w(chan, start, size, cols):
        return w.at[chan, span(start, size), cols]

    def in_dm(chan, start, size, cols):
        return dm.at[span(chan * MA0 + start, size), cols]

    class Reduce:
        def __init__(self, chunk, distances, count, first, slots, ref):
            self.first, self.count, self.ref = first, count, ref
            send, recv = rs_send.at[chunk], rs_recv.at[chunk]
            q = count // 4
            cut = q // 32 * 16
            rest = q - cut
            bufs = [buf.at[chunk % 2] for buf in (rb0, rb1, rb2)]
            used = [0, 0, 0]
            k = 0

            def place(level, size):
                at = used[level]
                used[level] += size
                return bufs[level].at[at : at + size, :]

            def rows(part, start, size):
                return first + part * q + start, size

            def copy(chan, rows, cols, dst, device):
                nonlocal k
                k += 1
                return remote(ref(chan, *rows, cols), dst, send.at[k - 1], recv.at[k - 1], device)

            self.s0, self.s1, self.s2, self.s3 = [], [], [], []
            near_x, far_x = quarter, y_bit * 2 + 1 - x_bit
            far_y = (1 - y_bit) * 2 + x_bit
            for j in distances:
                chan = lax.rem(c + j, n_chan)
                whole = first, count
                buf = place(0, count)
                self.s0.append((chan, first, count, buf, copy(chan, whole, theirs, buf, core_dev)))
                for part in range(2):
                    buf = place(1, cut)
                    self.s1.append((
                        chan, first + (part * 2 + x_bit) * q, cut, buf,
                        copy(chan, rows(part * 2 + 1 - x_bit, 0, cut), mine, buf, x_dev),
                    ))
                    buf = place(1, rest)
                    self.s1.append((
                        chan, first + (y_bit * 2 + part) * q + cut, rest, buf,
                        copy(chan, rows((1 - y_bit) * 2 + part, cut, rest), mine, buf, y_dev),
                    ))
                buf = place(2, cut)
                self.s2.append((
                    chan, first + quarter * q, cut, buf,
                    copy(chan, rows(far_y, 0, cut), mine, buf, y_dev),
                ))
                buf = place(2, rest)
                self.s2.append((
                    chan, first + quarter * q + cut, rest, buf,
                    copy(chan, rows(far_x, cut, rest), mine, buf, x_dev),
                ))
                if j:
                    self.s3.append(
                        copy(chan, rows(quarter, 0, q), mine, slots.at[j - 1], (b, chan))
                    )
            self.sent = [item[-1] for item in self.s0 + self.s1 + self.s2] + self.s3

        def add(self, items):
            for chan, start, size, buf, copy in items:
                copy.wait_recv()
                for at in range(0, size, 96):
                    n = min(96, size - at)
                    here = self.ref(chan, start + at, n, mine)
                    here[...] = (here[...].astype(F32) + buf[at : at + n, :].astype(F32)).astype(BF)

        def to_core(self):
            for item in self.s0:
                item[-1].start()

        def to_plane(self):
            self.add(self.s0)
            for item in self.s1:
                item[-1].start()

        def turn(self):
            self.add(self.s1)
            for item in self.s2:
                item[-1].start()

        def along(self):
            self.add(self.s2)
            for copy in self.s3:
                copy.start()

        def free(self):
            for copy in self.sent:
                copy.wait_send()

    class Spread:
        def __init__(self, chunk, ref, first, count, slots, recvs, dest, dest_first, ex_at):
            self.ref, self.first, self.q = ref, first, count // 4
            self.slots, self.recvs, self.dest = slots, recvs, dest
            send, recv = fin_send.at[chunk], fin_recv.at[chunk]
            self.at = span(dest_first + quarter * self.q, self.q)
            ref = dest.at[self.at, mine]
            self.copies = [
                remote(ref, ref, send.at[k], recv.at[k], device)
                for k, device in enumerate((x_dev, y_dev, diag_dev))
            ]
            ref_all = dest.at[dest_first : dest_first + count, mine]
            self.last = remote(ref_all, ref_all, send.at[3], recv.at[3], core_dev)
            self.extra = []
            for k, device in enumerate(extra_devs):
                buf = extra.at[k, ex_at : ex_at + self.q, :]
                self.extra.append((buf, remote(
                    ref, buf, ex_send.at[chunk, k], ex_recv.at[chunk, k], device
                )))

        def total(self):
            for copy in self.recvs:
                copy.wait_recv()
            v = self.ref(c, self.first + quarter * self.q, self.q, mine)[...].astype(F32)
            for j in range(n_chan - 1):
                v = v + self.slots[j].astype(F32)
            self.dest[self.at, mine] = v.astype(BF)
            for buf, copy in self.extra:
                copy.start()
                copy.wait()
                v = self.dest[self.at, mine].astype(F32) + buf[...].astype(F32)
                self.dest[self.at, mine] = v.astype(BF)
            for copy in self.copies:
                copy.start()

        def cross(self):
            for copy in self.copies:
                copy.wait_recv()
            self.last.start()

        def done(self):
            self.last.wait_recv()
            for copy in self.copies + [self.last]:
                copy.wait_send()

    reduce_f = [Reduce(j, [j], PIECE - WG0, WG0, zbf, in_w) for j in range(n_chan)]
    reduce_a = Reduce(n_chan, range(n_chan), WG0 - MA0, MA0, zba, in_w)
    reduce_b = Reduce(n_chan + 1, range(n_chan), MA0, 0, zbb, in_dm)
    spread_f = Spread(
        0, in_w, WG0, PIECE - WG0, zbf, [copy for r in reduce_f for copy in r.s3], dgu, 0, 0
    )
    spread_a = Spread(1, in_w, MA0, WG0 - MA0, zba, reduce_a.s3, mixf, MA0, (PIECE - WG0) // 4)
    spread_b = Spread(2, in_dm, 0, MA0, zbb, reduce_b.s3, mixf, 0, (PIECE - MA0) // 4)

    for copy in load_first:
        copy.wait()
    for g in gather_a:
        g.along()
    par_copies = exchange(parx, par_send, par_recv)
    for copy in par_copies:
        copy.start()
    for copy in load_second:
        copy.wait()
    for g in gather_b:
        g.along()
    hw = hid.shape[1]
    load_gate.wait()
    w[c, WG0 : WG0 + hw, :] = hid[:width, :].T
    load_up.wait()
    w[c, WG0 + hw : WD0, :] = dgu[:width, :hw].T
    load_down.wait()
    for g in gather_f:
        g.along()
    lane_r = lax.broadcasted_iota(jnp.int32, (half, half), 0) // HEAD_CH
    lane_c = lax.broadcasted_iota(jnp.int32, (half, half), 1) // HEAD_CH
    ones[...] = jnp.where(lane_r == lane_c, 1.0 / (2 * HEAD_CH), 0.0).astype(BF)
    sgrad[...] = jnp.zeros_like(sgrad)
    row = lax.broadcasted_iota(jnp.int32, (TM, TM), 0)
    col = lax.broadcasted_iota(jnp.int32, (TM, TM), 1)
    swap[...] = jnp.where(row == lax.rem(col, SEGS) * SEGS + col // SEGS, 1.0, 0.0).astype(BF)

    def blocks(i):
        return [span(seg_len * k + SEGS * i, SEGS) for k in range(SEGS)]

    def head_mean(v, exact=False):
        high = v.astype(BF)
        if not exact:
            return dot(high, ones[...], 1, 0)
        low = (v - high.astype(F32)).astype(BF)
        return dot(high, ones[...], 1, 0) + dot(low, ones[...], 1, 0)

    bucket = bucket_ref[0]
    base = c * n_rows
    offset = jnp.bitwise_and(base, bucket - 1)
    slot_limit = len_ref[0, 0]
    for k in range(1, len_ref.shape[1]):
        slot_limit = jnp.where(base >= k * bucket, len_ref[0, k], slot_limit)
    live_rows = slot_limit - offset
    not_start = jnp.where(offset == 0, 0.0, 1.0).astype(F32)

    for copy in par_copies:
        copy.wait()
    par = parx[0] + parx[1] + parx[2] + parx[3]
    bias = par[0:1, :]
    cos1, sin1 = par[1:2, :], par[2:3, :]
    gain_r, gain_i = par[3:4, :], par[4:5, :]
    rms_gain = rms_ref[...]
    cos16 = jnp.broadcast_to(cos1, (SEGS, half))
    sin16 = jnp.broadcast_to(sin1, (SEGS, half))

    def power(count):
        rr, ri = cos1, sin1
        while count > 1:
            rr, ri = rr * rr - ri * ri, 2.0 * rr * ri
            count //= 2
        return rr, ri

    seg_cos, seg_sin = power(seg_len)
    all_cos, all_sin = power(n_rows)

    def section(k):
        return jnp.concatenate(
            [w[cc, SECTION[k] : SECTION[k] + 96, :] for cc in range(n_chan)], axis=0
        )

    def out_rows(k):
        return jnp.concatenate(
            [w[cc, WO0 + 96 * k : WO0 + 96 * k + 96, :] for cc in range(n_chan)], axis=0
        )

    def order_tokens(i):
        part = jnp.concatenate([fin[at, :] for at in blocks(i)], axis=0)
        tok[rows_of(i, TM), :] = dot(swap[...], part, 1, 0).astype(BF)

    def order_seed(i):
        part = jnp.concatenate([dm[at, :] for at in blocks(i)], axis=0).astype(F32)
        k = lax.broadcasted_iota(jnp.int32, (TM, 1), 0)
        place = k // SEGS * seg_len + lax.rem(k, SEGS) + SEGS * i
        part = (part * jnp.where(place < live_rows, 1.0, 0.0)).astype(BF)
        sd[rows_of(i, TM), :] = dot(swap[...], part, 1, 0).astype(BF)

    load_tok.wait()
    tiles(n_tiles, order_tokens)
    for g in gather_a:
        g.plane()
    load_cot.wait()
    tiles(n_tiles, order_seed)
    for g in gather_b:
        g.plane()
    for g in gather_a:
        g.turn()
    for g in gather_a:
        g.cross()
    for g in gather_a:
        g.ready()

    def project(i):
        rows = rows_of(i, TM)
        x = tok[rows, :]
        for k in range(2):
            pre = dot(x, section(k), 1, 1)
            pv[rows, k * half : (k + 1) * half] = pre
            put(out, rows, k * lt, pre * sigmoid(pre))
        put(om, rows, 0, 1.0 / (1.0 + jnp.exp(dot(x, section(2), 1, 1) + bias)))

    tiles(n_tiles, project, {
        1: [g.turn for g in gather_b],
        3: [g.cross for g in gather_b],
    })
    gather_f[0].plane()

    def strided(t):
        return span(t * SEGS, SEGS)

    def first(t, carry):
        sr, si, prod = carry
        o = get(om, strided(t), 0, lt)
        f = 1.0 - o
        vr = get(out, strided(t), 0, lt)
        vi = get(out, strided(t), lt, lt)
        tr = cos16 * sr - sin16 * si
        ti = sin16 * sr + cos16 * si
        return f * tr + o * vr, f * ti + o * vi, prod * f

    zero = jnp.zeros((SEGS, half), F32)
    end_r, end_i, prod = lax.fori_loop(
        0, seg_len, first, (zero, zero, jnp.ones((SEGS, half), F32)), unroll=4
    )
    seg[0] = end_r
    seg[1] = end_i
    seg_prod[...] = prod

    def fold_forward(cr, ci, keep):
        total = jnp.ones((1, half), F32)
        for s in range(SEGS):
            if keep:
                seg[2, s : s + 1, :] = cr
                seg[3, s : s + 1, :] = ci
            p = seg_prod[s : s + 1, :]
            ar, ai = p * seg_cos, p * seg_sin
            cr, ci = (
                ar * cr - ai * ci + seg[0, s : s + 1, :],
                ar * ci + ai * cr + seg[1, s : s + 1, :],
            )
            total = total * p
        return cr, ci, total

    zrow = jnp.zeros((1, half), F32)
    er, ei, total = fold_forward(zrow, zrow, False)
    carx[c, 0:1, :] = er
    carx[c, 1:2, :] = ei
    carx[c, 2:3, :] = total * all_cos * not_start
    carx[c, 3:4, :] = total * all_sin * not_start
    car_copies = exchange(carx, car_send, car_recv)
    for copy in car_copies:
        copy.start()
    for g in gather_b:
        g.ready()

    def project_gate(i):
        rows = rows_of(i, TM)
        x = tok[rows, :]
        for k in range(2):
            pg[rows, k * half : (k + 1) * half] = dot(x, section(3 + k), 1, 1)

    tiles(n_tiles, project_gate, {1: [gather_f[1].plane], 2: [gather_f[0].turn]})
    for copy in car_copies:
        copy.wait()
    cr, ci = zrow, zrow
    for k in range(n_chan - 1):
        ar, ai = carx[k, 2:3, :], carx[k, 3:4, :]
        nr = ar * cr - ai * ci + carx[k, 0:1, :]
        ni = ar * ci + ai * cr + carx[k, 1:2, :]
        cr = jnp.where(k < c, nr, cr)
        ci = jnp.where(k < c, ni, ci)
    fold_forward(cr * not_start, ci * not_start, True)

    def second(t, carry):
        sr, si = carry
        o = get(om, strided(t), 0, lt)
        f = 1.0 - o
        vr = get(out, strided(t), 0, lt)
        vi = get(out, strided(t), lt, lt)
        tr = cos16 * sr - sin16 * si
        ti = sin16 * sr + cos16 * si
        put(ws, strided(t), 0, tr)
        put(ws, strided(t), lt, ti)
        return f * tr + o * vr, f * ti + o * vi

    lax.fori_loop(0, seg_len, second, (seg[2], seg[3]), unroll=4)

    def mixer_out(i):
        rows = rows_of(i, TM)
        o = get(om, rows, 0, lt)
        f = 1.0 - o
        gr, gi = pg[rows, :half], pg[rows, half:]
        yr = gr * sigmoid(gr) * (f * get(ws, rows, 0, lt) + o * get(out, rows, 0, lt))
        yi = gi * sigmoid(gi) * (f * get(ws, rows, lt, lt) + o * get(out, rows, lt, lt))
        mean = head_mean(yr + yi, True)
        yr, yi = yr - mean, yi - mean
        inv = lax.rsqrt(head_mean(yr * yr + yi * yi) + 1e-5)
        yr, yi = yr * inv, yi * inv
        rstd[rows, :] = inv
        xh[rows, :half] = yr
        xh[rows, half:] = yi
        lr, li = (yr * gain_r).astype(BF), (yi * gain_i).astype(BF)
        mix[rows, :half] = lr
        mix[rows, half:] = li
        r = tok[rows, :].astype(F32) + (
            dot(lr, out_rows(0), 1, 0) + dot(li, out_rows(1), 1, 0)
        )
        res[rows, :] = r
        put(out, rows, 0, r)
        rinv = lax.rsqrt(jnp.mean(r * r, axis=1, keepdims=True) + 1e-6)
        fin[rows, :] = (r * rinv * rms_gain).astype(BF)
        dff[rows, :] = jnp.zeros((TM, width), F32)

    tiles(n_tiles, mixer_out, {
        0: [gather_f[0].cross],
        1: [gather_f[1].turn, gather_f[2].plane],
        2: [gather_f[0].ready, gather_f[1].cross],
        3: [gather_f[2].turn],
    })

    for j in range(n_chan):
        cc = lax.rem(c + j, n_chan)

        def feed(i, cc=cc):
            rows = rows_of(i, TM)
            gate_up = dot(fin[rows, :], w[cc, WG0:WD0, :], 1, 1)
            d_hid = dot(sd[rows, :], w[cc, WD0:PIECE, :], 1, 1)
            gate, up = gate_up[:, :hw], gate_up[:, hw:]
            sig = sigmoid(gate)
            act = gate * sig
            h = (act * up).astype(BF)
            hid[rows, :] = h
            dg = (d_hid * up * (sig + act * (1.0 - sig))).astype(BF)
            du = (d_hid * act).astype(BF)
            dgu[rows, :hw] = dg
            dgu[rows, hw:] = du
            put(out, rows, 0, get(out, rows, 0, 2 * lt) + dot(h, w[cc, WD0:PIECE, :], 1, 0))
            dff[rows, :] += dot(dgu[rows, :], w[cc, WG0:WD0, :], 1, 0)

        if j == 0:
            tiles(n_tiles, feed, {0: [gather_f[2].cross], 1: [gather_f[1].ready]})
            for g in gather_f:
                g.along_free()
        else:
            before = reduce_f[j - 1]
            older = [reduce_f[j - 2]] if j > 1 else []
            if j == n_chan - 1:
                gather_f[j - 1].ready()
            tiles(n_tiles, feed, {1: [r.turn for r in older], 2: [before.to_plane]})
            gather_f[j - 1].free()
        for k in range(2):
            w[cc, WG0 + hw * k : WG0 + hw * (k + 1), :] = dot(
                dgu[:n_rows, hw * k : hw * (k + 1)], fin[...], 0, 0
            ).astype(BF)
        w[cc, WD0:PIECE, :] = dot(hid[...], sd[...], 0, 0).astype(BF)
        if j > 1:
            older[0].along()
        reduce_f[j].to_core()

    def mixer_back(i):
        rows = rows_of(i, TM)
        done = dot(swap[...], get(out, rows, 0, 2 * lt).astype(BF), 1, 0).astype(BF)
        for k, at in enumerate(blocks(i)):
            fin[at, :] = done[SEGS * k : SEGS * (k + 1), :]
        r = res[rows, :]
        rinv = lax.rsqrt(jnp.mean(r * r, axis=1, keepdims=True) + 1e-6)
        rhat = r * rinv
        d = dff[rows, :]
        sgrad[2] += fold_rows(d * rhat)
        t = d * rms_gain
        dres = sd[rows, :].astype(F32) + rinv * (
            t - rhat * jnp.mean(t * rhat, axis=1, keepdims=True)
        )
        dff[rows, :] = dres
        low = dres.astype(BF)
        dm[rows, :] = low
        dr = dot(low, out_rows(0), 1, 1)
        di = dot(low, out_rows(1), 1, 1)
        xr, xi = xh[rows, :half], xh[rows, half:]
        sgrad[1, :, :half] += fold_rows(dr * xr)
        sgrad[1, :, half:] += fold_rows(di * xi)
        dr, di = dr * gain_r, di * gain_i
        m1 = head_mean(dr + di)
        m2 = head_mean(dr * xr + di * xi)
        inv = rstd[rows, :]
        dr = inv * (dr - m1 - xr * m2)
        di = inv * (di - m1 - xi * m2)
        o = get(om, rows, 0, lt)
        f = 1.0 - o
        for k, dy in ((0, dr), (1, di)):
            cols = slice(k * half, (k + 1) * half)
            pre = pv[rows, cols]
            state = f * get(ws, rows, k * lt, lt) + o * (pre * sigmoid(pre))
            g = pg[rows, cols]
            sig = sigmoid(g)
            act = g * sig
            dp[rows, (3 + k) * half : (4 + k) * half] = (
                dy * state * (sig + act * (1.0 - sig))
            ).astype(BF)
            put(out, rows, k * lt, dy * act)
        acc = dff[rows, :]
        for k in range(3, 5):
            acc += dot(dp[rows, k * half : (k + 1) * half], section(k), 1, 0)
        dff[rows, :] = acc

    tiles(n_tiles, mixer_back, {
        0: [reduce_f[-2].turn],
        1: [reduce_f[-1].to_plane],
        3: [reduce_f[-2].along],
    })
    out_copy = pltpu.make_async_copy(fin, out_hbm, store_sem.at[0])
    out_copy.start()

    for g in gather_a + gather_b:
        g.along_free()
        g.free()
    for k in range(4):
        left = mix[:, k * half : (k + 1) * half] if k < 2 else dp[:, (k + 1) * half : (k + 2) * half]
        grad = dot(left, dm[:n_rows, :] if k < 2 else tok[...], 0, 0).astype(BF)
        to = WO0 + 96 * k if k < 2 else SECTION[k + 1]
        for cc in range(n_chan):
            w[cc, to : to + 96, :] = grad[96 * cc : 96 * cc + 96, :]
        if k == 1:
            reduce_f[-1].turn()
    reduce_a.to_core()

    def first_back(k, carry):
        qr, qi = carry
        t = seg_len - 1 - k
        f = 1.0 - get(om, strided(t), 0, lt)
        lr = get(out, strided(t), 0, lt) + qr
        li = get(out, strided(t), lt, lt) + qi
        return f * (cos16 * lr + sin16 * li), f * (cos16 * li - sin16 * lr)

    qr, qi = lax.fori_loop(0, seg_len, first_back, (zero, zero), unroll=4)
    seg[0] = qr
    seg[1] = qi

    def fold_back(cr, ci, keep):
        for s in range(SEGS - 1, -1, -1):
            if keep:
                seg[2, s : s + 1, :] = cr
                seg[3, s : s + 1, :] = ci
            p = seg_prod[s : s + 1, :]
            ar, ai = p * seg_cos, -(p * seg_sin)
            cr, ci = (
                ar * cr - ai * ci + seg[0, s : s + 1, :],
                ar * ci + ai * cr + seg[1, s : s + 1, :],
            )
        return cr, ci

    er, ei = fold_back(zrow, zrow, False)
    carb[c, 0:1, :] = er * not_start
    carb[c, 1:2, :] = ei * not_start
    car_copies = exchange(carb, cab_send, cab_recv)
    for copy in car_copies:
        copy.start()

    reduce_f[-1].along()
    reduce_a.to_plane()

    for copy in car_copies:
        copy.wait()
    cr, ci = zrow, zrow
    for k in range(n_chan - 1, 0, -1):
        ar, ai = carx[k, 2:3, :], -carx[k, 3:4, :]
        nr = ar * cr - ai * ci + carb[k, 0:1, :]
        ni = ar * ci + ai * cr + carb[k, 1:2, :]
        cr = jnp.where(k > c, nr, cr)
        ci = jnp.where(k > c, ni, ci)
    fold_back(cr, ci, True)

    def second_back(k, carry):
        qr, qi = carry
        t = seg_len - 1 - k
        f = 1.0 - get(om, strided(t), 0, lt)
        lr = get(out, strided(t), 0, lt) + qr
        li = get(out, strided(t), lt, lt) + qi
        put(out, strided(t), 0, lr)
        put(out, strided(t), lt, li)
        return f * (cos16 * lr + sin16 * li), f * (cos16 * li - sin16 * lr)

    lax.fori_loop(0, seg_len, second_back, (seg[2], seg[3]), unroll=4)
    def project_back(i):
        rows = rows_of(i, TM)
        o = get(om, rows, 0, lt)
        f = 1.0 - o
        df = jnp.zeros((TM, half), F32)
        for k in range(2):
            cols = slice(k * half, (k + 1) * half)
            pre = pv[rows, cols]
            sig = sigmoid(pre)
            act = pre * sig
            lam = get(out, rows, k * lt, lt)
            df += lam * (get(ws, rows, k * lt, lt) - act)
            dp[rows, cols] = (o * lam * (sig + act * (1.0 - sig))).astype(BF)
        dx = df * f * o
        dp[rows, 2 * half : 3 * half] = dx.astype(BF)
        sgrad[0, :, :half] += fold_rows(dx)
        sgrad[0, :, half:] += fold_rows(
            f
            * (
                get(out, rows, lt, lt) * get(ws, rows, 0, lt)
                - get(out, rows, 0, lt) * get(ws, rows, lt, lt)
            )
        )

    tiles(n_tiles, project_back)
    small = jnp.concatenate(
        [jnp.sum(sgrad[k], axis=0, keepdims=True) for k in range(3)]
        + [jnp.zeros((29, width), F32)],
        axis=0,
    ).astype(BF)
    for cc in range(n_chan):
        dm[MA0 * cc + PAD0 : MA0 * (cc + 1), :] = small
    for k in range(3):
        grad = dot(dp[:, k * half : (k + 1) * half], tok[...], 0, 0).astype(BF)
        for cc in range(n_chan):
            at = MA0 * cc + 96 * k
            dm[at : at + 96, :] = grad[96 * cc : 96 * cc + 96, :]
    reduce_b.to_core()
    def d_tokens(i):
        rows = rows_of(i, TM)
        acc = dff[rows, :]
        for k in range(3):
            acc += dot(dp[rows, k * half : (k + 1) * half], section(k), 1, 0)
        high = acc.astype(BF)
        low = (acc - high.astype(F32)).astype(BF)
        done = dot(swap[...], high, 1, 0) + dot(swap[...], low, 1, 0)
        for k, at in enumerate(blocks(i)):
            res[at, :] = done[SEGS * k : SEGS * (k + 1), :]

    tiles(n_tiles, d_tokens, {
        0: [spread_f.total, reduce_a.turn],
        2: [reduce_b.to_plane],
        3: [spread_f.cross],
    })
    gtok_copy = pltpu.make_async_copy(res, gtok_hbm, store_sem.at[1])
    gtok_copy.start()
    reduce_a.along()
    reduce_b.turn()
    spread_f.done()
    g_copies = [pltpu.make_async_copy(dgu, g_hbm.at[WG0:PIECE, :], store_sem.at[2])]
    g_copies[0].start()
    spread_a.total()
    reduce_b.along()
    spread_a.cross()
    spread_b.total()
    spread_a.done()
    spread_b.cross()
    spread_b.done()
    g_copies.append(pltpu.make_async_copy(mixf, g_hbm.at[:WG0, :], store_sem.at[3]))
    g_copies[1].start()
    for r in reduce_f + [reduce_a, reduce_b]:
        r.free()
    for copy in [out_copy, gtok_copy] + g_copies:
        copy.wait()


def post_kernel(
    g_hbm, gtok_hbm, out_hbm,
    win_ref, wf_ref, bf_ref, rot_ref, wg_ref, gn_ref, wout_ref, rms_ref, gate_ref, up_ref,
    down_ref, gtok_ref, out_ref,
    g, t_in, t_f, t_g, t_out, t_gate, t_up, t_down, t_gtok, t_block, rows8, load_sem, store_sem,
):
    nch = bf_ref.shape[1]
    heads = nch // HEAD_CH
    hw = (WD0 - WG0) // 2
    half = g.shape[1] // 2
    c = lax.axis_index("chan")
    cuts = (0, MA0, WG0, WG0 + hw, WD0, PIECE)
    loads = []
    for k in range(5):
        rows = pl.ds(cuts[k], cuts[k + 1] - cuts[k])
        loads.append(pltpu.make_async_copy(g_hbm.at[rows, :], g.at[rows, :], load_sem.at[k]))
        loads[-1].start()
    stage = [
        pltpu.make_async_copy(gtok_hbm, t_gtok, load_sem.at[5]),
        pltpu.make_async_copy(out_hbm, t_block, load_sem.at[6]),
    ]
    for copy in stage:
        copy.start()
    stores = []

    def store(src, dst):
        copy = pltpu.make_async_copy(src, dst, store_sem.at[len(stores)])
        copy.start()
        stores.append(copy)

    def joined(first):
        return jnp.concatenate(
            [
                g[first + nch * part + HEAD_CH * hh : first + nch * part + HEAD_CH * (hh + 1), :]
                for hh in range(heads)
                for part in range(2)
            ],
            axis=0,
        )

    loads[0].wait()
    t_in[...] = joined(0).astype(F32)
    store(t_in, win_ref)
    t_f[...] = g[2 * nch : 3 * nch, :].astype(F32)
    store(t_f, wf_ref)
    small = g[PAD0 : PAD0 + 16, :].astype(F32)
    turn = lax.rem(4 - c, 4) * nch
    rows8[0:8, :half] = pltpu.roll(small[0:8, :half], turn, 1)
    rows8[0:8, half:] = pltpu.roll(small[0:8, half:], turn, 1)
    bf_ref[...] = rows8[0:1, :nch]
    rot_ref[...] = rows8[0:1, half : half + nch]
    for hh in range(heads):
        for part in range(2):
            at = half * part + HEAD_CH * hh
            to = HEAD_CH * (2 * hh + part)
            gn_ref[:, to : to + HEAD_CH] = rows8[1:2, at : at + HEAD_CH]
    rows8[8:16, :] = pltpu.roll(small[0:8, :], 2 * turn, 1)
    rms_ref[...] = rows8[10:11, : 2 * nch]
    loads[1].wait()
    t_g[...] = joined(MA0).astype(F32)
    store(t_g, wg_ref)
    t_out[...] = joined(WO0).astype(F32)
    store(t_out, wout_ref)
    loads[2].wait()
    t_gate[...] = g[WG0 : WG0 + hw, :].T.astype(F32)
    store(t_gate, gate_ref)
    loads[3].wait()
    t_up[...] = g[WG0 + hw : WD0, :].T.astype(F32)
    store(t_up, up_ref)
    loads[4].wait()
    t_down[...] = g[WD0:PIECE, :].astype(F32)
    store(t_down, down_ref)
    for copy, src, dst in zip(stage, (t_gtok, t_block), (gtok_ref, out_ref), strict=True):
        copy.wait()
        store(src, dst)
    for copy in stores:
        copy.wait()


def post_call(g, grad_tokens, block_out, nch):
    width = g.shape[1]
    hw = (WD0 - WG0) // 2
    any_spec = pl.BlockSpec(memory_space=pl.ANY)
    vmem = pl.BlockSpec(memory_space=pltpu.VMEM)
    big = [(2 * nch, width), (nch, width), (2 * nch, width), (2 * nch, width), (width, hw),
           (width, hw), (hw, width)]
    shapes = [big[0], big[1], (1, nch), (1, nch), big[2], (1, 2 * nch), big[3], (1, 2 * nch),
              big[4], big[5], big[6], grad_tokens.shape]
    return pl.pallas_call(
        post_kernel,
        out_shape=[jax.ShapeDtypeStruct(shape, F32) for shape in shapes]
        + [jax.ShapeDtypeStruct(block_out.shape, BF)],
        in_specs=[any_spec] * 3,
        out_specs=[vmem if shape[0] == 1 else any_spec for shape in shapes] + [any_spec],
        scratch_shapes=[pltpu.VMEM(g.shape, BF)]
        + [pltpu.VMEM(shape, F32) for shape in big + [grad_tokens.shape]]
        + [
            pltpu.VMEM(block_out.shape, BF),
            pltpu.VMEM((16, width), F32),
            pltpu.SemaphoreType.DMA((7,)),
            pltpu.SemaphoreType.DMA((9,)),
        ],
        compiler_params=pltpu.CompilerParams(vmem_limit_bytes=48 * 2**20),
        name="place",
    )(g, grad_tokens, block_out)


def main_call(weights, tokens, cotangent, vectors, bucket, lengths):
    rows, width = tokens.shape
    half = width // 2
    nch = vectors[0].shape[1]
    n_chan, n_batch = lax.axis_size("chan"), lax.axis_size("batch")
    n_extra = max(1, n_batch.bit_length() - 4)
    w_shape = (n_chan, PIECE, width)
    hw = (WD0 - WG0) // 2
    any_spec = pl.BlockSpec(memory_space=pl.ANY)
    vmem = pl.BlockSpec(memory_space=pltpu.VMEM)
    smem = pl.BlockSpec(memory_space=pltpu.SMEM)
    full32 = pltpu.VMEM((rows, width), F32)
    half32 = pltpu.VMEM((rows, half), F32)
    tiles32 = pltpu.VMEM((width // 128, rows, 128), F32)
    full16 = pltpu.VMEM((rows, width), BF)
    return pl.pallas_call(
        functools.partial(main_kernel, n_batch, n_chan),
        out_shape=[
            jax.ShapeDtypeStruct((PIECE, width), BF),
            jax.ShapeDtypeStruct((rows, width), F32),
            jax.ShapeDtypeStruct((rows, width), BF),
        ],
        in_specs=[any_spec] * 9 + [vmem] * 4 + [smem, smem],
        out_specs=[any_spec] * 3,
        scratch_shapes=[
            pltpu.VMEM(w_shape, BF),
            full16, full16, full32, pltpu.VMEM((half // 128, rows, 128), F32), full32, tiles32,
            full32, half32, full32, full16, full16, tiles32, full32,
            pltpu.VMEM((rows, hw), BF), pltpu.VMEM((PIECE - WG0, 2 * hw), BF),
            pltpu.VMEM((max(rows, n_chan * MA0), width), BF), pltpu.VMEM((rows, 5 * half), BF),
            pltpu.VMEM((half, half), BF),
            pltpu.VMEM((TM, TM), BF),
            pltpu.VMEM((n_chan, 8, half), F32),
            pltpu.VMEM((n_chan, 8, half), F32),
            pltpu.VMEM((n_chan, 8, half), F32),
            pltpu.VMEM((4, SEGS, half), F32),
            pltpu.VMEM((3, 8, width), F32),
            pltpu.VMEM((SEGS, half), F32),
            pltpu.VMEM((2, n_chan * (WG0 - MA0), half), BF),
            pltpu.VMEM((2, n_chan * (WG0 - MA0) // 2, half), BF),
            pltpu.VMEM((2, n_chan * (WG0 - MA0) // 4, half), BF),
            pltpu.VMEM((n_chan - 1, (PIECE - WG0) // 4, half), BF),
            pltpu.VMEM((n_chan - 1, (WG0 - MA0) // 4, half), BF),
            pltpu.VMEM((n_chan - 1, MA0 // 4, half), BF),
            pltpu.VMEM((WG0, width), BF),
            pltpu.VMEM((n_extra, PIECE // 4, half) if n_batch > 8 else (1, 16, 128), BF),
            pltpu.VMEM((8, half), F32),
            pltpu.SemaphoreType.DMA((6 + 6 * nch // HEAD_CH,)),
            pltpu.SemaphoreType.DMA((4,)),
        ]
        + [pltpu.SemaphoreType.DMA((n_chan - 1,))] * 6
        + [pltpu.SemaphoreType.DMA((3 * (n_chan - 1), 9))] * 2
        + [pltpu.SemaphoreType.DMA((n_chan + 2, 8 * n_chan))] * 2
        + [pltpu.SemaphoreType.DMA((3, 4))] * 2
        + [pltpu.SemaphoreType.DMA((3, n_extra))] * 2,
        compiler_params=pltpu.CompilerParams(
            collective_id=0, has_side_effects=True, vmem_limit_bytes=60 * 2**20
        ),
        cost_estimate=pl.CostEstimate(
            flops=34 * 10**9, bytes_accessed=3 * 10**7, transcendentals=0
        ),
        name="block",
    )(*weights, tokens, cotangent, *vectors, bucket, lengths)


def local(
    tokens, w_in, w_forget, b_forget, rotation, w_outgate, gn_gain, w_out, rms_gain,
    w_gate, w_up, w_down, cotangent, buckets, lengths,
):
    g, grad_tokens, block_out = main_call(
        (w_in.T, w_forget.T, w_outgate.T, w_out, w_gate, w_up, w_down), tokens, cotangent,
        (b_forget[None], rotation[None], gn_gain[None], rms_gain[None]), buckets, lengths,
    )
    (
        grad_w_in, grad_w_forget, grad_b, grad_rot, grad_w_outgate, grad_gn, grad_w_out, grad_rms,
        grad_w_gate, grad_w_up, grad_w_down, grad_tokens, block_out,
    ) = post_call(g, grad_tokens, block_out, b_forget.shape[0])
    return (
        block_out, grad_tokens, grad_w_in.T, grad_w_forget.T, grad_b[0], grad_rot[0],
        grad_w_outgate.T, grad_gn[0], grad_w_out, grad_rms[0], grad_w_gate, grad_w_up, grad_w_down,
    )


def solution(mesh):
    both = P(("batch", "chan"), None)
    cols, rows, vec = P(None, "chan"), P("chan", None), P("chan")
    return jax.shard_map(
        local,
        mesh=mesh,
        in_specs=(
            both, cols, cols, vec, vec, cols, vec, rows, P(), cols, cols, rows, both,
            P("batch"), P("batch", None),
        ),
        out_specs=(
            both, both, cols, cols, vec, vec, cols, vec, rows, vec, cols, cols, rows,
        ),
        check_vma=False,
    )
```

```python
import functools

import jax
import jax.numpy as jnp
from jax import lax
from jax.experimental import pallas as pl
from jax.experimental.pallas import tpu as pltpu
from jax.sharding import PartitionSpec as P

MESH = pl.DeviceIdType.MESH
BF = jnp.bfloat16
F32 = jnp.float32
HEAD_CH = 32
SEGS = 16
TM = SEGS * SEGS
PAD0, MA0, WO0, WG0, WD0, PIECE = 288, 320, 512, 704, 1472, 1856
SECTION = (0, 96, 192, 320, 416)


def dot(left, right, left_dim, right_dim):
    return lax.dot_general(
        left, right, (((left_dim,), (right_dim,)), ((), ())), preferred_element_type=F32
    )


def rows_of(tile, size):
    return pl.ds(pl.multiple_of(tile * size, size), size)


def sigmoid(v):
    return 0.5 * jnp.tanh(0.5 * v) + 0.5


def tiles(count, body, steps=None):
    @pl.loop(0, count)
    def _(i):
        for at, calls in (steps or {}).items():

            @pl.when(i == at)
            def _(calls=calls):
                for call in calls:
                    call()

        body(i)


def get(ref, rows, first, count):
    return jnp.concatenate([ref[first + k, rows, :] for k in range(count)], axis=1)


def put(ref, rows, first, v):
    for k in range(v.shape[1] // 128):
        ref[first + k, rows, :] = v[:, 128 * k : 128 * (k + 1)]


def fold_rows(v):
    return jnp.sum(v.reshape(v.shape[0] // 8, 8, v.shape[1]), axis=0)


def main_kernel(
    n_batch, n_chan,
    win_hbm, wf_hbm, wg_hbm, wout_hbm, wgate_hbm, wup_hbm, wdown_hbm, tok_hbm, cot_hbm,
    bias_ref, rot_ref, gn_ref, rms_ref, bucket_ref, len_ref,
    g_hbm, gtok_hbm, out_hbm,
    w, tok, sd, pv, om, pg, ws, xh, rstd, res, fin, mix, out, dff, hid, dgu, dm, dp,
    ones, swap, parx, carx, carb, seg, sgrad, seg_prod,
    rb0, rb1, rb2, mb0, mb1, mb2, zbf, zbm, mixf, extra,
    par_own,
    load_sem, store_sem, par_send, par_recv, car_send, car_recv, cab_send, cab_recv,
    ag_send, ag_recv, rs_send, rs_recv, fin_send, fin_recv, ex_send, ex_recv,
):
    n_rows, width = tok.shape
    half = width // 2
    lt = half // 128
    n_tiles = n_rows // TM
    seg_len = n_rows // SEGS
    b = lax.axis_index("batch")
    c = lax.axis_index("chan")
    peers = [lax.rem(c + j, n_chan) for j in range(1, n_chan)]
    core = lax.rem(b, 2)
    quarter = lax.rem(b // 2, 4)
    x_bit, y_bit = lax.rem(quarter, 2), quarter // 2

    def flip(bit):
        here = b
        for k in range(n_batch.bit_length()):
            if bit >> k & 1:
                here = here + (1 << k) - (2 << k) * lax.rem(b // (1 << k), 2)
        return here

    core_dev, x_dev, y_dev, diag_dev = ((flip(bit), c) for bit in (1, 2, 4, 6))
    extra_devs = [(flip(1 << k), c) for k in range(3, n_batch.bit_length() - 1)]
    mine = pl.ds(pl.multiple_of(core * half, 128), half)
    theirs = pl.ds(pl.multiple_of((1 - core) * half, 128), half)

    def span(start, size):
        return pl.ds(pl.multiple_of(start, 16), size)

    def remote(src, dst, send_sem, recv_sem, device):
        return pltpu.make_async_remote_copy(
            src, dst, send_sem, recv_sem, device_id=device, device_id_type=MESH
        )

    nch = bias_ref.shape[1]
    heads = nch // HEAD_CH

    def load(src, dst, k):
        copy = pltpu.make_async_copy(src, dst, load_sem.at[k])
        copy.start()
        return copy

    def load_heads(src, first, at):
        return [
            load(
                src.at[HEAD_CH * (2 * hh + part) : HEAD_CH * (2 * hh + part + 1), :],
                w.at[c, pl.ds(first + nch * part + HEAD_CH * hh, HEAD_CH), :],
                at + 2 * hh + part,
            )
            for hh in range(heads)
            for part in range(2)
        ]

    load_first = load_heads(win_hbm, 0, 5 + n_chan) + [load(wf_hbm, w.at[c, pl.ds(2 * nch, nch), :], 0)]
    load_second = (
        load_heads(wg_hbm, MA0, 5 + n_chan + 2 * heads)
        + load_heads(wout_hbm, WO0, 5 + n_chan + 4 * heads)
    )
    load_gate = load(wgate_hbm, hid.at[:width, :], 1)
    load_up = load(wup_hbm, dgu.at[:width, : hid.shape[1]], 2)
    load_down = load(wdown_hbm, w.at[c, WD0:PIECE, :], 3)
    load_tok = load(tok_hbm, fin, 4)
    per = n_rows // n_chan
    load_cot = [
        load(cot_hbm.at[per * k : per * (k + 1), :], dm.at[k, :per, :], 5 + k) for k in range(n_chan)
    ]

    barrier = pltpu.get_barrier_semaphore()
    talk = [core_dev, x_dev, y_dev, diag_dev] + extra_devs + [(b, peer) for peer in peers]
    for device in talk:
        pl.semaphore_signal(barrier, inc=1, device_id=device, device_id_type=MESH)

    w[c, PAD0:MA0, :] = jnp.zeros((MA0 - PAD0, width), BF)
    par_own[...] = jnp.zeros_like(par_own)
    par_own[0:1, :nch] = bias_ref[...]
    par_own[1:2, :nch] = jnp.cos(rot_ref[...])
    par_own[2:3, :nch] = jnp.sin(rot_ref[...])
    for hh in range(heads):
        for part in range(2):
            at = HEAD_CH * (2 * hh + part)
            par_own[3 + part : 4 + part, HEAD_CH * hh : HEAD_CH * (hh + 1)] = gn_ref[
                :, at : at + HEAD_CH
            ]
    parx[c] = pltpu.roll(par_own[...], c * nch, 1)
    pl.semaphore_wait(barrier, len(talk))

    def exchange(ref, send_sem, recv_sem):
        copies = [
            remote(ref.at[c], ref.at[c], send_sem.at[j], recv_sem.at[j], (b, peer))
            for j, peer in enumerate(peers)
        ]
        return copies

    def chain(ref, send_sem, recv_sem, up):
        def each(out, call):
            for k in range(n_chan):
                above = c < k if out == up else c > k
                copy = remote(
                    ref.at[c] if out else ref.at[k], ref.at[c] if out else ref.at[k],
                    send_sem.at[k], recv_sem.at[c] if out else recv_sem.at[k], (b, k),
                )
                pl.when(above)(functools.partial(call, copy))

        def send():
            each(True, lambda copy: copy.start())

        def receive():
            each(False, lambda copy: copy.wait_recv())
            each(True, lambda copy: copy.wait_send())

        return send, receive

    class Gather:
        def __init__(self, unit, j, first, count, turns):
            self.first, self.count, self.turns = first, count, turns
            src = lax.rem(c + j, n_chan)
            peer = lax.rem(c + n_chan - j, n_chan)
            send, recv = ag_send.at[unit], ag_recv.at[unit]

            def copy(k, chan, rows, device):
                ref = w.at[chan, rows, mine]
                return remote(ref, ref, send.at[k], recv.at[k], device)

            from_x = y_bit * 2 + 1 - x_bit
            from_y = (1 - y_bit) * 2 + x_bit
            own = self.rows(quarter)
            self.z = copy(0, c, own, (b, peer))
            self.p1 = [copy(1, src, own, x_dev), copy(2, src, own, y_dev)]
            self.c1 = copy(3, src, own, core_dev)
            if turns:
                cut = count // 4 // 32 * 16
                rest = count // 4 - cut
                self.p2 = [
                    copy(4, src, self.rows(from_x, 0, cut), y_dev),
                    copy(5, src, self.rows(from_y, cut, rest), x_dev),
                ]
            else:
                self.p2 = [copy(4, src, own, diag_dev)]
            self.c2 = [copy(6, src, self.rows(from_x), core_dev),
                       copy(7, src, self.rows(from_y), core_dev)]
            self.c3 = copy(8, src, self.rows(3 - quarter), core_dev)

        def rows(self, part, start=0, size=None):
            size = self.count // 4 if size is None else size
            return span(self.first + part * (self.count // 4) + start, size)

        def along(self):
            self.z.start()

        def plane(self):
            self.z.wait_recv()
            for copy in self.p1 + [self.c1] + ([] if self.turns else self.p2):
                copy.start()

        def turn(self):
            for copy in self.p1:
                copy.wait_recv()
            for copy in (self.p2 if self.turns else []) + self.c2:
                copy.start()

        def cross(self):
            for copy in self.p2:
                copy.wait_recv()
            self.c3.start()

        def ready(self):
            for copy in [self.c1] + self.c2 + [self.c3]:
                copy.wait_recv()

        def along_free(self):
            self.z.wait_send()

        def free(self):
            for copy in self.p1 + self.p2 + [self.c1] + self.c2 + [self.c3]:
                copy.wait_send()

    ring = range(1, n_chan)
    gather_a = [Gather(j - 1, j, 0, MA0, False) for j in ring]
    gather_b = [Gather(2 + j, j, MA0, WO0 - MA0, True) for j in ring]
    gather_o = [Gather(5 + j, j, WO0, WG0 - WO0, True) for j in ring]
    gather_f = [Gather(8 + j, j, WG0, PIECE - WG0, True) for j in ring]

    place_f = [[buf.at[k] for buf in (rb0, rb1, rb2)] for k in range(2)]
    place_m = [[buf.at[k] for buf in (mb0, mb1, mb2)] for k in (0, 1, 2, 0)]

    class Reduce:
        def __init__(self, chunk, place, ref, chan, first, count, slots):
            self.ref = ref
            send, recv = rs_send.at[chunk], rs_recv.at[chunk]
            q = count // 4
            cut = q // 32 * 16
            rest = q - cut
            chans = pl.ds(0, n_chan) if chan is None else pl.ds(chan, 1)
            n = n_chan if chan is None else 1
            far_x = y_bit * 2 + 1 - x_bit
            far_y = (1 - y_bit) * 2 + x_bit

            def item(k, level, at, part, keep, start, size, cols, device):
                buf = place[level].at[:n, at : at + size, :]
                src = ref.at[chans, span(first + part * q + start, size), cols]
                to = chans, span(first + keep * q + start, size)
                return to, buf, size, remote(src, buf, send.at[k], recv.at[k], device)

            whole = place[0].at[:n, :count, :]
            src = ref.at[chans, first : first + count, theirs]
            self.s0 = [(
                (chans, pl.ds(first, count)), whole, count,
                remote(src, whole, send.at[0], recv.at[0], core_dev),
            )]
            self.s1 = []
            for k in range(2):
                self.s1.append(item(
                    1 + k, 1, k * cut, k * 2 + 1 - x_bit, k * 2 + x_bit, 0, cut, mine, x_dev))
                self.s1.append(item(
                    3 + k, 1, 2 * cut + k * rest, (1 - y_bit) * 2 + k, y_bit * 2 + k, cut, rest,
                    mine, y_dev))
            self.s2 = [
                item(5, 2, 0, far_y, quarter, 0, cut, mine, y_dev),
                item(6, 2, cut, far_x, quarter, cut, rest, mine, x_dev),
            ]
            own = span(first + quarter * q, q)
            self.s3 = [
                remote(
                    ref.at[lax.rem(c + j, n_chan), own, mine], slots.at[j - 1],
                    send.at[6 + j], recv.at[6 + j], (b, lax.rem(c + j, n_chan)),
                )
                for j in range(1, n_chan)
                if chan is None or chunk == j
            ]
            self.sent = [it[-1] for it in self.s0 + self.s1 + self.s2] + self.s3

        def add(self, items):
            for (chans, rows), buf, size, copy in items:
                copy.wait_recv()
                step = 96 if buf.shape[0] == 1 else 16
                for at in range(0, size, step):
                    n = min(step, size - at)
                    here = self.ref.at[chans, span(rows.start + at, n), mine]
                    here[...] = here[...] + buf[:, at : at + n, :]

        def to_core(self):
            for item in self.s0:
                item[-1].start()

        def to_plane(self):
            self.add(self.s0)
            for item in self.s1:
                item[-1].start()

        def turn(self):
            self.add(self.s1)
            for item in self.s2:
                item[-1].start()

        def along(self):
            self.add(self.s2)
            for copy in self.s3:
                copy.start()

        def free(self):
            for copy in self.sent:
                copy.wait_send()

    class Spread:
        def __init__(self, chunk, ref, first, count, slots, recvs, dest, dest_first, ex_at, turns=False):
            self.ref, self.first, self.q = ref, first, count // 4
            self.slots, self.recvs, self.dest = slots, recvs, dest
            send, recv = fin_send.at[chunk], fin_recv.at[chunk]
            self.at = span(dest_first + quarter * self.q, self.q)
            ref = dest.at[self.at, mine]
            self.copies = [
                remote(ref, ref, send.at[k], recv.at[k], device)
                for k, device in enumerate((x_dev, y_dev) if turns else (x_dev, y_dev, diag_dev))
            ]
            self.p2 = []
            if turns:
                cut = self.q // 32 * 16
                parts = (
                    (y_bit * 2 + 1 - x_bit, 0, cut, y_dev),
                    ((1 - y_bit) * 2 + x_bit, cut, self.q - cut, x_dev),
                )
                for k, (part, start, size, device) in enumerate(parts):
                    half_ref = dest.at[span(dest_first + part * self.q + start, size), mine]
                    self.p2.append(remote(
                        half_ref, half_ref, send.at[4 + k], recv.at[4 + k], device
                    ))
            ref_all = dest.at[dest_first : dest_first + count, mine]
            self.last = remote(ref_all, ref_all, send.at[3], recv.at[3], core_dev)
            self.extra = []
            for k, device in enumerate(extra_devs):
                buf = extra.at[k, ex_at : ex_at + self.q, :]
                self.extra.append((buf, remote(
                    ref, buf, ex_send.at[chunk, k], ex_recv.at[chunk, k], device
                )))

        def total(self):
            for copy in self.recvs:
                copy.wait_recv()
            v = self.ref[c, span(self.first + quarter * self.q, self.q), mine].astype(F32)
            for j in range(n_chan - 1):
                v = v + self.slots[j].astype(F32)
            self.dest[self.at, mine] = v.astype(BF)
            for buf, copy in self.extra:
                copy.start()
                copy.wait()
                v = self.dest[self.at, mine].astype(F32) + buf[...].astype(F32)
                self.dest[self.at, mine] = v.astype(BF)
            for copy in self.copies:
                copy.start()

        def turn(self):
            for copy in self.copies:
                copy.wait_recv()
            for copy in self.p2:
                copy.start()

        def cross(self):
            for copy in self.p2 or self.copies:
                copy.wait_recv()
            self.last.start()

        def done(self):
            self.last.wait_recv()
            for copy in self.copies + self.p2 + [self.last]:
                copy.wait_send()

    f_rows = PIECE - WG0
    reduce_f = [
        Reduce(j, place_f[j % 2], w, lax.rem(c + j, n_chan), WG0, f_rows, zbf)
        for j in range(n_chan)
    ]
    reduce_o = Reduce(n_chan, place_m[0], w, None, WO0, WG0 - WO0, zbm.at[0])
    reduce_g = Reduce(n_chan + 1, place_m[1], w, None, MA0, WO0 - MA0, zbm.at[1])
    reduce_v = Reduce(n_chan + 2, place_m[2], dm, None, 0, 2 * nch, zbm.at[2])
    reduce_k = Reduce(
        n_chan + 3, place_m[3], dm, None, 2 * nch, MA0 - 2 * nch,
        zbm.at[3, :, : (MA0 - 2 * nch) // 4],
    )
    spread_f = Spread(
        0, w, WG0, f_rows, zbf, [copy for r in reduce_f for copy in r.s3], dgu, 0, 0, True
    )
    at = [f_rows // 4 + k * (nch // 2) for k in range(4)]
    spread_o = Spread(1, w, WO0, WG0 - WO0, zbm.at[0], reduce_o.s3, mixf, WO0, at[0])
    spread_g = Spread(2, w, MA0, WO0 - MA0, zbm.at[1], reduce_g.s3, mixf, MA0, at[1])
    spread_v = Spread(3, dm, 0, 2 * nch, zbm.at[2], reduce_v.s3, mixf, 0, at[2])
    spread_k = Spread(
        4, dm, 2 * nch, MA0 - 2 * nch, zbm.at[3, :, : (MA0 - 2 * nch) // 4], reduce_k.s3, mixf,
        2 * nch, at[3],
    )

    for copy in load_first:
        copy.wait()
    par_copies = exchange(parx, par_send, par_recv)
    for copy in par_copies:
        copy.start()
    for g in gather_a:
        g.along()
    for copy in load_second:
        copy.wait()
    hw = hid.shape[1]
    load_gate.wait()
    w[c, WG0 : WG0 + hw, :] = hid[:width, :].T
    load_up.wait()
    w[c, WG0 + hw : WD0, :] = dgu[:width, :hw].T
    load_down.wait()
    lane_r = lax.broadcasted_iota(jnp.int32, (half, half), 0) // HEAD_CH
    lane_c = lax.broadcasted_iota(jnp.int32, (half, half), 1) // HEAD_CH
    ones[...] = jnp.where(lane_r == lane_c, 1.0 / (2 * HEAD_CH), 0.0).astype(BF)
    sgrad[...] = jnp.zeros_like(sgrad)
    row = lax.broadcasted_iota(jnp.int32, (TM, TM), 0)
    col = lax.broadcasted_iota(jnp.int32, (TM, TM), 1)
    swap[...] = jnp.where(row == lax.rem(col, SEGS) * SEGS + col // SEGS, 1.0, 0.0).astype(BF)

    def blocks(i):
        return [span(seg_len * k + SEGS * i, SEGS) for k in range(SEGS)]

    def head_mean(v, exact=False):
        high = v.astype(BF)
        if not exact:
            return dot(high, ones[...], 1, 0)
        low = (v - high.astype(F32)).astype(BF)
        return dot(high, ones[...], 1, 0) + dot(low, ones[...], 1, 0)

    bucket = bucket_ref[0]
    base = c * n_rows
    offset = jnp.bitwise_and(base, bucket - 1)
    slot_limit = len_ref[0, 0]
    for k in range(1, len_ref.shape[1]):
        slot_limit = jnp.where(base >= k * bucket, len_ref[0, k], slot_limit)
    live_rows = slot_limit - offset
    not_start = jnp.where(offset == 0, 0.0, 1.0).astype(F32)

    def section(k):
        return jnp.concatenate(
            [w[cc, SECTION[k] : SECTION[k] + 96, :] for cc in range(n_chan)], axis=0
        )

    def out_rows(k):
        return jnp.concatenate(
            [w[cc, WO0 + 96 * k : WO0 + 96 * k + 96, :] for cc in range(n_chan)], axis=0
        )

    def order_tokens(i):
        part = jnp.concatenate([fin[at, :] for at in blocks(i)], axis=0)
        tok[rows_of(i, TM), :] = dot(swap[...], part, 1, 0).astype(BF)

    def order_seed(i):
        part = jnp.concatenate(
            [
                dm[k, span(seg_len * m + SEGS * i, SEGS), :]
                for k in range(n_chan)
                for m in range(SEGS // n_chan)
            ],
            axis=0,
        ).astype(F32)
        k = lax.broadcasted_iota(jnp.int32, (TM, 1), 0)
        place = k // SEGS * seg_len + lax.rem(k, SEGS) + SEGS * i
        part = (part * jnp.where(place < live_rows, 1.0, 0.0)).astype(BF)
        sd[rows_of(i, TM), :] = dot(swap[...], part, 1, 0).astype(BF)

    load_tok.wait()
    tiles(n_tiles, order_tokens)
    for g in gather_a:
        g.plane()
    for g in gather_b + gather_o + [gather_f[0], gather_f[2]]:
        g.along()
    for g in gather_a:
        g.turn()
    for g in gather_b:
        g.plane()
    for g in gather_a:
        g.cross()
    for g in gather_a:
        g.ready()

    for copy in par_copies:
        copy.wait()
    par = parx[0] + parx[1] + parx[2] + parx[3]
    bias = par[0:1, :]
    cos1, sin1 = par[1:2, :], par[2:3, :]
    gain_r, gain_i = par[3:4, :], par[4:5, :]
    rms_gain = jnp.concatenate([rms_ref[k : k + 1, :] for k in range(width // 128)], axis=1)
    cos16 = jnp.broadcast_to(cos1, (SEGS, half))
    sin16 = jnp.broadcast_to(sin1, (SEGS, half))

    def power(count):
        rr, ri = cos1, sin1
        while count > 1:
            rr, ri = rr * rr - ri * ri, 2.0 * rr * ri
            count //= 2
        return rr, ri

    seg_cos, seg_sin = power(seg_len)
    all_cos, all_sin = power(n_rows)

    def project(i):
        rows = rows_of(i, TM)
        x = tok[rows, :]
        for k in range(2):
            pre = dot(x, section(k), 1, 1)
            pv[rows, k * half : (k + 1) * half] = pre
            put(out, rows, k * lt, pre * sigmoid(pre))
        put(om, rows, 0, 1.0 / (1.0 + jnp.exp(dot(x, section(2), 1, 1) + bias)))

    tiles(n_tiles, project, {
        0: [g.plane for g in gather_o],
        2: [g.turn for g in gather_b],
    })

    def strided(t):
        return span(t * SEGS, SEGS)

    def first(t, carry):
        sr, si, prod = carry
        o = get(om, strided(t), 0, lt)
        f = 1.0 - o
        vr = get(out, strided(t), 0, lt)
        vi = get(out, strided(t), lt, lt)
        tr = cos16 * sr - sin16 * si
        ti = sin16 * sr + cos16 * si
        return f * tr + o * vr, f * ti + o * vi, prod * f

    zero = jnp.zeros((SEGS, half), F32)
    end_r, end_i, prod = lax.fori_loop(
        0, seg_len, first, (zero, zero, jnp.ones((SEGS, half), F32)), unroll=4
    )
    seg[0] = end_r
    seg[1] = end_i
    seg_prod[...] = prod

    def fold_forward(cr, ci, keep):
        total = jnp.ones((1, half), F32)
        for s in range(SEGS):
            if keep:
                seg[2, s : s + 1, :] = cr
                seg[3, s : s + 1, :] = ci
            p = seg_prod[s : s + 1, :]
            ar, ai = p * seg_cos, p * seg_sin
            cr, ci = (
                ar * cr - ai * ci + seg[0, s : s + 1, :],
                ar * ci + ai * cr + seg[1, s : s + 1, :],
            )
            total = total * p
        return cr, ci, total

    zrow = jnp.zeros((1, half), F32)
    er, ei, total = fold_forward(zrow, zrow, False)
    carx[c, 0:1, :] = er
    carx[c, 1:2, :] = ei
    carx[c, 2:3, :] = total * all_cos * not_start
    carx[c, 3:4, :] = total * all_sin * not_start
    to_later, from_earlier = chain(carx, car_send, car_recv, True)
    to_later()
    for g in gather_b:
        g.cross()
    for g in gather_o:
        g.turn()
    gather_f[0].plane()
    for copy in load_cot:
        copy.wait()
    tiles(n_tiles, order_seed)
    from_earlier()
    gather_f[1].along()
    cr, ci = zrow, zrow
    for k in range(n_chan - 1):
        ar, ai = carx[k, 2:3, :], carx[k, 3:4, :]
        nr = ar * cr - ai * ci + carx[k, 0:1, :]
        ni = ar * ci + ai * cr + carx[k, 1:2, :]
        cr = jnp.where(k < c, nr, cr)
        ci = jnp.where(k < c, ni, ci)
    fold_forward(cr * not_start, ci * not_start, True)

    def second(t, carry):
        sr, si = carry
        o = get(om, strided(t), 0, lt)
        f = 1.0 - o
        vr = get(out, strided(t), 0, lt)
        vi = get(out, strided(t), lt, lt)
        tr = cos16 * sr - sin16 * si
        ti = sin16 * sr + cos16 * si
        put(ws, strided(t), 0, tr)
        put(ws, strided(t), lt, ti)
        return f * tr + o * vr, f * ti + o * vi

    lax.fori_loop(0, seg_len, second, (seg[2], seg[3]), unroll=4)
    for g in gather_b:
        g.ready()

    def project_gate(i):
        rows = rows_of(i, TM)
        x = tok[rows, :]
        for k in range(2):
            pg[rows, k * half : (k + 1) * half] = dot(x, section(3 + k), 1, 1)

    tiles(n_tiles, project_gate, {2: [g.cross for g in gather_o]})
    for g in gather_o:
        g.ready()

    def mixer_out(i):
        rows = rows_of(i, TM)
        o = get(om, rows, 0, lt)
        f = 1.0 - o
        gr, gi = pg[rows, :half], pg[rows, half:]
        yr = gr * sigmoid(gr) * (f * get(ws, rows, 0, lt) + o * get(out, rows, 0, lt))
        yi = gi * sigmoid(gi) * (f * get(ws, rows, lt, lt) + o * get(out, rows, lt, lt))
        mean = head_mean(yr + yi, True)
        yr, yi = yr - mean, yi - mean
        inv = lax.rsqrt(head_mean(yr * yr + yi * yi) + 1e-5)
        yr, yi = yr * inv, yi * inv
        rstd[rows, :] = inv
        xh[rows, :half] = yr
        xh[rows, half:] = yi
        lr, li = (yr * gain_r).astype(BF), (yi * gain_i).astype(BF)
        mix[rows, :half] = lr
        mix[rows, half:] = li
        r = tok[rows, :].astype(F32) + (
            dot(lr, out_rows(0), 1, 0) + dot(li, out_rows(1), 1, 0)
        )
        res[rows, :] = r
        put(out, rows, 0, r)
        rinv = lax.rsqrt(jnp.mean(r * r, axis=1, keepdims=True) + 1e-6)
        fin[rows, :] = (r * rinv * rms_gain).astype(BF)
        dff[rows, :] = jnp.zeros((TM, width), F32)

    tiles(n_tiles, mixer_out, {
        0: [gather_f[0].turn],
        1: [gather_f[2].plane],
        3: [gather_f[0].cross],
    })

    for j in range(n_chan):
        cc = lax.rem(c + j, n_chan)

        def feed(i, cc=cc):
            rows = rows_of(i, TM)
            gate_up = dot(fin[rows, :], w[cc, WG0:WD0, :], 1, 1)
            d_hid = dot(sd[rows, :], w[cc, WD0:PIECE, :], 1, 1)
            gate, up = gate_up[:, :hw], gate_up[:, hw:]
            sig = sigmoid(gate)
            act = gate * sig
            h = (act * up).astype(BF)
            hid[rows, :] = h
            dg = (d_hid * up * (sig + act * (1.0 - sig))).astype(BF)
            du = (d_hid * act).astype(BF)
            dgu[rows, :hw] = dg
            dgu[rows, hw:] = du
            put(out, rows, 0, get(out, rows, 0, 2 * lt) + dot(h, w[cc, WD0:PIECE, :], 1, 0))
            dff[rows, :] += dot(dgu[rows, :], w[cc, WG0:WD0, :], 1, 0)

        if j == 0:
            tiles(n_tiles, feed, {
                0: [gather_f[2].turn],
                1: [gather_f[1].plane],
                3: [gather_f[2].cross],
            })
            for g in gather_f:
                g.along_free()
            gather_f[0].ready()
        else:
            before = reduce_f[j - 1]
            older = [reduce_f[j - 2]] if j > 1 else []
            if j > 1:
                gather_f[j - 1].ready()
            tiles(n_tiles, feed, {
                1: [r.turn for r in older],
                2: [before.to_plane],
                **({0: [gather_f[1].turn], 3: [gather_f[1].cross]} if j == 1 else {}),
            })
            gather_f[j - 1].free()
        for k in range(2):
            w[cc, WG0 + hw * k : WG0 + hw * (k + 1), :] = dot(
                dgu[:n_rows, hw * k : hw * (k + 1)], fin[...], 0, 0
            ).astype(BF)
        w[cc, WD0:PIECE, :] = dot(hid[...], sd[...], 0, 0).astype(BF)
        if j > 1:
            older[0].along()
        reduce_f[j].to_core()

    def mixer_back(i):
        rows = rows_of(i, TM)
        done = dot(swap[...], get(out, rows, 0, 2 * lt).astype(BF), 1, 0).astype(BF)
        for k, at in enumerate(blocks(i)):
            fin[at, :] = done[SEGS * k : SEGS * (k + 1), :]
        r = res[rows, :]
        rinv = lax.rsqrt(jnp.mean(r * r, axis=1, keepdims=True) + 1e-6)
        rhat = r * rinv
        d = dff[rows, :]
        sgrad[2] += fold_rows(d * rhat)
        t = d * rms_gain
        dres = sd[rows, :].astype(F32) + rinv * (
            t - rhat * jnp.mean(t * rhat, axis=1, keepdims=True)
        )
        dff[rows, :] = dres
        low = dres.astype(BF)
        dm[i * TM // per, span(lax.rem(i * TM, per), TM), :] = low
        dr = dot(low, out_rows(0), 1, 1)
        di = dot(low, out_rows(1), 1, 1)
        xr, xi = xh[rows, :half], xh[rows, half:]
        sgrad[1, :, :half] += fold_rows(dr * xr)
        sgrad[1, :, half:] += fold_rows(di * xi)
        dr, di = dr * gain_r, di * gain_i
        m1 = head_mean(dr + di)
        m2 = head_mean(dr * xr + di * xi)
        inv = rstd[rows, :]
        dr = inv * (dr - m1 - xr * m2)
        di = inv * (di - m1 - xi * m2)
        o = get(om, rows, 0, lt)
        f = 1.0 - o
        for k, dy in ((0, dr), (1, di)):
            cols = slice(k * half, (k + 1) * half)
            pre = pv[rows, cols]
            state = f * get(ws, rows, k * lt, lt) + o * (pre * sigmoid(pre))
            g = pg[rows, cols]
            sig = sigmoid(g)
            act = g * sig
            dp[rows, (3 + k) * half : (4 + k) * half] = (
                dy * state * (sig + act * (1.0 - sig))
            ).astype(BF)
            put(out, rows, k * lt, dy * act)
        acc = dff[rows, :]
        for k in range(3, 5):
            acc += dot(dp[rows, k * half : (k + 1) * half], section(k), 1, 0)
        dff[rows, :] = acc

    tiles(n_tiles, mixer_back, {
        1: [reduce_f[-2].turn, reduce_f[-1].to_plane],
    })
    out_copy = pltpu.make_async_copy(fin, out_hbm, store_sem.at[0])
    out_copy.start()

    reduce_f[-1].turn()

    def first_back(k, carry):
        qr, qi = carry
        t = seg_len - 1 - k
        f = 1.0 - get(om, strided(t), 0, lt)
        lr = get(out, strided(t), 0, lt) + qr
        li = get(out, strided(t), lt, lt) + qi
        return f * (cos16 * lr + sin16 * li), f * (cos16 * li - sin16 * lr)

    qr, qi = lax.fori_loop(0, seg_len, first_back, (zero, zero), unroll=4)
    seg[0] = qr
    seg[1] = qi

    def fold_back(cr, ci, keep):
        for s in range(SEGS - 1, -1, -1):
            if keep:
                seg[2, s : s + 1, :] = cr
                seg[3, s : s + 1, :] = ci
            p = seg_prod[s : s + 1, :]
            ar, ai = p * seg_cos, -(p * seg_sin)
            cr, ci = (
                ar * cr - ai * ci + seg[0, s : s + 1, :],
                ar * ci + ai * cr + seg[1, s : s + 1, :],
            )
        return cr, ci

    er, ei = fold_back(zrow, zrow, False)
    carb[c, 0:1, :] = er * not_start
    carb[c, 1:2, :] = ei * not_start
    carb[c, 2:4, :] = carx[c, 2:4, :]
    to_earlier, from_later = chain(carb, cab_send, cab_recv, False)
    to_earlier()
    reduce_f[-2].along()

    for g in gather_a + gather_b + gather_o:
        g.along_free()
        g.free()
    d_mixed = jnp.concatenate([dm[k, :per, :] for k in range(n_chan)], axis=0)
    for k in range(4):
        left = mix[:, k * half : (k + 1) * half] if k < 2 else dp[:, (k + 1) * half : (k + 2) * half]
        grad = dot(left, d_mixed if k < 2 else tok[...], 0, 0).astype(BF)
        to = WO0 + 96 * k if k < 2 else SECTION[k + 1]
        for cc in range(n_chan):
            w[cc, to : to + 96, :] = grad[96 * cc : 96 * cc + 96, :]
        if k == 1:
            reduce_o.to_core()
    reduce_o.to_plane()
    reduce_g.to_core()

    from_later()
    reduce_f[-1].along()
    cr, ci = zrow, zrow
    for k in range(n_chan - 1, 0, -1):
        ar, ai = carb[k, 2:3, :], -carb[k, 3:4, :]
        nr = ar * cr - ai * ci + carb[k, 0:1, :]
        ni = ar * ci + ai * cr + carb[k, 1:2, :]
        cr = jnp.where(k > c, nr, cr)
        ci = jnp.where(k > c, ni, ci)
    fold_back(cr, ci, True)

    def second_back(k, carry):
        qr, qi = carry
        t = seg_len - 1 - k
        f = 1.0 - get(om, strided(t), 0, lt)
        lr = get(out, strided(t), 0, lt) + qr
        li = get(out, strided(t), lt, lt) + qi
        put(out, strided(t), 0, lr)
        put(out, strided(t), lt, li)
        return f * (cos16 * lr + sin16 * li), f * (cos16 * li - sin16 * lr)

    lax.fori_loop(0, seg_len, second_back, (seg[2], seg[3]), unroll=4)
    def project_back(i):
        rows = rows_of(i, TM)
        o = get(om, rows, 0, lt)
        f = 1.0 - o
        df = jnp.zeros((TM, half), F32)
        for k in range(2):
            cols = slice(k * half, (k + 1) * half)
            pre = pv[rows, cols]
            sig = sigmoid(pre)
            act = pre * sig
            lam = get(out, rows, k * lt, lt)
            df += lam * (get(ws, rows, k * lt, lt) - act)
            dp[rows, cols] = (o * lam * (sig + act * (1.0 - sig))).astype(BF)
        dx = df * f * o
        dp[rows, 2 * half : 3 * half] = dx.astype(BF)
        sgrad[0, :, :half] += fold_rows(dx)
        sgrad[0, :, half:] += fold_rows(
            f
            * (
                get(out, rows, lt, lt) * get(ws, rows, 0, lt)
                - get(out, rows, 0, lt) * get(ws, rows, lt, lt)
            )
        )

    reduce_g.to_plane()
    tiles(n_tiles, project_back)
    for k in range(3):
        grad = dot(dp[:, k * half : (k + 1) * half], tok[...], 0, 0).astype(BF)
        for cc in range(n_chan):
            dm[cc, 96 * k : 96 * k + 96, :] = grad[96 * cc : 96 * cc + 96, :]
        if k == 1:
            reduce_v.to_core()
            reduce_o.turn()
    small = jnp.concatenate(
        [jnp.sum(sgrad[k], axis=0, keepdims=True) for k in range(3)]
        + [jnp.zeros((29, width), F32)],
        axis=0,
    ).astype(BF)
    for cc in range(n_chan):
        dm[cc, PAD0:MA0, :] = small
    reduce_k.to_core()
    def d_tokens(i):
        rows = rows_of(i, TM)
        acc = dff[rows, :]
        for k in range(3):
            acc += dot(dp[rows, k * half : (k + 1) * half], section(k), 1, 0)
        high = acc.astype(BF)
        low = (acc - high.astype(F32)).astype(BF)
        done = dot(swap[...], high, 1, 0) + dot(swap[...], low, 1, 0)
        for k, at in enumerate(blocks(i)):
            res[at, :] = done[SEGS * k : SEGS * (k + 1), :]

    tiles(n_tiles, d_tokens, {
        1: [reduce_v.to_plane, reduce_g.turn],
        2: [reduce_o.along, reduce_k.to_plane],
    })
    gtok_copy = pltpu.make_async_copy(res, gtok_hbm, store_sem.at[1])
    gtok_copy.start()
    reduce_v.turn()
    reduce_k.turn()
    spread_f.total()
    reduce_g.along()
    reduce_v.along()
    reduce_k.along()
    spread_o.total()
    spread_f.turn()
    spread_g.total()
    spread_v.total()
    spread_k.total()
    spread_f.cross()
    for sp in (spread_o, spread_g, spread_v, spread_k):
        sp.cross()
    spread_f.done()
    g_copies = [pltpu.make_async_copy(dgu, g_hbm.at[WG0:PIECE, :], store_sem.at[2])]
    g_copies[0].start()
    for sp in (spread_o, spread_g, spread_v, spread_k):
        sp.done()
    g_copies.append(pltpu.make_async_copy(mixf, g_hbm.at[:WG0, :], store_sem.at[3]))
    g_copies[1].start()
    for r in reduce_f + [reduce_o, reduce_g, reduce_v, reduce_k]:
        r.free()
    for copy in [out_copy, gtok_copy] + g_copies:
        copy.wait()


def post_kernel(
    g_hbm, gtok_hbm, out_hbm,
    win_ref, wf_ref, bf_ref, rot_ref, wg_ref, gn_ref, wout_ref, rms_ref, gate_ref, up_ref,
    down_ref, gtok_ref, out_ref,
    g, t_in, t_f, t_g, t_out, t_gate, t_up, t_down, t_gtok, t_block, rows8, load_sem, store_sem,
):
    nch = bf_ref.shape[1]
    heads = nch // HEAD_CH
    hw = (WD0 - WG0) // 2
    half = g.shape[1] // 2
    c = lax.axis_index("chan")
    cuts = (0, MA0, WG0, WG0 + hw, WD0, PIECE)
    loads = []
    for k in range(5):
        rows = pl.ds(cuts[k], cuts[k + 1] - cuts[k])
        loads.append(pltpu.make_async_copy(g_hbm.at[rows, :], g.at[rows, :], load_sem.at[k]))
        loads[-1].start()
    stage = [
        pltpu.make_async_copy(gtok_hbm, t_gtok, load_sem.at[5]),
        pltpu.make_async_copy(out_hbm, t_block, load_sem.at[6]),
    ]
    for copy in stage:
        copy.start()
    stores = []

    def store(src, dst):
        copy = pltpu.make_async_copy(src, dst, store_sem.at[len(stores)])
        copy.start()
        stores.append(copy)

    def joined(first):
        return jnp.concatenate(
            [
                g[first + nch * part + HEAD_CH * hh : first + nch * part + HEAD_CH * (hh + 1), :]
                for hh in range(heads)
                for part in range(2)
            ],
            axis=0,
        )

    loads[0].wait()
    t_in[...] = joined(0).astype(F32)
    store(t_in, win_ref)
    t_f[...] = g[2 * nch : 3 * nch, :].astype(F32)
    store(t_f, wf_ref)
    small = g[PAD0 : PAD0 + 16, :].astype(F32)
    turn = lax.rem(4 - c, 4) * nch
    rows8[0:8, :half] = pltpu.roll(small[0:8, :half], turn, 1)
    rows8[0:8, half:] = pltpu.roll(small[0:8, half:], turn, 1)
    bf_ref[...] = rows8[0:1, :nch]
    rot_ref[...] = rows8[0:1, half : half + nch]
    for hh in range(heads):
        for part in range(2):
            at = half * part + HEAD_CH * hh
            to = HEAD_CH * (2 * hh + part)
            gn_ref[:, to : to + HEAD_CH] = rows8[1:2, at : at + HEAD_CH]
    rows8[8:16, :] = pltpu.roll(small[0:8, :], 2 * turn, 1)
    rms_ref[...] = rows8[10:11, : 2 * nch]
    loads[1].wait()
    t_g[...] = joined(MA0).astype(F32)
    store(t_g, wg_ref)
    t_out[...] = joined(WO0).astype(F32)
    store(t_out, wout_ref)
    loads[2].wait()
    t_gate[...] = g[WG0 : WG0 + hw, :].T.astype(F32)
    store(t_gate, gate_ref)
    loads[3].wait()
    t_up[...] = g[WG0 + hw : WD0, :].T.astype(F32)
    store(t_up, up_ref)
    loads[4].wait()
    t_down[...] = g[WD0:PIECE, :].astype(F32)
    store(t_down, down_ref)
    for copy, src, dst in zip(stage, (t_gtok, t_block), (gtok_ref, out_ref), strict=True):
        copy.wait()
        store(src, dst)
    for copy in stores:
        copy.wait()


def post_call(g, grad_tokens, block_out, nch):
    width = g.shape[1]
    hw = (WD0 - WG0) // 2
    any_spec = pl.BlockSpec(memory_space=pl.ANY)
    vmem = pl.BlockSpec(memory_space=pltpu.VMEM)
    big = [(2 * nch, width), (nch, width), (2 * nch, width), (2 * nch, width), (width, hw),
           (width, hw), (hw, width)]
    shapes = [big[0], big[1], (1, nch), (1, nch), big[2], (1, 2 * nch), big[3], (1, 2 * nch),
              big[4], big[5], big[6], grad_tokens.shape]
    return pl.pallas_call(
        post_kernel,
        out_shape=[jax.ShapeDtypeStruct(shape, F32) for shape in shapes]
        + [jax.ShapeDtypeStruct(block_out.shape, BF)],
        in_specs=[any_spec] * 3,
        out_specs=[vmem if shape[0] == 1 else any_spec for shape in shapes] + [any_spec],
        scratch_shapes=[pltpu.VMEM(g.shape, BF)]
        + [pltpu.VMEM(shape, F32) for shape in big + [grad_tokens.shape]]
        + [
            pltpu.VMEM(block_out.shape, BF),
            pltpu.VMEM((16, width), F32),
            pltpu.SemaphoreType.DMA((7,)),
            pltpu.SemaphoreType.DMA((9,)),
        ],
        compiler_params=pltpu.CompilerParams(vmem_limit_bytes=60 * 2**20),
        name="place",
    )(g, grad_tokens, block_out)


def main_call(weights, tokens, cotangent, vectors, bucket, lengths):
    rows, width = tokens.shape
    half = width // 2
    nch = vectors[0].shape[1]
    n_chan, n_batch = lax.axis_size("chan"), lax.axis_size("batch")
    n_extra = max(1, n_batch.bit_length() - 4)
    w_shape = (n_chan, PIECE, width)
    hw = (WD0 - WG0) // 2
    any_spec = pl.BlockSpec(memory_space=pl.ANY)
    vmem = pl.BlockSpec(memory_space=pltpu.VMEM)
    smem = pl.BlockSpec(memory_space=pltpu.SMEM)
    full32 = pltpu.VMEM((rows, width), F32)
    half32 = pltpu.VMEM((rows, half), F32)
    tiles32 = pltpu.VMEM((width // 128, rows, 128), F32)
    full16 = pltpu.VMEM((rows, width), BF)
    return pl.pallas_call(
        functools.partial(main_kernel, n_batch, n_chan),
        out_shape=[
            jax.ShapeDtypeStruct((PIECE, width), BF),
            jax.ShapeDtypeStruct((rows, width), F32),
            jax.ShapeDtypeStruct((rows, width), BF),
        ],
        in_specs=[any_spec] * 9 + [vmem] * 4 + [smem, smem],
        out_specs=[any_spec] * 3,
        scratch_shapes=[
            pltpu.VMEM(w_shape, BF),
            full16, full16, full32, pltpu.VMEM((half // 128, rows, 128), F32), full32, tiles32,
            full32, half32, full32, full16, full16, tiles32, full32,
            pltpu.VMEM((rows, hw), BF), pltpu.VMEM((PIECE - WG0, 2 * hw), BF),
            pltpu.VMEM((n_chan, MA0, width), BF), pltpu.VMEM((rows, 5 * half), BF),
            pltpu.VMEM((half, half), BF),
            pltpu.VMEM((TM, TM), BF),
            pltpu.VMEM((n_chan, 8, half), F32),
            pltpu.VMEM((n_chan, 8, half), F32),
            pltpu.VMEM((n_chan, 8, half), F32),
            pltpu.VMEM((4, SEGS, half), F32),
            pltpu.VMEM((3, 8, width), F32),
            pltpu.VMEM((SEGS, half), F32),
            pltpu.VMEM((2, 1, PIECE - WG0, half), BF),
            pltpu.VMEM((2, 1, (PIECE - WG0) // 2, half), BF),
            pltpu.VMEM((2, 1, (PIECE - WG0) // 4, half), BF),
            pltpu.VMEM((3, n_chan, WG0 - WO0, half), BF),
            pltpu.VMEM((3, n_chan, (WG0 - WO0) // 2, half), BF),
            pltpu.VMEM((3, n_chan, (WG0 - WO0) // 4, half), BF),
            pltpu.VMEM((n_chan - 1, (PIECE - WG0) // 4, half), BF),
            pltpu.VMEM((4, n_chan - 1, (WG0 - WO0) // 4, half), BF),
            pltpu.VMEM((WG0, width), BF),
            pltpu.VMEM((n_extra, (PIECE + 64) // 4, half) if n_batch > 8 else (1, 16, 128), BF),
            pltpu.VMEM((8, half), F32),
            pltpu.SemaphoreType.DMA((5 + n_chan + 6 * nch // HEAD_CH,)),
            pltpu.SemaphoreType.DMA((4,)),
        ]
        + [pltpu.SemaphoreType.DMA((n_chan,))] * 6
        + [pltpu.SemaphoreType.DMA((4 * (n_chan - 1), 9))] * 2
        + [pltpu.SemaphoreType.DMA((n_chan + 4, 10))] * 2
        + [pltpu.SemaphoreType.DMA((5, 6))] * 2
        + [pltpu.SemaphoreType.DMA((5, n_extra))] * 2,
        compiler_params=pltpu.CompilerParams(
            collective_id=0, has_side_effects=True, vmem_limit_bytes=62 * 2**20
        ),
        cost_estimate=pl.CostEstimate(
            flops=34 * 10**9, bytes_accessed=3 * 10**7, transcendentals=0
        ),
        name="block",
    )(*weights, tokens, cotangent, *vectors, bucket, lengths)


def local(
    tokens, w_in, w_forget, b_forget, rotation, w_outgate, gn_gain, w_out, rms_gain,
    w_gate, w_up, w_down, cotangent, buckets, lengths,
):
    g, grad_tokens, block_out = main_call(
        (w_in.T, w_forget.T, w_outgate.T, w_out, w_gate, w_up, w_down), tokens, cotangent,
        (b_forget[None], rotation[None], gn_gain[None], rms_gain.reshape(-1, 128)), buckets, lengths,
    )
    (
        grad_w_in, grad_w_forget, grad_b, grad_rot, grad_w_outgate, grad_gn, grad_w_out, grad_rms,
        grad_w_gate, grad_w_up, grad_w_down, grad_tokens, block_out,
    ) = post_call(g, grad_tokens, block_out, b_forget.shape[0])
    return (
        block_out, grad_tokens, grad_w_in.T, grad_w_forget.T, grad_b[0], grad_rot[0],
        grad_w_outgate.T, grad_gn[0], grad_w_out, grad_rms[0], grad_w_gate, grad_w_up, grad_w_down,
    )


def solution(mesh):
    both = P(("batch", "chan"), None)
    cols, rows, vec = P(None, "chan"), P("chan", None), P("chan")
    return jax.shard_map(
        local,
        mesh=mesh,
        in_specs=(
            both, cols, cols, vec, vec, cols, vec, rows, P(), cols, cols, rows, both,
            P("batch"), P("batch", None),
        ),
        out_specs=(
            both, both, cols, cols, vec, vec, cols, vec, rows, vec, cols, cols, rows,
        ),
        check_vma=False,
    )
```

```python
import functools

import jax
import jax.numpy as jnp
from jax import lax
from jax.experimental import pallas as pl
from jax.experimental.pallas import tpu as pltpu
from jax.sharding import PartitionSpec as P

MESH = pl.DeviceIdType.MESH
BF = jnp.bfloat16
F32 = jnp.float32
HEAD_CH = 32
SEGS = 16
TM = SEGS * SEGS
ORDER = (0, 1, 3, 2)
PAD0, MA0, WO0, WG0, WD0, PIECE = 288, 320, 512, 704, 1472, 1856
SECTION = (0, 96, 192, 320, 416)


def dot(left, right, left_dim, right_dim):
    return lax.dot_general(
        left, right, (((left_dim,), (right_dim,)), ((), ())), preferred_element_type=F32
    )


def rows_of(tile, size):
    return pl.ds(pl.multiple_of(tile * size, size), size)


def sigmoid(v):
    return 0.5 * jnp.tanh(0.5 * v) + 0.5


def tiles(count, body, steps=None):
    @pl.loop(0, count)
    def _(i):
        for at, calls in (steps or {}).items():

            @pl.when(i == at)
            def _(calls=calls):
                for call in calls:
                    call()

        body(i)


def get(ref, rows, first, count):
    return jnp.concatenate([ref[first + k, rows, :] for k in range(count)], axis=1)


def put(ref, rows, first, v):
    for k in range(v.shape[1] // 128):
        ref[first + k, rows, :] = v[:, 128 * k : 128 * (k + 1)]


def fold_rows(v):
    return jnp.sum(v.reshape(v.shape[0] // 8, 8, v.shape[1]), axis=0)


def main_kernel(
    n_batch, n_chan,
    win_hbm, wf_hbm, wg_hbm, wout_hbm, wgate_hbm, wup_hbm, wdown_hbm, tok_hbm, cot_hbm,
    bias_ref, rot_ref, gn_ref, rms_ref, bucket_ref, len_ref,
    g_hbm, gtok_hbm, out_hbm,
    w, tok, sd, pv, om, pg, ws, xh, rstd, res, fin, mix, out, dff, hid, dgu, dm, dp,
    ones, swap, parx, carx, carb, seg, sgrad, seg_prod,
    rb0, rb1, rb2, mb0, mb1, mb2, zbf, zbq, zbm, mixf, extra,
    par_own,
    load_sem, store_sem, par_send, par_recv, car_send, car_recv, cab_send, cab_recv,
    ag_send, ag_recv, rs_send, rs_recv, fin_send, fin_recv, ex_send, ex_recv,
):
    n_rows, width = tok.shape
    half = width // 2
    lt = half // 128
    n_tiles = n_rows // TM
    seg_len = n_rows // SEGS
    b = lax.axis_index("batch")
    c = lax.axis_index("chan")
    peers = [lax.rem(c + j, n_chan) for j in range(1, n_chan)]
    core = lax.rem(b, 2)
    quarter = lax.rem(b // 2, 4)
    x_bit, y_bit = lax.rem(quarter, 2), quarter // 2

    def flip(bit):
        here = b
        for k in range(n_batch.bit_length()):
            if bit >> k & 1:
                here = here + (1 << k) - (2 << k) * lax.rem(b // (1 << k), 2)
        return here

    core_dev, x_dev, y_dev, diag_dev = ((flip(bit), c) for bit in (1, 2, 4, 6))
    extra_devs = [(flip(1 << k), c) for k in range(3, n_batch.bit_length() - 1)]
    mine = pl.ds(pl.multiple_of(core * half, 128), half)
    theirs = pl.ds(pl.multiple_of((1 - core) * half, 128), half)

    def span(start, size):
        return pl.ds(pl.multiple_of(start, 16), size)

    def remote(src, dst, send_sem, recv_sem, device):
        return pltpu.make_async_remote_copy(
            src, dst, send_sem, recv_sem, device_id=device, device_id_type=MESH
        )

    nch = bias_ref.shape[1]
    heads = nch // HEAD_CH

    def load(src, dst, k):
        copy = pltpu.make_async_copy(src, dst, load_sem.at[k])
        copy.start()
        return copy

    def load_heads(src, first, at):
        return [
            load(
                src.at[HEAD_CH * (2 * hh + part) : HEAD_CH * (2 * hh + part + 1), :],
                w.at[c, pl.ds(first + nch * part + HEAD_CH * hh, HEAD_CH), :],
                at + 2 * hh + part,
            )
            for hh in range(heads)
            for part in range(2)
        ]

    load_first = load_heads(win_hbm, 0, 5 + n_chan) + [load(wf_hbm, w.at[c, pl.ds(2 * nch, nch), :], 0)]
    load_second = (
        load_heads(wg_hbm, MA0, 5 + n_chan + 2 * heads)
        + load_heads(wout_hbm, WO0, 5 + n_chan + 4 * heads)
    )
    load_gate = load(wgate_hbm, hid.at[:width, :], 1)
    load_up = load(wup_hbm, dgu.at[:width, : hid.shape[1]], 2)
    load_down = load(wdown_hbm, w.at[c, WD0:PIECE, :], 3)
    load_tok = load(tok_hbm, fin, 4)
    per = n_rows // n_chan
    load_cot = [
        load(cot_hbm.at[per * k : per * (k + 1), :], dm.at[k, :per, :], 5 + k) for k in range(n_chan)
    ]

    barrier = pltpu.get_barrier_semaphore()
    talk = [core_dev, x_dev, y_dev, diag_dev] + extra_devs + [(b, peer) for peer in peers]
    for device in talk:
        pl.semaphore_signal(barrier, inc=1, device_id=device, device_id_type=MESH)

    w[c, PAD0:MA0, :] = jnp.zeros((MA0 - PAD0, width), BF)
    par_own[...] = jnp.zeros_like(par_own)
    par_own[0:1, :nch] = bias_ref[...]
    par_own[1:2, :nch] = jnp.cos(rot_ref[...])
    par_own[2:3, :nch] = jnp.sin(rot_ref[...])
    for hh in range(heads):
        for part in range(2):
            at = HEAD_CH * (2 * hh + part)
            par_own[3 + part : 4 + part, HEAD_CH * hh : HEAD_CH * (hh + 1)] = gn_ref[
                :, at : at + HEAD_CH
            ]
    parx[c] = pltpu.roll(par_own[...], c * nch, 1)
    pl.semaphore_wait(barrier, len(talk))

    def exchange(ref, send_sem, recv_sem):
        copies = [
            remote(ref.at[c], ref.at[c], send_sem.at[j], recv_sem.at[j], (b, peer))
            for j, peer in enumerate(peers)
        ]
        return copies

    def chain(ref, send_sem, recv_sem, up):
        def each(out, call):
            for k in range(n_chan):
                above = c < k if out == up else c > k
                copy = remote(
                    ref.at[c] if out else ref.at[k], ref.at[c] if out else ref.at[k],
                    send_sem.at[k], recv_sem.at[c] if out else recv_sem.at[k], (b, k),
                )
                pl.when(above)(functools.partial(call, copy))

        def send():
            each(True, lambda copy: copy.start())

        def receive():
            each(False, lambda copy: copy.wait_recv())
            each(True, lambda copy: copy.wait_send())

        return send, receive

    class Gather:
        def __init__(self, unit, j, first, count, turns):
            self.first, self.count, self.turns = first, count, turns
            src = lax.rem(c + j, n_chan)
            peer = lax.rem(c + n_chan - j, n_chan)
            send, recv = ag_send.at[unit], ag_recv.at[unit]

            def copy(k, chan, rows, device):
                ref = w.at[chan, rows, mine]
                return remote(ref, ref, send.at[k], recv.at[k], device)

            from_x = y_bit * 2 + 1 - x_bit
            from_y = (1 - y_bit) * 2 + x_bit
            own = self.rows(quarter)
            self.z = copy(0, c, own, (b, peer))
            self.p1 = [copy(1, src, own, x_dev), copy(2, src, own, y_dev)]
            self.c1 = copy(3, src, own, core_dev)
            if turns:
                cut = count // 4 // 32 * 16
                cut = cut if unit // (n_chan - 1) % 2 else count // 4 - cut
                rest = count // 4 - cut
                self.p2 = [
                    copy(4, src, self.rows(from_x, 0, cut), y_dev),
                    copy(5, src, self.rows(from_y, cut, rest), x_dev),
                ]
            else:
                self.p2 = [copy(4, src, own, diag_dev)]
            self.c2 = [copy(6, src, self.rows(from_x), core_dev),
                       copy(7, src, self.rows(from_y), core_dev)]
            self.c3 = copy(8, src, self.rows(3 - quarter), core_dev)

        def rows(self, part, start=0, size=None):
            size = self.count // 4 if size is None else size
            return span(self.first + part * (self.count // 4) + start, size)

        def along(self):
            self.z.start()

        def plane(self):
            self.z.wait_recv()
            for copy in self.p1 + [self.c1] + ([] if self.turns else self.p2):
                copy.start()

        def turn(self):
            for copy in self.p1:
                copy.wait_recv()
            for copy in (self.p2 if self.turns else []) + self.c2:
                copy.start()

        def cross(self):
            for copy in self.p2:
                copy.wait_recv()
            self.c3.start()

        def ready(self):
            for copy in [self.c1] + self.c2 + [self.c3]:
                copy.wait_recv()

        def along_free(self):
            self.z.wait_send()

        def free(self):
            for copy in self.p1 + self.p2 + [self.c1] + self.c2 + [self.c3]:
                copy.wait_send()

    ring = range(1, n_chan)
    gather_v = [Gather(j - 1, j, 0, 2 * nch, True) for j in ring]
    gather_k = [Gather(11 + j, j, 2 * nch, MA0 - 2 * nch, True) for j in ring]
    gather_b = [Gather(2 + j, j, MA0, WO0 - MA0, True) for j in ring]
    gather_o = [Gather(5 + j, j, WO0, WG0 - WO0, True) for j in ring]
    gather_f = [Gather(8 + j, j, WG0, PIECE - WG0, True) for j in ORDER[1:]]

    place_f = [[buf.at[k] for buf in (rb0, rb1, rb2)] for k in range(2)]
    place_m = [[buf.at[k] for buf in (mb0, mb1, mb2)] for k in (0, 1, 2, 0)]

    class Reduce:
        def __init__(self, chunk, place, ref, dist, first, count, slots, late=False):
            chan = None if dist is None else lax.rem(c + dist, n_chan)
            self.ref, self.slots = ref, slots
            send, recv = rs_send.at[chunk], rs_recv.at[chunk]
            q = count // 4
            cut = q // 32 * 16 if chunk % 2 else q - q // 32 * 16
            rest = q - cut
            chans = pl.ds(0, n_chan) if chan is None else pl.ds(chan, 1)
            n = n_chan if chan is None else 1
            far_x = y_bit * 2 + 1 - x_bit
            far_y = (1 - y_bit) * 2 + x_bit

            def item(k, level, at, part, keep, start, size, cols, device):
                buf = place[level].at[:n, at : at + size, :]
                src = ref.at[chans, span(first + part * q + start, size), cols]
                to = chans, span(first + keep * q + start, size)
                return to, buf, size, remote(src, buf, send.at[k], recv.at[k], device)

            whole = place[0].at[:n, :count, :]
            src = ref.at[chans, first : first + count, theirs]
            self.s0 = [(
                (chans, pl.ds(first, count)), whole, count,
                remote(src, whole, send.at[0], recv.at[0], core_dev),
            )]
            self.s1 = []
            for k in range(2):
                self.s1.append(item(
                    1 + k, 1, k * cut, k * 2 + 1 - x_bit, k * 2 + x_bit, 0, cut, mine, x_dev))
                self.s1.append(item(
                    3 + k, 1, 2 * cut + k * rest, (1 - y_bit) * 2 + k, y_bit * 2 + k, cut, rest,
                    mine, y_dev))
            self.s2 = []
            if not (late and dist):
                self.s2 = [
                    item(5, 2, 0, far_y, quarter, 0, cut, mine, y_dev),
                    item(6, 2, cut, far_x, quarter, cut, rest, mine, x_dev),
                ]
            own = span(first + quarter * q, q)
            self.pairs = [(first + (k * 2 + x_bit) * q, cut, k * cut) for k in range(2)]
            self.pairs += [
                (first + (y_bit * 2 + k) * q + cut, rest, 2 * cut + k * rest) for k in range(2)
            ]
            if late and dist:
                self.s3 = [
                    remote(
                        ref.at[chan, span(start, size), mine],
                        slots.at[dist // 2, at : at + size, :],
                        send.at[7 + k], recv.at[7 + k], (b, chan),
                    )
                    for k, (start, size, at) in enumerate(self.pairs)
                ]
            elif dist:
                self.s3 = [remote(
                    ref.at[chan, own, mine], slots, send.at[7], recv.at[7], (b, chan)
                )]
            else:
                self.s3 = [
                    remote(
                        ref.at[lax.rem(c + j, n_chan), own, mine], slots.at[j - 1],
                        send.at[6 + j], recv.at[6 + j], (b, lax.rem(c + j, n_chan)),
                    )
                    for j in range(1, n_chan)
                    if dist is None
                ]
            self.sent = [it[-1] for it in self.s0 + self.s1 + self.s2] + self.s3

        def add(self, items):
            for (chans, rows), buf, size, copy in items:
                copy.wait_recv()
                step = 96 if buf.shape[0] == 1 else 16
                for at in range(0, size, step):
                    n = min(step, size - at)
                    here = self.ref.at[chans, span(rows.start + at, n), mine]
                    here[...] = here[...] + buf[:, at : at + n, :]

        def to_core(self):
            for item in self.s0:
                item[-1].start()

        def to_plane(self):
            self.add(self.s0)
            for item in self.s1:
                item[-1].start()

        def pair(self):
            self.add(self.s1)

        def send_along(self):
            for copy in self.s3:
                copy.start()

        def pair_along(self):
            self.pair()
            self.send_along()

        def collect(self, copies):
            for copy in copies:
                copy.wait_recv()
            for start, size, at in self.pairs:
                for k in range(0, size, 48):
                    here = span(start + k, 48)
                    v = self.ref[c, here, mine].astype(F32)
                    for j in range(self.slots.shape[0]):
                        v = v + self.slots[j, at + k : at + k + 48, :].astype(F32)
                    self.ref[c, here, mine] = v.astype(BF)
            for item in self.s2:
                item[-1].start()

        def turn(self):
            self.add(self.s1)
            for item in self.s2:
                item[-1].start()

        def along(self):
            self.add(self.s2)
            for copy in self.s3:
                copy.start()

        def free(self):
            for copy in self.sent:
                copy.wait_send()

    class Spread:
        def __init__(self, chunk, ref, first, count, slots, recvs, dest, dest_first, ex_at, turns=False):
            self.ref, self.first, self.q = ref, first, count // 4
            self.slots, self.recvs, self.dest = slots, recvs, dest
            send, recv = fin_send.at[chunk], fin_recv.at[chunk]
            self.at = span(dest_first + quarter * self.q, self.q)
            ref = dest.at[self.at, mine]
            self.copies = [
                remote(ref, ref, send.at[k], recv.at[k], device)
                for k, device in enumerate((x_dev, y_dev) if turns else (x_dev, y_dev, diag_dev))
            ]
            self.p2 = []
            if turns:
                cut = self.q // 32 * 16
                parts = (
                    (y_bit * 2 + 1 - x_bit, 0, cut, y_dev),
                    ((1 - y_bit) * 2 + x_bit, cut, self.q - cut, x_dev),
                )
                for k, (part, start, size, device) in enumerate(parts):
                    half_ref = dest.at[span(dest_first + part * self.q + start, size), mine]
                    self.p2.append(remote(
                        half_ref, half_ref, send.at[4 + k], recv.at[4 + k], device
                    ))
            ref_all = dest.at[dest_first : dest_first + count, mine]
            self.last = remote(ref_all, ref_all, send.at[3], recv.at[3], core_dev)
            self.extra = []
            for k, device in enumerate(extra_devs):
                buf = extra.at[k, ex_at : ex_at + self.q, :]
                self.extra.append((buf, remote(
                    ref, buf, ex_send.at[chunk, k], ex_recv.at[chunk, k], device
                )))

        def total(self):
            for copy in self.recvs:
                copy.wait_recv()
            v = self.ref[c, span(self.first + quarter * self.q, self.q), mine].astype(F32)
            for j in range(len(self.recvs)):
                v = v + self.slots[j][...].astype(F32)
            self.dest[self.at, mine] = v.astype(BF)
            for buf, copy in self.extra:
                copy.start()
                copy.wait()
                v = self.dest[self.at, mine].astype(F32) + buf[...].astype(F32)
                self.dest[self.at, mine] = v.astype(BF)
            for copy in self.copies:
                copy.start()

        def turn(self):
            for copy in self.copies:
                copy.wait_recv()
            for copy in self.p2:
                copy.start()

        def cross(self):
            for copy in self.p2 or self.copies:
                copy.wait_recv()
            self.last.start()

        def done(self):
            self.last.wait_recv()
            for copy in self.copies + self.p2 + [self.last]:
                copy.wait_send()

    f_rows = PIECE - WG0
    reduce_f = [
        Reduce(k, place_f[k % 2], w, j, WG0, f_rows, zbf if j != 2 else zbq, j != 2)
        for k, j in enumerate(ORDER)
    ]
    reduce_o = Reduce(n_chan, place_m[0], sd, None, 0, WG0 - WO0, zbm.at[0])
    reduce_g = Reduce(n_chan + 1, place_m[1], w, None, WO0, WO0 - MA0, zbm.at[1])
    reduce_v = Reduce(n_chan + 2, place_m[2], dm, None, 0, 2 * nch, zbm.at[2])
    reduce_k = Reduce(
        n_chan + 3, place_m[3], dm, None, 2 * nch, MA0 - 2 * nch,
        zbm.at[3, :, : (MA0 - 2 * nch) // 4],
    )
    spread_f = Spread(0, w, WG0, f_rows, [zbq], reduce_f[-1].s3, dgu, 0, 0, True)
    at = [f_rows // 4 + k * (nch // 2) for k in range(4)]
    spread_o = Spread(1, sd, 0, WG0 - WO0, zbm.at[0], reduce_o.s3, mixf, WO0, at[0])
    spread_g = Spread(2, w, WO0, WO0 - MA0, zbm.at[1], reduce_g.s3, mixf, MA0, at[1])
    spread_v = Spread(3, dm, 0, 2 * nch, zbm.at[2], reduce_v.s3, mixf, 0, at[2])
    spread_k = Spread(
        4, dm, 2 * nch, MA0 - 2 * nch, zbm.at[3, :, : (MA0 - 2 * nch) // 4], reduce_k.s3, mixf,
        2 * nch, at[3],
    )

    for copy in load_first:
        copy.wait()
    par_copies = exchange(parx, par_send, par_recv)
    for copy in par_copies:
        copy.start()
    for g in gather_v + gather_k:
        g.along()
    for copy in load_second:
        copy.wait()
    hw = hid.shape[1]
    load_gate.wait()
    w[c, WG0 : WG0 + hw, :] = hid[:width, :].T
    load_up.wait()
    w[c, WG0 + hw : WD0, :] = dgu[:width, :hw].T
    load_down.wait()
    lane_r = lax.broadcasted_iota(jnp.int32, (half, half), 0) // HEAD_CH
    lane_c = lax.broadcasted_iota(jnp.int32, (half, half), 1) // HEAD_CH
    ones[...] = jnp.where(lane_r == lane_c, 1.0 / (2 * HEAD_CH), 0.0).astype(BF)
    sgrad[...] = jnp.zeros_like(sgrad)
    row = lax.broadcasted_iota(jnp.int32, (TM, TM), 0)
    col = lax.broadcasted_iota(jnp.int32, (TM, TM), 1)
    swap[...] = jnp.where(row == lax.rem(col, SEGS) * SEGS + col // SEGS, 1.0, 0.0).astype(BF)

    def blocks(i):
        return [span(seg_len * k + SEGS * i, SEGS) for k in range(SEGS)]

    def head_mean(v, exact=False):
        high = v.astype(BF)
        if not exact:
            return dot(high, ones[...], 1, 0)
        low = (v - high.astype(F32)).astype(BF)
        return dot(high, ones[...], 1, 0) + dot(low, ones[...], 1, 0)

    bucket = bucket_ref[0]
    base = c * n_rows
    offset = jnp.bitwise_and(base, bucket - 1)
    slot_limit = len_ref[0, 0]
    for k in range(1, len_ref.shape[1]):
        slot_limit = jnp.where(base >= k * bucket, len_ref[0, k], slot_limit)
    live_rows = slot_limit - offset
    not_start = jnp.where(offset == 0, 0.0, 1.0).astype(F32)

    def section(k):
        return jnp.concatenate(
            [w[cc, SECTION[k] : SECTION[k] + 96, :] for cc in range(n_chan)], axis=0
        )

    def out_rows(k):
        return jnp.concatenate(
            [w[cc, WO0 + 96 * k : WO0 + 96 * k + 96, :] for cc in range(n_chan)], axis=0
        )

    def order_tokens(i):
        part = jnp.concatenate([fin[at, :] for at in blocks(i)], axis=0)
        tok[rows_of(i, TM), :] = dot(swap[...], part, 1, 0).astype(BF)

    def order_seed(i):
        part = jnp.concatenate(
            [
                dm[k, span(seg_len * m + SEGS * i, SEGS), :]
                for k in range(n_chan)
                for m in range(SEGS // n_chan)
            ],
            axis=0,
        ).astype(F32)
        k = lax.broadcasted_iota(jnp.int32, (TM, 1), 0)
        place = k // SEGS * seg_len + lax.rem(k, SEGS) + SEGS * i
        part = (part * jnp.where(place < live_rows, 1.0, 0.0)).astype(BF)
        sd[i] = dot(swap[...], part, 1, 0).astype(BF)

    load_tok.wait()
    tiles(n_tiles, order_tokens)
    for g in gather_v:
        g.plane()
    for copy in load_cot:
        copy.wait()
    tiles(n_tiles, order_seed)
    for g in gather_k:
        g.plane()
    for g in gather_b + gather_o + gather_f[:2]:
        g.along()
    for g in gather_v:
        g.turn()
    for g in gather_k:
        g.turn()
    for g in gather_v:
        g.cross()
    for g in gather_k:
        g.cross()
    for g in gather_v:
        g.ready()

    for copy in par_copies:
        copy.wait()
    par = parx[0] + parx[1] + parx[2] + parx[3]
    bias = par[0:1, :]
    cos1, sin1 = par[1:2, :], par[2:3, :]
    gain_r, gain_i = par[3:4, :], par[4:5, :]
    rms_gain = jnp.concatenate([rms_ref[k : k + 1, :] for k in range(width // 128)], axis=1)
    cos16 = jnp.broadcast_to(cos1, (SEGS, half))
    sin16 = jnp.broadcast_to(sin1, (SEGS, half))

    def power(count):
        rr, ri = cos1, sin1
        while count > 1:
            rr, ri = rr * rr - ri * ri, 2.0 * rr * ri
            count //= 2
        return rr, ri

    seg_cos, seg_sin = power(seg_len)
    all_cos, all_sin = power(n_rows)

    def project(i):
        rows = rows_of(i, TM)
        x = tok[rows, :]
        for k in range(2):
            pre = dot(x, section(k), 1, 1)
            pv[rows, k * half : (k + 1) * half] = pre
            put(out, rows, k * lt, pre * sigmoid(pre))

    def project_forget(i):
        rows = rows_of(i, TM)
        pre = dot(tok[rows, :], section(2), 1, 1) + bias
        put(om, rows, 0, 1.0 / (1.0 + jnp.exp(pre)))

    tiles(n_tiles, project, {1: [g.plane for g in gather_b]})
    for g in gather_k:
        g.ready()
    tiles(n_tiles, project_forget, {1: [g.plane for g in gather_o]})

    def strided(t):
        return span(t * SEGS, SEGS)

    def first(t, carry):
        sr, si, prod = carry
        o = get(om, strided(t), 0, lt)
        f = 1.0 - o
        vr = get(out, strided(t), 0, lt)
        vi = get(out, strided(t), lt, lt)
        tr = cos16 * sr - sin16 * si
        ti = sin16 * sr + cos16 * si
        return f * tr + o * vr, f * ti + o * vi, prod * f

    zero = jnp.zeros((SEGS, half), F32)
    end_r, end_i, prod = lax.fori_loop(
        0, seg_len, first, (zero, zero, jnp.ones((SEGS, half), F32)), unroll=4
    )
    seg[0] = end_r
    seg[1] = end_i
    seg_prod[...] = prod

    def fold_forward(cr, ci, keep):
        total = jnp.ones((1, half), F32)
        for s in range(SEGS):
            if keep:
                seg[2, s : s + 1, :] = cr
                seg[3, s : s + 1, :] = ci
            p = seg_prod[s : s + 1, :]
            ar, ai = p * seg_cos, p * seg_sin
            cr, ci = (
                ar * cr - ai * ci + seg[0, s : s + 1, :],
                ar * ci + ai * cr + seg[1, s : s + 1, :],
            )
            total = total * p
        return cr, ci, total

    zrow = jnp.zeros((1, half), F32)
    er, ei, total = fold_forward(zrow, zrow, False)
    carx[c, 0:1, :] = er
    carx[c, 1:2, :] = ei
    carx[c, 2:3, :] = total * all_cos * not_start
    carx[c, 3:4, :] = total * all_sin * not_start
    to_later, from_earlier = chain(carx, car_send, car_recv, True)
    to_later()
    for g in gather_b:
        g.turn()
    for g in gather_o:
        g.turn()
    gather_f[0].plane()
    for g in gather_b:
        g.cross()
    from_earlier()
    gather_f[2].along()
    cr, ci = zrow, zrow
    for k in range(n_chan - 1):
        ar, ai = carx[k, 2:3, :], carx[k, 3:4, :]
        nr = ar * cr - ai * ci + carx[k, 0:1, :]
        ni = ar * ci + ai * cr + carx[k, 1:2, :]
        cr = jnp.where(k < c, nr, cr)
        ci = jnp.where(k < c, ni, ci)
    fold_forward(cr * not_start, ci * not_start, True)

    def second(t, carry):
        sr, si = carry
        o = get(om, strided(t), 0, lt)
        f = 1.0 - o
        vr = get(out, strided(t), 0, lt)
        vi = get(out, strided(t), lt, lt)
        tr = cos16 * sr - sin16 * si
        ti = sin16 * sr + cos16 * si
        put(ws, strided(t), 0, tr)
        put(ws, strided(t), lt, ti)
        return f * tr + o * vr, f * ti + o * vi

    lax.fori_loop(0, seg_len, second, (seg[2], seg[3]), unroll=4)
    for g in gather_b:
        g.ready()

    def project_gate(i):
        rows = rows_of(i, TM)
        x = tok[rows, :]
        for k in range(2):
            pg[rows, k * half : (k + 1) * half] = dot(x, section(3 + k), 1, 1)

    tiles(n_tiles, project_gate, {2: [g.cross for g in gather_o]})
    for g in gather_o:
        g.ready()

    def mixer_out(i):
        rows = rows_of(i, TM)
        o = get(om, rows, 0, lt)
        f = 1.0 - o
        gr, gi = pg[rows, :half], pg[rows, half:]
        yr = gr * sigmoid(gr) * (f * get(ws, rows, 0, lt) + o * get(out, rows, 0, lt))
        yi = gi * sigmoid(gi) * (f * get(ws, rows, lt, lt) + o * get(out, rows, lt, lt))
        mean = head_mean(yr + yi, True)
        yr, yi = yr - mean, yi - mean
        inv = lax.rsqrt(head_mean(yr * yr + yi * yi) + 1e-5)
        yr, yi = yr * inv, yi * inv
        rstd[rows, :] = inv
        xh[rows, :half] = yr.astype(BF)
        xh[rows, half:] = yi.astype(BF)
        lr, li = (yr * gain_r).astype(BF), (yi * gain_i).astype(BF)
        mix[rows, :half] = lr
        mix[rows, half:] = li
        r = tok[rows, :].astype(F32) + (
            dot(lr, out_rows(0), 1, 0) + dot(li, out_rows(1), 1, 0)
        )
        res[rows, :] = r
        put(out, rows, 0, r)
        rinv = lax.rsqrt(jnp.mean(r * r, axis=1, keepdims=True) + 1e-6)
        fin[rows, :] = (r * rinv * rms_gain).astype(BF)
        dff[rows, :] = jnp.zeros((TM, width), F32)

    tiles(n_tiles, mixer_out, {
        1: [gather_f[0].turn],
        2: [gather_f[1].plane],
    })

    for j in range(n_chan):
        cc = lax.rem(c + ORDER[j], n_chan)

        def feed(i, cc=cc):
            rows = rows_of(i, 2 * TM)
            gate_up = dot(fin[rows, :], w[cc, WG0:WD0, :], 1, 1)
            d_hid = dot(jnp.concatenate([sd[2 * i], sd[2 * i + 1]], axis=0), w[cc, WD0:PIECE, :], 1, 1)
            gate, up = gate_up[:, :hw], gate_up[:, hw:]
            sig = sigmoid(gate)
            act = gate * sig
            h = (act * up).astype(BF)
            hid[rows, :] = h
            dg = (d_hid * up * (sig + act * (1.0 - sig))).astype(BF)
            du = (d_hid * act).astype(BF)
            dgu[rows, :hw] = dg
            dgu[rows, hw:] = du
            put(out, rows, 0, get(out, rows, 0, 2 * lt) + dot(h, w[cc, WD0:PIECE, :], 1, 0))
            dff[rows, :] += dot(dgu[rows, :], w[cc, WG0:WD0, :], 1, 0)

        if j == 0:
            tiles(n_tiles // 2, feed, {1: [gather_f[0].cross]})
            gather_f[1].turn()
            for g in gather_f:
                g.along_free()
            gather_f[0].ready()
        else:
            before = reduce_f[j - 1]
            older = [reduce_f[j - 2]] if j > 1 else []
            if j > 1:
                gather_f[j - 1].ready()
            tiles(n_tiles // 2, feed, {
                1: ([gather_f[1].cross] if j == 1 else [])
                + [r.pair_along for r in older] + [before.to_plane],
            })
            if j == 2:
                gather_f[2].cross()
            gather_f[j - 1].free()
        for k in range(2):
            w[cc, WG0 + hw * k : WG0 + hw * (k + 1), :] = dot(
                dgu[:n_rows, hw * k : hw * (k + 1)], fin[...], 0, 0
            ).astype(BF)
        seeds = jnp.concatenate([sd[k] for k in range(n_tiles)], axis=0)
        if j == 1:
            gather_f[2].turn()
        w[cc, WD0:PIECE, :] = dot(hid[...], seeds, 0, 0).astype(BF)
        reduce_f[j].to_core()
        if j == 0:
            gather_f[2].plane()

    def norm_back(i):
        rows = rows_of(i, TM)
        fin[rows, :] = get(out, rows, 0, 2 * lt).astype(BF)
        r = res[rows, :]
        rinv = lax.rsqrt(jnp.mean(r * r, axis=1, keepdims=True) + 1e-6)
        rhat = r * rinv
        d = dff[rows, :]
        sgrad[2] += fold_rows(d * rhat)
        t = d * rms_gain
        dres = sd[i].astype(F32) + rinv * (
            t - rhat * jnp.mean(t * rhat, axis=1, keepdims=True)
        )
        dff[rows, :] = dres
        dm[i, :TM, :] = dres.astype(BF)

    tiles(n_tiles, norm_back)
    reduce_f[-2].pair()
    d_mixed = jnp.concatenate([dm[k, :TM, :] for k in range(n_tiles)], axis=0)
    for k in range(2):
        grad = dot(mix[:, k * half : (k + 1) * half], d_mixed, 0, 0).astype(BF)
        for cc in range(n_chan):
            sd[cc, 96 * k : 96 * k + 96, :] = grad[96 * cc : 96 * cc + 96, :]
    reduce_o.to_core()
    reduce_f[-1].to_plane()

    def mixer_back(i):
        rows = rows_of(i, TM)
        low = dm[i, :TM, :]
        dr = dot(low, out_rows(0), 1, 1)
        di = dot(low, out_rows(1), 1, 1)
        xr, xi = xh[rows, :half].astype(F32), xh[rows, half:].astype(F32)
        sgrad[1, :, :half] += fold_rows(dr * xr)
        sgrad[1, :, half:] += fold_rows(di * xi)
        dr, di = dr * gain_r, di * gain_i
        m1 = head_mean(dr + di)
        m2 = head_mean(dr * xr + di * xi)
        inv = rstd[rows, :]
        dr = inv * (dr - m1 - xr * m2)
        di = inv * (di - m1 - xi * m2)
        o = get(om, rows, 0, lt)
        f = 1.0 - o
        for k, dy in ((0, dr), (1, di)):
            cols = slice(k * half, (k + 1) * half)
            pre = pv[rows, cols]
            state = f * get(ws, rows, k * lt, lt) + o * (pre * sigmoid(pre))
            g = pg[rows, cols]
            sig = sigmoid(g)
            act = g * sig
            dp[rows, (3 + k) * half : (4 + k) * half] = (
                dy * state * (sig + act * (1.0 - sig))
            ).astype(BF)
            put(out, rows, k * lt, dy * act)
    tiles(n_tiles, mixer_back, {2: [reduce_o.to_plane]})

    def collect_f():
        reduce_f[0].collect([copy for r in reduce_f[1:-1] for copy in r.s3])

    def own_f():
        reduce_f[0].add(reduce_f[0].s2)

    def first_back(k, carry):
        qr, qi = carry
        t = seg_len - 1 - k
        f = 1.0 - get(om, strided(t), 0, lt)
        lr = get(out, strided(t), 0, lt) + qr
        li = get(out, strided(t), lt, lt) + qi
        return f * (cos16 * lr + sin16 * li), f * (cos16 * li - sin16 * lr)

    qr, qi = lax.fori_loop(0, seg_len, first_back, (zero, zero), unroll=4)
    seg[0] = qr
    seg[1] = qi

    def fold_back(cr, ci, keep):
        for s in range(SEGS - 1, -1, -1):
            if keep:
                seg[2, s : s + 1, :] = cr
                seg[3, s : s + 1, :] = ci
            p = seg_prod[s : s + 1, :]
            ar, ai = p * seg_cos, -(p * seg_sin)
            cr, ci = (
                ar * cr - ai * ci + seg[0, s : s + 1, :],
                ar * ci + ai * cr + seg[1, s : s + 1, :],
            )
        return cr, ci

    er, ei = fold_back(zrow, zrow, False)
    carb[c, 0:1, :] = er * not_start
    carb[c, 1:2, :] = ei * not_start
    carb[c, 2:4, :] = carx[c, 2:4, :]
    to_earlier, from_later = chain(carb, cab_send, cab_recv, False)
    to_earlier()
    reduce_f[-2].send_along()

    for g in gather_v + gather_k + gather_b + gather_o:
        g.along_free()
        g.free()
    for k in range(2):
        grad = dot(dp[:, (3 + k) * half : (4 + k) * half], tok[...], 0, 0).astype(BF)
        for cc in range(n_chan):
            at = WO0 + 96 * k
            w[cc, at : at + 96, :] = grad[96 * cc : 96 * cc + 96, :]
    reduce_g.to_core()
    reduce_f[-1].turn()

    from_later()
    cr, ci = zrow, zrow
    for k in range(n_chan - 1, 0, -1):
        ar, ai = carb[k, 2:3, :], -carb[k, 3:4, :]
        nr = ar * cr - ai * ci + carb[k, 0:1, :]
        ni = ar * ci + ai * cr + carb[k, 1:2, :]
        cr = jnp.where(k > c, nr, cr)
        ci = jnp.where(k > c, ni, ci)
    fold_back(cr, ci, True)

    def second_back(k, carry):
        qr, qi = carry
        t = seg_len - 1 - k
        f = 1.0 - get(om, strided(t), 0, lt)
        lr = get(out, strided(t), 0, lt) + qr
        li = get(out, strided(t), lt, lt) + qi
        put(out, strided(t), 0, lr)
        put(out, strided(t), lt, li)
        return f * (cos16 * lr + sin16 * li), f * (cos16 * li - sin16 * lr)

    lax.fori_loop(0, seg_len, second_back, (seg[2], seg[3]), unroll=4)
    def project_back(i):
        rows = rows_of(i, TM)
        o = get(om, rows, 0, lt)
        f = 1.0 - o
        df = jnp.zeros((TM, half), F32)
        for k in range(2):
            cols = slice(k * half, (k + 1) * half)
            pre = pv[rows, cols]
            sig = sigmoid(pre)
            act = pre * sig
            lam = get(out, rows, k * lt, lt)
            df += lam * (get(ws, rows, k * lt, lt) - act)
            dp[rows, cols] = (o * lam * (sig + act * (1.0 - sig))).astype(BF)
        dx = df * f * o
        dp[rows, 2 * half : 3 * half] = dx.astype(BF)
        sgrad[0, :, :half] += fold_rows(dx)
        sgrad[0, :, half:] += fold_rows(
            f
            * (
                get(out, rows, lt, lt) * get(ws, rows, 0, lt)
                - get(out, rows, 0, lt) * get(ws, rows, lt, lt)
            )
        )

    tiles(n_tiles, project_back, {3: [reduce_f[-1].along]})
    reduce_o.turn()
    for k in range(3):
        grad = dot(dp[:, k * half : (k + 1) * half], tok[...], 0, 0).astype(BF)
        for cc in range(n_chan):
            dm[cc, 96 * k : 96 * k + 96, :] = grad[96 * cc : 96 * cc + 96, :]
        if k == 1:
            reduce_v.to_core()
            reduce_g.to_plane()
    small = jnp.concatenate(
        [jnp.sum(sgrad[k], axis=0, keepdims=True) for k in range(3)]
        + [jnp.zeros((29, width), F32)],
        axis=0,
    ).astype(BF)
    for cc in range(n_chan):
        dm[cc, PAD0:MA0, :] = small
    reduce_k.to_core()
    def order_out(i):
        done = dot(swap[...], fin[rows_of(i, TM), :], 1, 0).astype(BF)
        for k, at in enumerate(blocks(i)):
            mix[at, :] = done[SEGS * k : SEGS * (k + 1), :]

    def d_tokens(i):
        rows = rows_of(i, TM)
        acc = dff[rows, :]
        for k in range(5):
            acc += dot(dp[rows, k * half : (k + 1) * half], section(k), 1, 0)
        high = acc.astype(BF)
        low = (acc - high.astype(F32)).astype(BF)
        done = dot(swap[...], high, 1, 0) + dot(swap[...], low, 1, 0)
        for k, at in enumerate(blocks(i)):
            res[at, :] = done[SEGS * k : SEGS * (k + 1), :]

    tiles(n_tiles, d_tokens, {
        0: [reduce_o.along],
        1: [reduce_v.to_plane],
        2: [reduce_k.to_plane],
        3: [collect_f],
    })
    gtok_copy = pltpu.make_async_copy(res, gtok_hbm, store_sem.at[1])
    gtok_copy.start()
    reduce_v.turn()
    reduce_g.turn()
    reduce_k.turn()
    own_f()
    spread_f.total()
    tiles(n_tiles, order_out)
    out_copy = pltpu.make_async_copy(mix, out_hbm, store_sem.at[0])
    out_copy.start()
    reduce_v.along()
    spread_o.total()
    reduce_k.along()
    reduce_g.along()
    spread_f.turn()
    spread_v.total()
    spread_k.total()
    spread_f.cross()
    spread_o.cross()
    spread_g.total()
    for sp in (spread_v, spread_k, spread_g):
        sp.cross()
    spread_f.done()
    g_copies = [pltpu.make_async_copy(dgu, g_hbm.at[WG0:PIECE, :], store_sem.at[2])]
    g_copies[0].start()
    for sp in (spread_o, spread_g, spread_v, spread_k):
        sp.done()
    g_copies.append(pltpu.make_async_copy(mixf, g_hbm.at[:WG0, :], store_sem.at[3]))
    g_copies[1].start()
    for r in reduce_f + [reduce_o, reduce_g, reduce_v, reduce_k]:
        r.free()
    for copy in [out_copy, gtok_copy] + g_copies:
        copy.wait()


def post_kernel(
    g_hbm, gtok_hbm, out_hbm,
    win_ref, wf_ref, bf_ref, rot_ref, wg_ref, gn_ref, wout_ref, rms_ref, gate_ref, up_ref,
    down_ref, gtok_ref, out_ref,
    g, t_in, t_f, t_g, t_out, t_gate, t_up, t_down, t_gtok, t_block, rows8, load_sem, store_sem,
):
    nch = bf_ref.shape[1]
    heads = nch // HEAD_CH
    hw = (WD0 - WG0) // 2
    half = g.shape[1] // 2
    c = lax.axis_index("chan")
    cuts = (0, MA0, WG0, WG0 + hw, WD0, PIECE)
    loads = []
    for k in range(5):
        rows = pl.ds(cuts[k], cuts[k + 1] - cuts[k])
        loads.append(pltpu.make_async_copy(g_hbm.at[rows, :], g.at[rows, :], load_sem.at[k]))
        loads[-1].start()
    through = []
    for src, mid, dst in ((gtok_hbm, t_gtok, gtok_ref), (out_hbm, t_block, out_ref)):
        n = mid.shape[0] // 4
        for k in range(4):
            rows = pl.ds(n * k, n)
            sem = load_sem.at[5 + len(through)]
            through.append((
                pltpu.make_async_copy(src.at[rows, :], mid.at[rows, :], sem),
                mid.at[rows, :], dst.at[rows, :],
            ))
            through[-1][0].start()
    stores = []

    def store(src, dst):
        copy = pltpu.make_async_copy(src, dst, store_sem.at[len(stores)])
        copy.start()
        stores.append(copy)

    def pass_on(count):
        for _ in range(count):
            copy, mid, dst = through.pop(0)
            copy.wait()
            store(mid, dst)

    def joined(first):
        return jnp.concatenate(
            [
                g[first + nch * part + HEAD_CH * hh : first + nch * part + HEAD_CH * (hh + 1), :]
                for hh in range(heads)
                for part in range(2)
            ],
            axis=0,
        )

    loads[0].wait()
    t_in[...] = joined(0).astype(F32)
    store(t_in, win_ref)
    t_f[...] = g[2 * nch : 3 * nch, :].astype(F32)
    store(t_f, wf_ref)
    small = g[PAD0 : PAD0 + 16, :].astype(F32)
    turn = lax.rem(4 - c, 4) * nch
    rows8[0:8, :half] = pltpu.roll(small[0:8, :half], turn, 1)
    rows8[0:8, half:] = pltpu.roll(small[0:8, half:], turn, 1)
    bf_ref[...] = rows8[0:1, :nch]
    rot_ref[...] = rows8[0:1, half : half + nch]
    for hh in range(heads):
        for part in range(2):
            at = half * part + HEAD_CH * hh
            to = HEAD_CH * (2 * hh + part)
            gn_ref[:, to : to + HEAD_CH] = rows8[1:2, at : at + HEAD_CH]
    rows8[8:16, :] = pltpu.roll(small[0:8, :], 2 * turn, 1)
    rms_ref[...] = rows8[10:11, : 2 * nch]
    pass_on(1)
    loads[1].wait()
    t_g[...] = joined(MA0).astype(F32)
    store(t_g, wg_ref)
    t_out[...] = joined(WO0).astype(F32)
    store(t_out, wout_ref)
    pass_on(2)
    loads[2].wait()
    t_gate[...] = g[WG0 : WG0 + hw, :].T.astype(F32)
    store(t_gate, gate_ref)
    pass_on(2)
    loads[3].wait()
    t_up[...] = g[WG0 + hw : WD0, :].T.astype(F32)
    store(t_up, up_ref)
    pass_on(2)
    loads[4].wait()
    t_down[...] = g[WD0:PIECE, :].astype(F32)
    store(t_down, down_ref)
    pass_on(1)
    for copy in stores:
        copy.wait()


def post_call(g, grad_tokens, block_out, nch):
    width = g.shape[1]
    hw = (WD0 - WG0) // 2
    any_spec = pl.BlockSpec(memory_space=pl.ANY)
    vmem = pl.BlockSpec(memory_space=pltpu.VMEM)
    big = [(2 * nch, width), (nch, width), (2 * nch, width), (2 * nch, width), (width, hw),
           (width, hw), (hw, width)]
    shapes = [big[0], big[1], (1, nch), (1, nch), big[2], (1, 2 * nch), big[3], (1, 2 * nch),
              big[4], big[5], big[6], grad_tokens.shape]
    return pl.pallas_call(
        post_kernel,
        out_shape=[jax.ShapeDtypeStruct(shape, F32) for shape in shapes]
        + [jax.ShapeDtypeStruct(block_out.shape, BF)],
        in_specs=[any_spec] * 3,
        out_specs=[vmem if shape[0] == 1 else any_spec for shape in shapes] + [any_spec],
        scratch_shapes=[pltpu.VMEM(g.shape, BF)]
        + [pltpu.VMEM(shape, F32) for shape in big + [grad_tokens.shape]]
        + [
            pltpu.VMEM(block_out.shape, BF),
            pltpu.VMEM((16, width), F32),
            pltpu.SemaphoreType.DMA((13,)),
            pltpu.SemaphoreType.DMA((15,)),
        ],
        compiler_params=pltpu.CompilerParams(vmem_limit_bytes=60 * 2**20),
        name="place",
    )(g, grad_tokens, block_out)


def main_call(weights, tokens, cotangent, vectors, bucket, lengths):
    rows, width = tokens.shape
    half = width // 2
    nch = vectors[0].shape[1]
    n_chan, n_batch = lax.axis_size("chan"), lax.axis_size("batch")
    n_extra = max(1, n_batch.bit_length() - 4)
    w_shape = (n_chan, PIECE, width)
    hw = (WD0 - WG0) // 2
    any_spec = pl.BlockSpec(memory_space=pl.ANY)
    vmem = pl.BlockSpec(memory_space=pltpu.VMEM)
    smem = pl.BlockSpec(memory_space=pltpu.SMEM)
    full32 = pltpu.VMEM((rows, width), F32)
    half32 = pltpu.VMEM((rows, half), F32)
    tiles32 = pltpu.VMEM((width // 128, rows, 128), F32)
    full16 = pltpu.VMEM((rows, width), BF)
    return pl.pallas_call(
        functools.partial(main_kernel, n_batch, n_chan),
        out_shape=[
            jax.ShapeDtypeStruct((PIECE, width), BF),
            jax.ShapeDtypeStruct((rows, width), F32),
            jax.ShapeDtypeStruct((rows, width), BF),
        ],
        in_specs=[any_spec] * 9 + [vmem] * 4 + [smem, smem],
        out_specs=[any_spec] * 3,
        scratch_shapes=[
            pltpu.VMEM(w_shape, BF),
            full16, pltpu.VMEM((rows // TM, TM, width), BF), full32,
            pltpu.VMEM((half // 128, rows, 128), F32), full32, tiles32,
            full16, half32, full32, full16, full16, tiles32, full32,
            pltpu.VMEM((rows, hw), BF), pltpu.VMEM((PIECE - WG0, 2 * hw), BF),
            pltpu.VMEM((n_chan, MA0, width), BF), pltpu.VMEM((rows, 5 * half), BF),
            pltpu.VMEM((half, half), BF),
            pltpu.VMEM((TM, TM), BF),
            pltpu.VMEM((n_chan, 8, half), F32),
            pltpu.VMEM((n_chan, 8, half), F32),
            pltpu.VMEM((n_chan, 8, half), F32),
            pltpu.VMEM((4, SEGS, half), F32),
            pltpu.VMEM((3, 8, width), F32),
            pltpu.VMEM((SEGS, half), F32),
            pltpu.VMEM((2, 1, PIECE - WG0, half), BF),
            pltpu.VMEM((2, 1, (PIECE - WG0) // 2, half), BF),
            pltpu.VMEM((2, 1, (PIECE - WG0) // 4, half), BF),
            pltpu.VMEM((3, n_chan, WG0 - WO0, half), BF),
            pltpu.VMEM((3, n_chan, (WG0 - WO0) // 2, half), BF),
            pltpu.VMEM((3, n_chan, (WG0 - WO0) // 4, half), BF),
            pltpu.VMEM((2, (PIECE - WG0) // 2, half), BF),
            pltpu.VMEM(((PIECE - WG0) // 4, half), BF),
            pltpu.VMEM((4, n_chan - 1, (WG0 - WO0) // 4, half), BF),
            pltpu.VMEM((WG0, width), BF),
            pltpu.VMEM((n_extra, (PIECE + 64) // 4, half) if n_batch > 8 else (1, 16, 128), BF),
            pltpu.VMEM((8, half), F32),
            pltpu.SemaphoreType.DMA((5 + n_chan + 6 * nch // HEAD_CH,)),
            pltpu.SemaphoreType.DMA((4,)),
        ]
        + [pltpu.SemaphoreType.DMA((n_chan,))] * 6
        + [pltpu.SemaphoreType.DMA((5 * (n_chan - 1), 9))] * 2
        + [pltpu.SemaphoreType.DMA((n_chan + 4, 11))] * 2
        + [pltpu.SemaphoreType.DMA((5, 6))] * 2
        + [pltpu.SemaphoreType.DMA((5, n_extra))] * 2,
        compiler_params=pltpu.CompilerParams(
            collective_id=0, has_side_effects=True, vmem_limit_bytes=63 * 2**20
        ),
        cost_estimate=pl.CostEstimate(
            flops=34 * 10**9, bytes_accessed=3 * 10**7, transcendentals=0
        ),
        name="block",
    )(*weights, tokens, cotangent, *vectors, bucket, lengths)


def local(
    tokens, w_in, w_forget, b_forget, rotation, w_outgate, gn_gain, w_out, rms_gain,
    w_gate, w_up, w_down, cotangent, buckets, lengths,
):
    g, grad_tokens, block_out = main_call(
        (w_in.T, w_forget.T, w_outgate.T, w_out, w_gate, w_up, w_down), tokens, cotangent,
        (b_forget[None], rotation[None], gn_gain[None], rms_gain.reshape(-1, 128)), buckets, lengths,
    )
    (
        grad_w_in, grad_w_forget, grad_b, grad_rot, grad_w_outgate, grad_gn, grad_w_out, grad_rms,
        grad_w_gate, grad_w_up, grad_w_down, grad_tokens, block_out,
    ) = post_call(g, grad_tokens, block_out, b_forget.shape[0])
    return (
        block_out, grad_tokens, grad_w_in.T, grad_w_forget.T, grad_b[0], grad_rot[0],
        grad_w_outgate.T, grad_gn[0], grad_w_out, grad_rms[0], grad_w_gate, grad_w_up, grad_w_down,
    )


def solution(mesh):
    both = P(("batch", "chan"), None)
    cols, rows, vec = P(None, "chan"), P("chan", None), P("chan")
    return jax.shard_map(
        local,
        mesh=mesh,
        in_specs=(
            both, cols, cols, vec, vec, cols, vec, rows, P(), cols, cols, rows, both,
            P("batch"), P("batch", None),
        ),
        out_specs=(
            both, both, cols, cols, vec, vec, cols, vec, rows, vec, cols, cols, rows,
        ),
        check_vma=False,
    )
```

```python
import functools

import jax
import jax.numpy as jnp
from jax import lax
from jax.experimental import pallas as pl
from jax.experimental.pallas import tpu as pltpu
from jax.sharding import PartitionSpec as P

MESH = pl.DeviceIdType.MESH
BF = jnp.bfloat16
F32 = jnp.float32
HEAD_CH = 32
SEGS = 16
TM = SEGS * SEGS
ORDER = (0, 1, 3, 2)
PAD0, MA0, WO0, WG0, WD0, PIECE = 288, 320, 512, 704, 1472, 1856
SECTION = (0, 96, 192, 320, 416)


def dot(left, right, left_dim, right_dim):
    return lax.dot_general(
        left, right, (((left_dim,), (right_dim,)), ((), ())), preferred_element_type=F32
    )


def rows_of(tile, size):
    return pl.ds(pl.multiple_of(tile * size, size), size)


def sigmoid(v):
    return 0.5 * jnp.tanh(0.5 * v) + 0.5


def tiles(count, body, steps=None):
    @pl.loop(0, count)
    def _(i):
        for at, calls in (steps or {}).items():

            @pl.when(i == at)
            def _(calls=calls):
                for call in calls:
                    call()

        body(i)


def get(ref, rows, first, count):
    return jnp.concatenate([ref[first + k, rows, :] for k in range(count)], axis=1)


def put(ref, rows, first, v):
    for k in range(v.shape[1] // 128):
        ref[first + k, rows, :] = v[:, 128 * k : 128 * (k + 1)]


def fold_rows(v):
    return jnp.sum(v.reshape(v.shape[0] // 8, 8, v.shape[1]), axis=0)


def main_kernel(
    n_batch, n_chan,
    win_hbm, wf_hbm, wg_hbm, wout_hbm, wgate_hbm, wup_hbm, wdown_hbm, tok_hbm, cot_hbm,
    bias_ref, rot_ref, gn_ref, rms_ref, bucket_ref, len_ref,
    g_hbm, gtok_hbm, out_hbm,
    w, tok, sd, pv, om, pg, ws, xh, rstd, res, fin, mix, out, dff, hid, dgu, dm, dp,
    ones, swap, parx, carx, carb, seg, sgrad, seg_prod,
    rb0, rb1, rb2, mb0, mb1, mb2, zbf, zbq, zbm, mixf, extra,
    par_own,
    load_sem, store_sem, par_send, par_recv, car_send, car_recv, cab_send, cab_recv,
    ag_send, ag_recv, rs_send, rs_recv, fin_send, fin_recv, ex_send, ex_recv,
):
    n_rows, width = tok.shape
    half = width // 2
    lt = half // 128
    n_tiles = n_rows // TM
    seg_len = n_rows // SEGS
    b = lax.axis_index("batch")
    c = lax.axis_index("chan")
    peers = [lax.rem(c + j, n_chan) for j in range(1, n_chan)]
    core = lax.rem(b, 2)
    quarter = lax.rem(b // 2, 4)
    x_bit, y_bit = lax.rem(quarter, 2), quarter // 2

    def flip(bit):
        here = b
        for k in range(n_batch.bit_length()):
            if bit >> k & 1:
                here = here + (1 << k) - (2 << k) * lax.rem(b // (1 << k), 2)
        return here

    core_dev, x_dev, y_dev, diag_dev = ((flip(bit), c) for bit in (1, 2, 4, 6))
    extra_devs = [(flip(1 << k), c) for k in range(3, n_batch.bit_length() - 1)]
    mine = pl.ds(pl.multiple_of(core * half, 128), half)
    theirs = pl.ds(pl.multiple_of((1 - core) * half, 128), half)

    def span(start, size):
        return pl.ds(pl.multiple_of(start, 16), size)

    def remote(src, dst, send_sem, recv_sem, device):
        return pltpu.make_async_remote_copy(
            src, dst, send_sem, recv_sem, device_id=device, device_id_type=MESH
        )

    nch = bias_ref.shape[1]
    heads = nch // HEAD_CH

    def load(src, dst, k):
        copy = pltpu.make_async_copy(src, dst, load_sem.at[k])
        copy.start()
        return copy

    def load_heads(src, first, at):
        return [
            load(
                src.at[HEAD_CH * (2 * hh + part) : HEAD_CH * (2 * hh + part + 1), :],
                w.at[c, pl.ds(first + nch * part + HEAD_CH * hh, HEAD_CH), :],
                at + 2 * hh + part,
            )
            for hh in range(heads)
            for part in range(2)
        ]

    load_first = load_heads(win_hbm, 0, 5 + n_chan) + [load(wf_hbm, w.at[c, pl.ds(2 * nch, nch), :], 0)]
    load_second = (
        load_heads(wg_hbm, MA0, 5 + n_chan + 2 * heads)
        + load_heads(wout_hbm, WO0, 5 + n_chan + 4 * heads)
    )
    load_gate = load(wgate_hbm, hid.at[:width, :], 1)
    load_up = load(wup_hbm, dgu.at[:width, : hid.shape[1]], 2)
    load_down = load(wdown_hbm, w.at[c, WD0:PIECE, :], 3)
    load_tok = load(tok_hbm, fin, 4)
    per = n_rows // n_chan
    load_cot = [
        load(cot_hbm.at[per * k : per * (k + 1), :], dm.at[k, :per, :], 5 + k) for k in range(n_chan)
    ]

    barrier = pltpu.get_barrier_semaphore()
    talk = [core_dev, x_dev, y_dev, diag_dev] + extra_devs + [(b, peer) for peer in peers]
    for device in talk:
        pl.semaphore_signal(barrier, inc=1, device_id=device, device_id_type=MESH)

    w[c, PAD0:MA0, :] = jnp.zeros((MA0 - PAD0, width), BF)
    par_own[...] = jnp.zeros_like(par_own)
    par_own[0:1, :nch] = bias_ref[...]
    par_own[1:2, :nch] = jnp.cos(rot_ref[...])
    par_own[2:3, :nch] = jnp.sin(rot_ref[...])
    for hh in range(heads):
        for part in range(2):
            at = HEAD_CH * (2 * hh + part)
            par_own[3 + part : 4 + part, HEAD_CH * hh : HEAD_CH * (hh + 1)] = gn_ref[
                :, at : at + HEAD_CH
            ]
    parx[c] = pltpu.roll(par_own[...], c * nch, 1)
    pl.semaphore_wait(barrier, len(talk))

    def exchange(ref, send_sem, recv_sem):
        copies = [
            remote(ref.at[c], ref.at[c], send_sem.at[j], recv_sem.at[j], (b, peer))
            for j, peer in enumerate(peers)
        ]
        return copies

    def chain(ref, send_sem, recv_sem, up):
        def each(out, call):
            for k in range(n_chan):
                above = c < k if out == up else c > k
                copy = remote(
                    ref.at[c] if out else ref.at[k], ref.at[c] if out else ref.at[k],
                    send_sem.at[k], recv_sem.at[c] if out else recv_sem.at[k], (b, k),
                )
                pl.when(above)(functools.partial(call, copy))

        def send():
            each(True, lambda copy: copy.start())

        def receive():
            each(False, lambda copy: copy.wait_recv())
            each(True, lambda copy: copy.wait_send())

        return send, receive

    class Gather:
        def __init__(self, unit, j, first, count, turns):
            self.first, self.count, self.turns = first, count, turns
            src = lax.rem(c + j, n_chan)
            peer = lax.rem(c + n_chan - j, n_chan)
            send, recv = ag_send.at[unit], ag_recv.at[unit]

            def copy(k, chan, rows, device):
                ref = w.at[chan, rows, mine]
                return remote(ref, ref, send.at[k], recv.at[k], device)

            from_x = y_bit * 2 + 1 - x_bit
            from_y = (1 - y_bit) * 2 + x_bit
            own = self.rows(quarter)
            self.z = copy(0, c, own, (b, peer))
            self.p1 = [copy(1, src, own, x_dev), copy(2, src, own, y_dev)]
            self.c1 = copy(3, src, own, core_dev)
            if turns:
                cut = count // 4 // 32 * 16
                cut = cut if unit // (n_chan - 1) % 2 else count // 4 - cut
                rest = count // 4 - cut
                self.p2 = [
                    copy(4, src, self.rows(from_x, 0, cut), y_dev),
                    copy(5, src, self.rows(from_y, cut, rest), x_dev),
                ]
            else:
                self.p2 = [copy(4, src, own, diag_dev)]
            self.c2 = [copy(6, src, self.rows(from_x), core_dev),
                       copy(7, src, self.rows(from_y), core_dev)]
            self.c3 = copy(8, src, self.rows(3 - quarter), core_dev)

        def rows(self, part, start=0, size=None):
            size = self.count // 4 if size is None else size
            return span(self.first + part * (self.count // 4) + start, size)

        def along(self):
            self.z.start()

        def plane(self):
            self.z.wait_recv()
            for copy in self.p1 + [self.c1] + ([] if self.turns else self.p2):
                copy.start()

        def turn(self):
            for copy in self.p1:
                copy.wait_recv()
            for copy in (self.p2 if self.turns else []) + self.c2:
                copy.start()

        def cross(self):
            for copy in self.p2:
                copy.wait_recv()
            self.c3.start()

        def ready(self):
            for copy in [self.c1] + self.c2 + [self.c3]:
                copy.wait_recv()

        def along_free(self):
            self.z.wait_send()

        def free(self):
            for copy in self.p1 + self.p2 + [self.c1] + self.c2 + [self.c3]:
                copy.wait_send()

    ring = range(1, n_chan)
    gather_v = [Gather(j - 1, j, 0, 2 * nch, True) for j in ring]
    gather_k = [Gather(11 + j, j, 2 * nch, MA0 - 2 * nch, True) for j in ring]
    gather_b = [Gather(2 + j, j, MA0, WO0 - MA0, True) for j in ring]
    gather_o = [Gather(5 + j, j, WO0, WG0 - WO0, True) for j in ring]
    gather_f = [Gather(8 + j, j, WG0, PIECE - WG0, True) for j in ORDER[1:]]

    place_f = [[buf.at[k] for buf in (rb0, rb1, rb2)] for k in range(2)]
    place_m = [[buf.at[k] for buf in (mb0, mb1, mb2)] for k in (0, 1, 2, 0)]

    class Reduce:
        def __init__(self, chunk, place, ref, dist, first, count, slots, late=False):
            chan = None if dist is None else lax.rem(c + dist, n_chan)
            self.ref, self.slots = ref, slots
            send, recv = rs_send.at[chunk], rs_recv.at[chunk]
            q = count // 4
            cut = q // 32 * 16 if chunk % 2 else q - q // 32 * 16
            rest = q - cut
            chans = pl.ds(0, n_chan) if chan is None else pl.ds(chan, 1)
            n = n_chan if chan is None else 1
            far_x = y_bit * 2 + 1 - x_bit
            far_y = (1 - y_bit) * 2 + x_bit

            def item(k, level, at, part, keep, start, size, cols, device):
                buf = place[level].at[:n, at : at + size, :]
                src = ref.at[chans, span(first + part * q + start, size), cols]
                to = chans, span(first + keep * q + start, size)
                return to, buf, size, remote(src, buf, send.at[k], recv.at[k], device)

            whole = place[0].at[:n, :count, :]
            src = ref.at[chans, first : first + count, theirs]
            self.s0 = [(
                (chans, pl.ds(first, count)), whole, count,
                remote(src, whole, send.at[0], recv.at[0], core_dev),
            )]
            self.s1 = []
            for k in range(2):
                self.s1.append(item(
                    1 + k, 1, k * cut, k * 2 + 1 - x_bit, k * 2 + x_bit, 0, cut, mine, x_dev))
                self.s1.append(item(
                    3 + k, 1, 2 * cut + k * rest, (1 - y_bit) * 2 + k, y_bit * 2 + k, cut, rest,
                    mine, y_dev))
            self.s2 = []
            if not (late and dist):
                self.s2 = [
                    item(5, 2, 0, far_y, quarter, 0, cut, mine, y_dev),
                    item(6, 2, cut, far_x, quarter, cut, rest, mine, x_dev),
                ]
            own = span(first + quarter * q, q)
            self.pairs = [(first + (k * 2 + x_bit) * q, cut, k * cut) for k in range(2)]
            self.pairs += [
                (first + (y_bit * 2 + k) * q + cut, rest, 2 * cut + k * rest) for k in range(2)
            ]
            if late and dist:
                self.s3 = [
                    remote(
                        ref.at[chan, span(start, size), mine],
                        slots.at[dist // 2, at : at + size, :],
                        send.at[7 + k], recv.at[7 + k], (b, chan),
                    )
                    for k, (start, size, at) in enumerate(self.pairs)
                ]
            elif dist:
                self.s3 = [remote(
                    ref.at[chan, own, mine], slots, send.at[7], recv.at[7], (b, chan)
                )]
            else:
                self.s3 = [
                    remote(
                        ref.at[lax.rem(c + j, n_chan), own, mine], slots.at[j - 1],
                        send.at[6 + j], recv.at[6 + j], (b, lax.rem(c + j, n_chan)),
                    )
                    for j in range(1, n_chan)
                    if dist is None
                ]
            self.sent = [it[-1] for it in self.s0 + self.s1 + self.s2] + self.s3

        def add(self, items):
            for (chans, rows), buf, size, copy in items:
                copy.wait_recv()
                step = 96 if buf.shape[0] == 1 else 16
                for at in range(0, size, step):
                    n = min(step, size - at)
                    here = self.ref.at[chans, span(rows.start + at, n), mine]
                    here[...] = here[...] + buf[:, at : at + n, :]

        def to_core(self):
            for item in self.s0:
                item[-1].start()

        def to_plane(self):
            self.add(self.s0)
            for item in self.s1:
                item[-1].start()

        def pair(self):
            self.add(self.s1)

        def send_along(self):
            for copy in self.s3:
                copy.start()

        def pair_along(self):
            self.pair()
            self.send_along()

        def collect(self, copies):
            for copy in copies:
                copy.wait_recv()
            for start, size, at in self.pairs:
                for k in range(0, size, 48):
                    here = span(start + k, 48)
                    v = self.ref[c, here, mine].astype(F32)
                    for j in range(self.slots.shape[0]):
                        v = v + self.slots[j, at + k : at + k + 48, :].astype(F32)
                    self.ref[c, here, mine] = v.astype(BF)
            for item in self.s2:
                item[-1].start()

        def turn(self):
            self.add(self.s1)
            for item in self.s2:
                item[-1].start()

        def along(self):
            self.add(self.s2)
            for copy in self.s3:
                copy.start()

        def free(self):
            for copy in self.sent:
                copy.wait_send()

    class Spread:
        def __init__(self, chunk, ref, first, count, slots, recvs, dest, dest_first, ex_at, turns=False):
            self.ref, self.first, self.q = ref, first, count // 4
            self.slots, self.recvs, self.dest = slots, recvs, dest
            send, recv = fin_send.at[chunk], fin_recv.at[chunk]
            self.at = span(dest_first + quarter * self.q, self.q)
            ref = dest.at[self.at, mine]
            self.copies = [
                remote(ref, ref, send.at[k], recv.at[k], device)
                for k, device in enumerate((x_dev, y_dev) if turns else (x_dev, y_dev, diag_dev))
            ]
            self.p2 = []
            if turns:
                cut = self.q // 32 * 16
                parts = (
                    (y_bit * 2 + 1 - x_bit, 0, cut, y_dev),
                    ((1 - y_bit) * 2 + x_bit, cut, self.q - cut, x_dev),
                )
                for k, (part, start, size, device) in enumerate(parts):
                    half_ref = dest.at[span(dest_first + part * self.q + start, size), mine]
                    self.p2.append(remote(
                        half_ref, half_ref, send.at[4 + k], recv.at[4 + k], device
                    ))
            ref_all = dest.at[dest_first : dest_first + count, mine]
            self.last = remote(ref_all, ref_all, send.at[3], recv.at[3], core_dev)
            self.extra = []
            for k, device in enumerate(extra_devs):
                buf = extra.at[k, ex_at : ex_at + self.q, :]
                self.extra.append((buf, remote(
                    ref, buf, ex_send.at[chunk, k], ex_recv.at[chunk, k], device
                )))

        def total(self):
            for copy in self.recvs:
                copy.wait_recv()
            v = self.ref[c, span(self.first + quarter * self.q, self.q), mine].astype(F32)
            for j in range(len(self.recvs)):
                v = v + self.slots[j][...].astype(F32)
            self.dest[self.at, mine] = v.astype(BF)
            for buf, copy in self.extra:
                copy.start()
                copy.wait()
                v = self.dest[self.at, mine].astype(F32) + buf[...].astype(F32)
                self.dest[self.at, mine] = v.astype(BF)
            for copy in self.copies:
                copy.start()

        def turn(self):
            for copy in self.copies:
                copy.wait_recv()
            for copy in self.p2:
                copy.start()

        def cross(self):
            for copy in self.p2 or self.copies:
                copy.wait_recv()
            self.last.start()

        def done(self):
            self.last.wait_recv()
            for copy in self.copies + self.p2 + [self.last]:
                copy.wait_send()

    f_rows = PIECE - WG0
    reduce_f = [
        Reduce(k, place_f[k % 2], w, j, WG0, f_rows, zbf if j != 2 else zbq, j != 2)
        for k, j in enumerate(ORDER)
    ]
    reduce_o = Reduce(n_chan, place_m[0], sd, None, 0, WG0 - WO0, zbm.at[0])
    reduce_g = Reduce(n_chan + 1, place_m[1], w, None, WO0, WO0 - MA0, zbm.at[1])
    reduce_v = Reduce(n_chan + 2, place_m[2], dm, None, 0, 2 * nch, zbm.at[2])
    reduce_k = Reduce(
        n_chan + 3, place_m[3], dm, None, 2 * nch, MA0 - 2 * nch,
        zbm.at[3, :, : (MA0 - 2 * nch) // 4],
    )
    spread_f = Spread(0, w, WG0, f_rows, [zbq], reduce_f[-1].s3, dgu, 0, 0, True)
    at = [f_rows // 4 + k * (nch // 2) for k in range(4)]
    spread_o = Spread(1, sd, 0, WG0 - WO0, zbm.at[0], reduce_o.s3, mixf, WO0, at[0])
    spread_g = Spread(2, w, WO0, WO0 - MA0, zbm.at[1], reduce_g.s3, mixf, MA0, at[1])
    spread_v = Spread(3, dm, 0, 2 * nch, zbm.at[2], reduce_v.s3, mixf, 0, at[2])
    spread_k = Spread(
        4, dm, 2 * nch, MA0 - 2 * nch, zbm.at[3, :, : (MA0 - 2 * nch) // 4], reduce_k.s3, mixf,
        2 * nch, at[3],
    )

    for copy in load_first:
        copy.wait()
    par_copies = exchange(parx, par_send, par_recv)
    for copy in par_copies:
        copy.start()
    for g in gather_v + gather_k:
        g.along()
    for copy in load_second:
        copy.wait()
    hw = hid.shape[1]
    load_gate.wait()
    w[c, WG0 : WG0 + hw, :] = hid[:width, :].T
    load_up.wait()
    w[c, WG0 + hw : WD0, :] = dgu[:width, :hw].T
    load_down.wait()
    lane_r = lax.broadcasted_iota(jnp.int32, (half, half), 0) // HEAD_CH
    lane_c = lax.broadcasted_iota(jnp.int32, (half, half), 1) // HEAD_CH
    ones[...] = jnp.where(lane_r == lane_c, 1.0 / (2 * HEAD_CH), 0.0).astype(BF)
    sgrad[...] = jnp.zeros_like(sgrad)
    row = lax.broadcasted_iota(jnp.int32, (TM, TM), 0)
    col = lax.broadcasted_iota(jnp.int32, (TM, TM), 1)
    swap[...] = jnp.where(row == lax.rem(col, SEGS) * SEGS + col // SEGS, 1.0, 0.0).astype(BF)

    def blocks(i):
        return [span(seg_len * k + SEGS * i, SEGS) for k in range(SEGS)]

    def head_mean(v, exact=False):
        high = v.astype(BF)
        if not exact:
            return dot(high, ones[...], 1, 0)
        low = (v - high.astype(F32)).astype(BF)
        return dot(high, ones[...], 1, 0) + dot(low, ones[...], 1, 0)

    bucket = bucket_ref[0]
    base = c * n_rows
    offset = jnp.bitwise_and(base, bucket - 1)
    slot_limit = len_ref[0, 0]
    for k in range(1, len_ref.shape[1]):
        slot_limit = jnp.where(base >= k * bucket, len_ref[0, k], slot_limit)
    live_rows = slot_limit - offset
    not_start = jnp.where(offset == 0, 0.0, 1.0).astype(F32)

    def section(k):
        return jnp.concatenate(
            [w[cc, SECTION[k] : SECTION[k] + 96, :] for cc in range(n_chan)], axis=0
        )

    def out_rows(k):
        return jnp.concatenate(
            [w[cc, WO0 + 96 * k : WO0 + 96 * k + 96, :] for cc in range(n_chan)], axis=0
        )

    def order_tokens(i):
        part = jnp.concatenate([fin[at, :] for at in blocks(i)], axis=0)
        tok[rows_of(i, TM), :] = dot(swap[...], part, 1, 0).astype(BF)

    def order_seed(i):
        part = jnp.concatenate(
            [
                dm[k, span(seg_len * m + SEGS * i, SEGS), :]
                for k in range(n_chan)
                for m in range(SEGS // n_chan)
            ],
            axis=0,
        ).astype(F32)
        k = lax.broadcasted_iota(jnp.int32, (TM, 1), 0)
        place = k // SEGS * seg_len + lax.rem(k, SEGS) + SEGS * i
        part = (part * jnp.where(place < live_rows, 1.0, 0.0)).astype(BF)
        sd[i] = dot(swap[...], part, 1, 0).astype(BF)

    load_tok.wait()
    tiles(n_tiles, order_tokens)
    for g in gather_v:
        g.plane()
    for copy in load_cot:
        copy.wait()
    tiles(n_tiles, order_seed)
    for g in gather_k:
        g.plane()
    for g in gather_b + gather_o + gather_f[:2]:
        g.along()
    for g in gather_v:
        g.turn()
    for g in gather_k:
        g.turn()
    for g in gather_v:
        g.cross()
    for g in gather_k:
        g.cross()
    for g in gather_v:
        g.ready()

    for copy in par_copies:
        copy.wait()
    par = parx[0] + parx[1] + parx[2] + parx[3]
    bias = par[0:1, :]
    cos1, sin1 = par[1:2, :], par[2:3, :]
    gain_r, gain_i = par[3:4, :], par[4:5, :]
    rms_gain = jnp.concatenate([rms_ref[k : k + 1, :] for k in range(width // 128)], axis=1)
    cos16 = jnp.broadcast_to(cos1, (SEGS, half))
    sin16 = jnp.broadcast_to(sin1, (SEGS, half))

    def power(count):
        rr, ri = cos1, sin1
        while count > 1:
            rr, ri = rr * rr - ri * ri, 2.0 * rr * ri
            count //= 2
        return rr, ri

    seg_cos, seg_sin = power(seg_len)
    all_cos, all_sin = power(n_rows)

    def project(i):
        rows = rows_of(i, TM)
        x = tok[rows, :]
        for k in range(2):
            pre = dot(x, section(k), 1, 1)
            pv[rows, k * half : (k + 1) * half] = pre
            put(out, rows, k * lt, pre * sigmoid(pre))

    def project_forget(i):
        rows = rows_of(i, TM)
        pre = dot(tok[rows, :], section(2), 1, 1) + bias
        put(om, rows, 0, 1.0 / (1.0 + jnp.exp(pre)))

    tiles(n_tiles, project, {1: [g.plane for g in gather_b]})
    for g in gather_k:
        g.ready()
    tiles(n_tiles, project_forget, {1: [g.plane for g in gather_o]})

    def strided(t):
        return span(t * SEGS, SEGS)

    def first(t, carry):
        sr, si, prod = carry
        o = get(om, strided(t), 0, lt)
        f = 1.0 - o
        vr = get(out, strided(t), 0, lt)
        vi = get(out, strided(t), lt, lt)
        tr = cos16 * sr - sin16 * si
        ti = sin16 * sr + cos16 * si
        return f * tr + o * vr, f * ti + o * vi, prod * f

    zero = jnp.zeros((SEGS, half), F32)
    end_r, end_i, prod = lax.fori_loop(
        0, seg_len, first, (zero, zero, jnp.ones((SEGS, half), F32)), unroll=4
    )
    seg[0] = end_r
    seg[1] = end_i
    seg_prod[...] = prod

    def fold_forward(cr, ci, keep):
        total = jnp.ones((1, half), F32)
        for s in range(SEGS):
            if keep:
                seg[2, s : s + 1, :] = cr
                seg[3, s : s + 1, :] = ci
            p = seg_prod[s : s + 1, :]
            ar, ai = p * seg_cos, p * seg_sin
            cr, ci = (
                ar * cr - ai * ci + seg[0, s : s + 1, :],
                ar * ci + ai * cr + seg[1, s : s + 1, :],
            )
            total = total * p
        return cr, ci, total

    zrow = jnp.zeros((1, half), F32)
    er, ei, total = fold_forward(zrow, zrow, False)
    carx[c, 0:1, :] = er
    carx[c, 1:2, :] = ei
    carx[c, 2:3, :] = total * all_cos * not_start
    carx[c, 3:4, :] = total * all_sin * not_start
    to_later, from_earlier = chain(carx, car_send, car_recv, True)
    to_later()
    for g in gather_b:
        g.turn()
    for g in gather_o:
        g.turn()
    gather_f[0].plane()
    for g in gather_b:
        g.cross()
    from_earlier()
    gather_f[2].along()
    cr, ci = zrow, zrow
    for k in range(n_chan - 1):
        ar, ai = carx[k, 2:3, :], carx[k, 3:4, :]
        nr = ar * cr - ai * ci + carx[k, 0:1, :]
        ni = ar * ci + ai * cr + carx[k, 1:2, :]
        cr = jnp.where(k < c, nr, cr)
        ci = jnp.where(k < c, ni, ci)
    fold_forward(cr * not_start, ci * not_start, True)

    def second(t, carry):
        sr, si = carry
        o = get(om, strided(t), 0, lt)
        f = 1.0 - o
        vr = get(out, strided(t), 0, lt)
        vi = get(out, strided(t), lt, lt)
        tr = cos16 * sr - sin16 * si
        ti = sin16 * sr + cos16 * si
        put(ws, strided(t), 0, tr)
        put(ws, strided(t), lt, ti)
        return f * tr + o * vr, f * ti + o * vi

    lax.fori_loop(0, seg_len, second, (seg[2], seg[3]), unroll=4)
    for g in gather_b:
        g.ready()

    def project_gate(i):
        rows = rows_of(i, TM)
        x = tok[rows, :]
        for k in range(2):
            pg[rows, k * half : (k + 1) * half] = dot(x, section(3 + k), 1, 1)

    tiles(n_tiles, project_gate, {2: [g.cross for g in gather_o]})
    for g in gather_o:
        g.ready()

    def mixer_out(i):
        rows = rows_of(i, TM)
        o = get(om, rows, 0, lt)
        f = 1.0 - o
        gr, gi = pg[rows, :half], pg[rows, half:]
        yr = gr * sigmoid(gr) * (f * get(ws, rows, 0, lt) + o * get(out, rows, 0, lt))
        yi = gi * sigmoid(gi) * (f * get(ws, rows, lt, lt) + o * get(out, rows, lt, lt))
        mean = head_mean(yr + yi, True)
        yr, yi = yr - mean, yi - mean
        inv = lax.rsqrt(head_mean(yr * yr + yi * yi) + 1e-5)
        yr, yi = yr * inv, yi * inv
        rstd[rows, :] = inv
        xh[rows, :half] = yr.astype(BF)
        xh[rows, half:] = yi.astype(BF)
        lr, li = (yr * gain_r).astype(BF), (yi * gain_i).astype(BF)
        mix[rows, :half] = lr
        mix[rows, half:] = li
        r = tok[rows, :].astype(F32) + (
            dot(lr, out_rows(0), 1, 0) + dot(li, out_rows(1), 1, 0)
        )
        res[rows, :] = r
        put(out, rows, 0, r)
        rinv = lax.rsqrt(jnp.mean(r * r, axis=1, keepdims=True) + 1e-6)
        fin[rows, :] = (r * rinv * rms_gain).astype(BF)
        dff[rows, :] = jnp.zeros((TM, width), F32)

    tiles(n_tiles, mixer_out, {
        1: [gather_f[0].turn],
        2: [gather_f[1].plane],
    })

    for j in range(n_chan):
        cc = lax.rem(c + ORDER[j], n_chan)

        def feed(i, cc=cc):
            rows = rows_of(i, 2 * TM)
            gate_up = dot(fin[rows, :], w[cc, WG0:WD0, :], 1, 1)
            d_hid = dot(jnp.concatenate([sd[2 * i], sd[2 * i + 1]], axis=0), w[cc, WD0:PIECE, :], 1, 1)
            gate, up = gate_up[:, :hw], gate_up[:, hw:]
            sig = sigmoid(gate)
            act = gate * sig
            h = (act * up).astype(BF)
            hid[rows, :] = h
            dg = (d_hid * up * (sig + act * (1.0 - sig))).astype(BF)
            du = (d_hid * act).astype(BF)
            dgu[rows, :hw] = dg
            dgu[rows, hw:] = du
            put(out, rows, 0, get(out, rows, 0, 2 * lt) + dot(h, w[cc, WD0:PIECE, :], 1, 0))
            dff[rows, :] += dot(dgu[rows, :], w[cc, WG0:WD0, :], 1, 0)

        if j == 0:
            tiles(n_tiles // 2, feed, {1: [gather_f[0].cross]})
            gather_f[1].turn()
            for g in gather_f:
                g.along_free()
            gather_f[0].ready()
        else:
            before = reduce_f[j - 1]
            older = [reduce_f[j - 2]] if j > 1 else []
            if j > 1:
                gather_f[j - 1].ready()
            tiles(n_tiles // 2, feed, {
                1: ([gather_f[1].cross] if j == 1 else [])
                + [r.pair_along for r in older] + [before.to_plane],
            })
            if j == 2:
                gather_f[2].cross()
            gather_f[j - 1].free()
        for k in range(2):
            w[cc, WG0 + hw * k : WG0 + hw * (k + 1), :] = dot(
                dgu[:n_rows, hw * k : hw * (k + 1)], fin[...], 0, 0
            ).astype(BF)
        seeds = jnp.concatenate([sd[k] for k in range(n_tiles)], axis=0)
        if j == 1:
            gather_f[2].turn()
        w[cc, WD0:PIECE, :] = dot(hid[...], seeds, 0, 0).astype(BF)
        reduce_f[j].to_core()
        if j == 0:
            gather_f[2].plane()

    def norm_back(i):
        rows = rows_of(i, TM)
        fin[rows, :] = get(out, rows, 0, 2 * lt).astype(BF)
        r = res[rows, :]
        rinv = lax.rsqrt(jnp.mean(r * r, axis=1, keepdims=True) + 1e-6)
        rhat = r * rinv
        d = dff[rows, :]
        sgrad[2] += fold_rows(d * rhat)
        t = d * rms_gain
        dres = sd[i].astype(F32) + rinv * (
            t - rhat * jnp.mean(t * rhat, axis=1, keepdims=True)
        )
        dff[rows, :] = dres
        dm[i, :TM, :] = dres.astype(BF)

    tiles(n_tiles, norm_back)
    reduce_f[-2].pair()
    d_mixed = jnp.concatenate([dm[k, :TM, :] for k in range(n_tiles)], axis=0)
    for k in range(2):
        grad = dot(mix[:, k * half : (k + 1) * half], d_mixed, 0, 0).astype(BF)
        for cc in range(n_chan):
            sd[cc, 96 * k : 96 * k + 96, :] = grad[96 * cc : 96 * cc + 96, :]
    reduce_o.to_core()
    reduce_f[-1].to_plane()

    def mixer_back(i):
        rows = rows_of(i, TM)
        low = dm[i, :TM, :]
        dr = dot(low, out_rows(0), 1, 1)
        di = dot(low, out_rows(1), 1, 1)
        xr, xi = xh[rows, :half].astype(F32), xh[rows, half:].astype(F32)
        sgrad[1, :, :half] += fold_rows(dr * xr)
        sgrad[1, :, half:] += fold_rows(di * xi)
        dr, di = dr * gain_r, di * gain_i
        m1 = head_mean(dr + di)
        m2 = head_mean(dr * xr + di * xi)
        inv = rstd[rows, :]
        dr = inv * (dr - m1 - xr * m2)
        di = inv * (di - m1 - xi * m2)
        o = get(om, rows, 0, lt)
        f = 1.0 - o
        for k, dy in ((0, dr), (1, di)):
            cols = slice(k * half, (k + 1) * half)
            pre = pv[rows, cols]
            state = f * get(ws, rows, k * lt, lt) + o * (pre * sigmoid(pre))
            g = pg[rows, cols]
            sig = sigmoid(g)
            act = g * sig
            dp[rows, (3 + k) * half : (4 + k) * half] = (
                dy * state * (sig + act * (1.0 - sig))
            ).astype(BF)
            put(out, rows, k * lt, dy * act)
    tiles(n_tiles, mixer_back, {2: [reduce_o.to_plane]})

    def collect_f():
        reduce_f[0].collect([copy for r in reduce_f[1:-1] for copy in r.s3])

    def own_f():
        reduce_f[0].add(reduce_f[0].s2)

    def first_back(k, carry):
        qr, qi = carry
        t = seg_len - 1 - k
        f = 1.0 - get(om, strided(t), 0, lt)
        lr = get(out, strided(t), 0, lt) + qr
        li = get(out, strided(t), lt, lt) + qi
        return f * (cos16 * lr + sin16 * li), f * (cos16 * li - sin16 * lr)

    qr, qi = lax.fori_loop(0, seg_len, first_back, (zero, zero), unroll=4)
    seg[0] = qr
    seg[1] = qi

    def fold_back(cr, ci, keep):
        for s in range(SEGS - 1, -1, -1):
            if keep:
                seg[2, s : s + 1, :] = cr
                seg[3, s : s + 1, :] = ci
            p = seg_prod[s : s + 1, :]
            ar, ai = p * seg_cos, -(p * seg_sin)
            cr, ci = (
                ar * cr - ai * ci + seg[0, s : s + 1, :],
                ar * ci + ai * cr + seg[1, s : s + 1, :],
            )
        return cr, ci

    er, ei = fold_back(zrow, zrow, False)
    carb[c, 0:1, :] = er * not_start
    carb[c, 1:2, :] = ei * not_start
    carb[c, 2:4, :] = carx[c, 2:4, :]
    to_earlier, from_later = chain(carb, cab_send, cab_recv, False)
    to_earlier()
    reduce_f[-2].send_along()

    for g in gather_v + gather_k + gather_b + gather_o:
        g.along_free()
        g.free()
    for k in range(2):
        grad = dot(dp[:, (3 + k) * half : (4 + k) * half], tok[...], 0, 0).astype(BF)
        for cc in range(n_chan):
            at = WO0 + 96 * k
            w[cc, at : at + 96, :] = grad[96 * cc : 96 * cc + 96, :]
    reduce_g.to_core()
    reduce_f[-1].turn()

    from_later()
    cr, ci = zrow, zrow
    for k in range(n_chan - 1, 0, -1):
        ar, ai = carb[k, 2:3, :], -carb[k, 3:4, :]
        nr = ar * cr - ai * ci + carb[k, 0:1, :]
        ni = ar * ci + ai * cr + carb[k, 1:2, :]
        cr = jnp.where(k > c, nr, cr)
        ci = jnp.where(k > c, ni, ci)
    fold_back(cr, ci, True)

    def second_back(k, carry):
        qr, qi = carry
        t = seg_len - 1 - k
        f = 1.0 - get(om, strided(t), 0, lt)
        lr = get(out, strided(t), 0, lt) + qr
        li = get(out, strided(t), lt, lt) + qi
        put(out, strided(t), 0, lr)
        put(out, strided(t), lt, li)
        return f * (cos16 * lr + sin16 * li), f * (cos16 * li - sin16 * lr)

    lax.fori_loop(0, seg_len, second_back, (seg[2], seg[3]), unroll=4)
    def project_back(i):
        rows = rows_of(i, TM)
        o = get(om, rows, 0, lt)
        f = 1.0 - o
        df = jnp.zeros((TM, half), F32)
        for k in range(2):
            cols = slice(k * half, (k + 1) * half)
            pre = pv[rows, cols]
            sig = sigmoid(pre)
            act = pre * sig
            lam = get(out, rows, k * lt, lt)
            df += lam * (get(ws, rows, k * lt, lt) - act)
            dp[rows, cols] = (o * lam * (sig + act * (1.0 - sig))).astype(BF)
        dx = df * f * o
        dp[rows, 2 * half : 3 * half] = dx.astype(BF)
        sgrad[0, :, :half] += fold_rows(dx)
        sgrad[0, :, half:] += fold_rows(
            f
            * (
                get(out, rows, lt, lt) * get(ws, rows, 0, lt)
                - get(out, rows, 0, lt) * get(ws, rows, lt, lt)
            )
        )

    tiles(n_tiles, project_back, {3: [reduce_f[-1].along]})
    reduce_o.turn()
    for k in range(3):
        grad = dot(dp[:, k * half : (k + 1) * half], tok[...], 0, 0).astype(BF)
        for cc in range(n_chan):
            dm[cc, 96 * k : 96 * k + 96, :] = grad[96 * cc : 96 * cc + 96, :]
        if k == 1:
            reduce_v.to_core()
            reduce_g.to_plane()
    small = jnp.concatenate(
        [jnp.sum(sgrad[k], axis=0, keepdims=True) for k in range(3)]
        + [jnp.zeros((29, width), F32)],
        axis=0,
    ).astype(BF)
    for cc in range(n_chan):
        dm[cc, PAD0:MA0, :] = small
    reduce_k.to_core()
    def order_out(i):
        done = dot(swap[...], fin[rows_of(i, TM), :], 1, 0).astype(BF)
        for k, at in enumerate(blocks(i)):
            mix[at, :] = done[SEGS * k : SEGS * (k + 1), :]

    def d_tokens(i):
        rows = rows_of(i, TM)
        acc = dff[rows, :]
        for k in range(5):
            acc += dot(dp[rows, k * half : (k + 1) * half], section(k), 1, 0)
        high = acc.astype(BF)
        low = (acc - high.astype(F32)).astype(BF)
        done = dot(swap[...], high, 1, 0) + dot(swap[...], low, 1, 0)
        for k, at in enumerate(blocks(i)):
            res[at, :] = done[SEGS * k : SEGS * (k + 1), :]

    tiles(n_tiles, d_tokens, {
        0: [reduce_o.along],
        1: [reduce_v.to_plane],
        2: [reduce_k.to_plane],
    })
    gtok_copy = pltpu.make_async_copy(res, gtok_hbm, store_sem.at[1])
    gtok_copy.start()
    reduce_v.turn()
    collect_f()
    reduce_k.turn()
    reduce_g.turn()
    own_f()
    spread_f.total()
    tiles(n_tiles, order_out)
    out_copy = pltpu.make_async_copy(mix, out_hbm, store_sem.at[0])
    out_copy.start()
    reduce_v.along()
    spread_o.total()
    reduce_k.along()
    reduce_g.along()
    spread_f.turn()
    spread_v.total()
    spread_k.total()
    spread_f.cross()
    spread_o.cross()
    spread_g.total()
    for sp in (spread_v, spread_k, spread_g):
        sp.cross()
    g_copies = []

    def leave(sp, src, rows):
        sp.done()
        copy = pltpu.make_async_copy(src, g_hbm.at[rows, :], store_sem.at[2 + len(g_copies)])
        copy.start()
        g_copies.append(copy)

    leave(spread_f, dgu, pl.ds(WG0, PIECE - WG0))
    for sp, lo, hi in (
        (spread_o, WO0, WG0), (spread_v, 0, 2 * nch), (spread_k, 2 * nch, MA0), (spread_g, MA0, WO0)
    ):
        leave(sp, mixf.at[lo:hi, :], pl.ds(lo, hi - lo))
    for r in reduce_f + [reduce_o, reduce_g, reduce_v, reduce_k]:
        r.free()
    for copy in [out_copy, gtok_copy] + g_copies:
        copy.wait()


def post_kernel(
    g_hbm, gtok_hbm, out_hbm,
    win_ref, wf_ref, bf_ref, rot_ref, wg_ref, gn_ref, wout_ref, rms_ref, gate_ref, up_ref,
    down_ref, gtok_ref, out_ref,
    g, t_in, t_f, t_g, t_out, t_gate, t_up, t_down, t_gtok, t_block, rows8, load_sem, store_sem,
):
    nch = bf_ref.shape[1]
    heads = nch // HEAD_CH
    hw = (WD0 - WG0) // 2
    half = g.shape[1] // 2
    c = lax.axis_index("chan")
    cuts = (0, MA0, WG0, WG0 + hw, WD0, PIECE)
    loads = []
    for k in range(5):
        rows = pl.ds(cuts[k], cuts[k + 1] - cuts[k])
        loads.append(pltpu.make_async_copy(g_hbm.at[rows, :], g.at[rows, :], load_sem.at[k]))
        loads[-1].start()
    through = []
    for src, mid, dst in ((gtok_hbm, t_gtok, gtok_ref), (out_hbm, t_block, out_ref)):
        n = mid.shape[0] // 4
        for k in range(4):
            rows = pl.ds(n * k, n)
            sem = load_sem.at[5 + len(through)]
            through.append((
                pltpu.make_async_copy(src.at[rows, :], mid.at[rows, :], sem),
                mid.at[rows, :], dst.at[rows, :],
            ))
            through[-1][0].start()
    stores = []

    def store(src, dst):
        copy = pltpu.make_async_copy(src, dst, store_sem.at[len(stores)])
        copy.start()
        stores.append(copy)

    def pass_on(count):
        for _ in range(count):
            copy, mid, dst = through.pop(0)
            copy.wait()
            store(mid, dst)

    def joined(first):
        return jnp.concatenate(
            [
                g[first + nch * part + HEAD_CH * hh : first + nch * part + HEAD_CH * (hh + 1), :]
                for hh in range(heads)
                for part in range(2)
            ],
            axis=0,
        )

    loads[0].wait()
    t_in[...] = joined(0).astype(F32)
    store(t_in, win_ref)
    t_f[...] = g[2 * nch : 3 * nch, :].astype(F32)
    store(t_f, wf_ref)
    small = g[PAD0 : PAD0 + 16, :].astype(F32)
    turn = lax.rem(4 - c, 4) * nch
    rows8[0:8, :half] = pltpu.roll(small[0:8, :half], turn, 1)
    rows8[0:8, half:] = pltpu.roll(small[0:8, half:], turn, 1)
    bf_ref[...] = rows8[0:1, :nch]
    rot_ref[...] = rows8[0:1, half : half + nch]
    for hh in range(heads):
        for part in range(2):
            at = half * part + HEAD_CH * hh
            to = HEAD_CH * (2 * hh + part)
            gn_ref[:, to : to + HEAD_CH] = rows8[1:2, at : at + HEAD_CH]
    rows8[8:16, :] = pltpu.roll(small[0:8, :], 2 * turn, 1)
    rms_ref[...] = rows8[10:11, : 2 * nch]
    pass_on(1)
    loads[1].wait()
    t_g[...] = joined(MA0).astype(F32)
    store(t_g, wg_ref)
    t_out[...] = joined(WO0).astype(F32)
    store(t_out, wout_ref)
    pass_on(2)
    loads[2].wait()
    t_gate[...] = g[WG0 : WG0 + hw, :].T.astype(F32)
    store(t_gate, gate_ref)
    pass_on(2)
    loads[3].wait()
    t_up[...] = g[WG0 + hw : WD0, :].T.astype(F32)
    store(t_up, up_ref)
    pass_on(2)
    loads[4].wait()
    t_down[...] = g[WD0:PIECE, :].astype(F32)
    store(t_down, down_ref)
    pass_on(1)
    for copy in stores:
        copy.wait()


def post_call(g, grad_tokens, block_out, nch):
    width = g.shape[1]
    hw = (WD0 - WG0) // 2
    any_spec = pl.BlockSpec(memory_space=pl.ANY)
    vmem = pl.BlockSpec(memory_space=pltpu.VMEM)
    big = [(2 * nch, width), (nch, width), (2 * nch, width), (2 * nch, width), (width, hw),
           (width, hw), (hw, width)]
    shapes = [big[0], big[1], (1, nch), (1, nch), big[2], (1, 2 * nch), big[3], (1, 2 * nch),
              big[4], big[5], big[6], grad_tokens.shape]
    return pl.pallas_call(
        post_kernel,
        out_shape=[jax.ShapeDtypeStruct(shape, F32) for shape in shapes]
        + [jax.ShapeDtypeStruct(block_out.shape, BF)],
        in_specs=[any_spec] * 3,
        out_specs=[vmem if shape[0] == 1 else any_spec for shape in shapes] + [any_spec],
        scratch_shapes=[pltpu.VMEM(g.shape, BF)]
        + [pltpu.VMEM(shape, F32) for shape in big + [grad_tokens.shape]]
        + [
            pltpu.VMEM(block_out.shape, BF),
            pltpu.VMEM((16, width), F32),
            pltpu.SemaphoreType.DMA((13,)),
            pltpu.SemaphoreType.DMA((15,)),
        ],
        compiler_params=pltpu.CompilerParams(vmem_limit_bytes=60 * 2**20),
        name="place",
    )(g, grad_tokens, block_out)


def main_call(weights, tokens, cotangent, vectors, bucket, lengths):
    rows, width = tokens.shape
    half = width // 2
    nch = vectors[0].shape[1]
    n_chan, n_batch = lax.axis_size("chan"), lax.axis_size("batch")
    n_extra = max(1, n_batch.bit_length() - 4)
    w_shape = (n_chan, PIECE, width)
    hw = (WD0 - WG0) // 2
    any_spec = pl.BlockSpec(memory_space=pl.ANY)
    vmem = pl.BlockSpec(memory_space=pltpu.VMEM)
    smem = pl.BlockSpec(memory_space=pltpu.SMEM)
    full32 = pltpu.VMEM((rows, width), F32)
    half32 = pltpu.VMEM((rows, half), F32)
    tiles32 = pltpu.VMEM((width // 128, rows, 128), F32)
    full16 = pltpu.VMEM((rows, width), BF)
    return pl.pallas_call(
        functools.partial(main_kernel, n_batch, n_chan),
        out_shape=[
            jax.ShapeDtypeStruct((PIECE, width), BF),
            jax.ShapeDtypeStruct((rows, width), F32),
            jax.ShapeDtypeStruct((rows, width), BF),
        ],
        in_specs=[any_spec] * 9 + [vmem] * 4 + [smem, smem],
        out_specs=[any_spec] * 3,
        scratch_shapes=[
            pltpu.VMEM(w_shape, BF),
            full16, pltpu.VMEM((rows // TM, TM, width), BF), full32,
            pltpu.VMEM((half // 128, rows, 128), F32), full32, tiles32,
            full16, half32, full32, full16, full16, tiles32, full32,
            pltpu.VMEM((rows, hw), BF), pltpu.VMEM((PIECE - WG0, 2 * hw), BF),
            pltpu.VMEM((n_chan, MA0, width), BF), pltpu.VMEM((rows, 5 * half), BF),
            pltpu.VMEM((half, half), BF),
            pltpu.VMEM((TM, TM), BF),
            pltpu.VMEM((n_chan, 8, half), F32),
            pltpu.VMEM((n_chan, 8, half), F32),
            pltpu.VMEM((n_chan, 8, half), F32),
            pltpu.VMEM((4, SEGS, half), F32),
            pltpu.VMEM((3, 8, width), F32),
            pltpu.VMEM((SEGS, half), F32),
            pltpu.VMEM((2, 1, PIECE - WG0, half), BF),
            pltpu.VMEM((2, 1, (PIECE - WG0) // 2, half), BF),
            pltpu.VMEM((2, 1, (PIECE - WG0) // 4, half), BF),
            pltpu.VMEM((3, n_chan, WG0 - WO0, half), BF),
            pltpu.VMEM((3, n_chan, (WG0 - WO0) // 2, half), BF),
            pltpu.VMEM((3, n_chan, (WG0 - WO0) // 4, half), BF),
            pltpu.VMEM((2, (PIECE - WG0) // 2, half), BF),
            pltpu.VMEM(((PIECE - WG0) // 4, half), BF),
            pltpu.VMEM((4, n_chan - 1, (WG0 - WO0) // 4, half), BF),
            pltpu.VMEM((WG0, width), BF),
            pltpu.VMEM((n_extra, (PIECE + 64) // 4, half) if n_batch > 8 else (1, 16, 128), BF),
            pltpu.VMEM((8, half), F32),
            pltpu.SemaphoreType.DMA((5 + n_chan + 6 * nch // HEAD_CH,)),
            pltpu.SemaphoreType.DMA((7,)),
        ]
        + [pltpu.SemaphoreType.DMA((n_chan,))] * 6
        + [pltpu.SemaphoreType.DMA((5 * (n_chan - 1), 9))] * 2
        + [pltpu.SemaphoreType.DMA((n_chan + 4, 11))] * 2
        + [pltpu.SemaphoreType.DMA((5, 6))] * 2
        + [pltpu.SemaphoreType.DMA((5, n_extra))] * 2,
        compiler_params=pltpu.CompilerParams(
            collective_id=0, has_side_effects=True, vmem_limit_bytes=63 * 2**20
        ),
        cost_estimate=pl.CostEstimate(
            flops=34 * 10**9, bytes_accessed=3 * 10**7, transcendentals=0
        ),
        name="block",
    )(*weights, tokens, cotangent, *vectors, bucket, lengths)


def local(
    tokens, w_in, w_forget, b_forget, rotation, w_outgate, gn_gain, w_out, rms_gain,
    w_gate, w_up, w_down, cotangent, buckets, lengths,
):
    g, grad_tokens, block_out = main_call(
        (w_in.T, w_forget.T, w_outgate.T, w_out, w_gate, w_up, w_down), tokens, cotangent,
        (b_forget[None], rotation[None], gn_gain[None], rms_gain.reshape(-1, 128)), buckets, lengths,
    )
    (
        grad_w_in, grad_w_forget, grad_b, grad_rot, grad_w_outgate, grad_gn, grad_w_out, grad_rms,
        grad_w_gate, grad_w_up, grad_w_down, grad_tokens, block_out,
    ) = post_call(g, grad_tokens, block_out, b_forget.shape[0])
    return (
        block_out, grad_tokens, grad_w_in.T, grad_w_forget.T, grad_b[0], grad_rot[0],
        grad_w_outgate.T, grad_gn[0], grad_w_out, grad_rms[0], grad_w_gate, grad_w_up, grad_w_down,
    )


def solution(mesh):
    both = P(("batch", "chan"), None)
    cols, rows, vec = P(None, "chan"), P("chan", None), P("chan")
    return jax.shard_map(
        local,
        mesh=mesh,
        in_specs=(
            both, cols, cols, vec, vec, cols, vec, rows, P(), cols, cols, rows, both,
            P("batch"), P("batch", None),
        ),
        out_specs=(
            both, both, cols, cols, vec, vec, cols, vec, rows, vec, cols, cols, rows,
        ),
        check_vma=False,
    )
```

```python
import functools

import jax
import jax.numpy as jnp
from jax import lax
from jax.experimental import pallas as pl
from jax.experimental.pallas import tpu as pltpu
from jax.sharding import PartitionSpec as P

MESH = pl.DeviceIdType.MESH
BF = jnp.bfloat16
F32 = jnp.float32
HEAD_CH = 32
SEGS = 16
TM = SEGS * SEGS
ORDER = (0, 1, 3, 2)
PAD0, MA0, WO0, WG0, WD0, PIECE = 288, 320, 512, 704, 1472, 1856
SECTION = (0, 96, 192, 320, 416)


def dot(left, right, left_dim, right_dim):
    return lax.dot_general(
        left, right, (((left_dim,), (right_dim,)), ((), ())), preferred_element_type=F32
    )


def rows_of(tile, size):
    return pl.ds(pl.multiple_of(tile * size, size), size)


def sigmoid(v):
    return 0.5 * jnp.tanh(0.5 * v) + 0.5


def tiles(count, body, steps=None):
    @pl.loop(0, count)
    def _(i):
        for at, calls in (steps or {}).items():

            @pl.when(i == at)
            def _(calls=calls):
                for call in calls:
                    call()

        body(i)


def get(ref, rows, first, count):
    return jnp.concatenate([ref[first + k, rows, :] for k in range(count)], axis=1)


def put(ref, rows, first, v):
    for k in range(v.shape[1] // 128):
        ref[first + k, rows, :] = v[:, 128 * k : 128 * (k + 1)]


def fold_rows(v):
    return jnp.sum(v.reshape(v.shape[0] // 8, 8, v.shape[1]), axis=0)


def main_kernel(
    n_batch, n_chan,
    win_hbm, wf_hbm, wg_hbm, wout_hbm, wgate_hbm, wup_hbm, wdown_hbm, tok_hbm, cot_hbm,
    bias_ref, rot_ref, gn_ref, rms_ref, bucket_ref, len_ref,
    g_hbm, gtok_hbm, out_hbm,
    w, tok, sd, pv, om, pg, ws, xh, rstd, res, fin, mix, out, dff, hid, dgu, dm, dp,
    ones, swap, parx, carx, carb, seg, sgrad, seg_prod,
    rb0, rb1, rb2, mb0, mb1, mb2, zbf, zbq, zbm, mixf, extra,
    par_own,
    load_sem, store_sem, par_send, par_recv, car_send, car_recv, cab_send, cab_recv,
    ag_send, ag_recv, rs_send, rs_recv, fin_send, fin_recv, ex_send, ex_recv,
):
    n_rows, width = tok.shape
    half = width // 2
    lt = half // 128
    n_tiles = n_rows // TM
    seg_len = n_rows // SEGS
    b = lax.axis_index("batch")
    c = lax.axis_index("chan")
    peers = [lax.rem(c + j, n_chan) for j in range(1, n_chan)]
    core = lax.rem(b, 2)
    quarter = lax.rem(b // 2, 4)
    x_bit, y_bit = lax.rem(quarter, 2), quarter // 2

    def flip(bit):
        here = b
        for k in range(n_batch.bit_length()):
            if bit >> k & 1:
                here = here + (1 << k) - (2 << k) * lax.rem(b // (1 << k), 2)
        return here

    core_dev, x_dev, y_dev, diag_dev = ((flip(bit), c) for bit in (1, 2, 4, 6))
    extra_devs = [(flip(1 << k), c) for k in range(3, n_batch.bit_length() - 1)]
    mine = pl.ds(pl.multiple_of(core * half, 128), half)
    theirs = pl.ds(pl.multiple_of((1 - core) * half, 128), half)

    def span(start, size):
        return pl.ds(pl.multiple_of(start, 16), size)

    def remote(src, dst, send_sem, recv_sem, device):
        return pltpu.make_async_remote_copy(
            src, dst, send_sem, recv_sem, device_id=device, device_id_type=MESH
        )

    nch = bias_ref.shape[1]
    heads = nch // HEAD_CH

    def load(src, dst, k):
        copy = pltpu.make_async_copy(src, dst, load_sem.at[k])
        copy.start()
        return copy

    def load_heads(src, first, at):
        return [
            load(
                src.at[HEAD_CH * (2 * hh + part) : HEAD_CH * (2 * hh + part + 1), :],
                w.at[c, pl.ds(first + nch * part + HEAD_CH * hh, HEAD_CH), :],
                at + 2 * hh + part,
            )
            for hh in range(heads)
            for part in range(2)
        ]

    load_first = load_heads(win_hbm, 0, 5 + n_chan) + [load(wf_hbm, w.at[c, pl.ds(2 * nch, nch), :], 0)]
    load_second = (
        load_heads(wg_hbm, MA0, 5 + n_chan + 2 * heads)
        + load_heads(wout_hbm, WO0, 5 + n_chan + 4 * heads)
    )
    load_gate = load(wgate_hbm, hid.at[:width, :], 1)
    load_up = load(wup_hbm, dgu.at[:width, : hid.shape[1]], 2)
    load_down = load(wdown_hbm, w.at[c, WD0:PIECE, :], 3)
    load_tok = load(tok_hbm, fin, 4)
    per = n_rows // n_chan
    load_cot = [
        load(cot_hbm.at[per * k : per * (k + 1), :], dm.at[k, :per, :], 5 + k) for k in range(n_chan)
    ]

    barrier = pltpu.get_barrier_semaphore()
    talk = [core_dev, x_dev, y_dev, diag_dev] + extra_devs + [(b, peer) for peer in peers]
    for device in talk:
        pl.semaphore_signal(barrier, inc=1, device_id=device, device_id_type=MESH)

    w[c, PAD0:MA0, :] = jnp.zeros((MA0 - PAD0, width), BF)
    par_own[...] = jnp.zeros_like(par_own)
    par_own[0:1, :nch] = bias_ref[...]
    par_own[1:2, :nch] = jnp.cos(rot_ref[...])
    par_own[2:3, :nch] = jnp.sin(rot_ref[...])
    for hh in range(heads):
        for part in range(2):
            at = HEAD_CH * (2 * hh + part)
            par_own[3 + part : 4 + part, HEAD_CH * hh : HEAD_CH * (hh + 1)] = gn_ref[
                :, at : at + HEAD_CH
            ]
    parx[c] = pltpu.roll(par_own[...], c * nch, 1)
    pl.semaphore_wait(barrier, len(talk))

    def exchange(ref, send_sem, recv_sem):
        copies = [
            remote(ref.at[c], ref.at[c], send_sem.at[j], recv_sem.at[j], (b, peer))
            for j, peer in enumerate(peers)
        ]
        return copies

    def chain(ref, send_sem, recv_sem, up):
        def each(out, call):
            for k in range(n_chan):
                above = c < k if out == up else c > k
                copy = remote(
                    ref.at[c] if out else ref.at[k], ref.at[c] if out else ref.at[k],
                    send_sem.at[k], recv_sem.at[c] if out else recv_sem.at[k], (b, k),
                )
                pl.when(above)(functools.partial(call, copy))

        def send():
            each(True, lambda copy: copy.start())

        def receive():
            each(False, lambda copy: copy.wait_recv())
            each(True, lambda copy: copy.wait_send())

        return send, receive

    class Gather:
        def __init__(self, unit, j, first, count, turns):
            self.first, self.count, self.turns = first, count, turns
            src = lax.rem(c + j, n_chan)
            peer = lax.rem(c + n_chan - j, n_chan)
            send, recv = ag_send.at[unit], ag_recv.at[unit]

            def copy(k, chan, rows, device):
                ref = w.at[chan, rows, mine]
                return remote(ref, ref, send.at[k], recv.at[k], device)

            from_x = y_bit * 2 + 1 - x_bit
            from_y = (1 - y_bit) * 2 + x_bit
            own = self.rows(quarter)
            self.z = copy(0, c, own, (b, peer))
            self.p1 = [copy(1, src, own, x_dev), copy(2, src, own, y_dev)]
            self.c1 = copy(3, src, own, core_dev)
            if turns:
                cut = count // 4 // 32 * 16
                cut = cut if unit // (n_chan - 1) % 2 else count // 4 - cut
                rest = count // 4 - cut
                self.p2 = [
                    copy(4, src, self.rows(from_x, 0, cut), y_dev),
                    copy(5, src, self.rows(from_y, cut, rest), x_dev),
                ]
            else:
                self.p2 = [copy(4, src, own, diag_dev)]
            self.c2 = [copy(6, src, self.rows(from_x), core_dev),
                       copy(7, src, self.rows(from_y), core_dev)]
            self.c3 = copy(8, src, self.rows(3 - quarter), core_dev)

        def rows(self, part, start=0, size=None):
            size = self.count // 4 if size is None else size
            return span(self.first + part * (self.count // 4) + start, size)

        def along(self):
            self.z.start()

        def plane(self):
            self.z.wait_recv()
            for copy in self.p1 + [self.c1] + ([] if self.turns else self.p2):
                copy.start()

        def turn(self):
            for copy in self.p1:
                copy.wait_recv()
            for copy in (self.p2 if self.turns else []) + self.c2:
                copy.start()

        def cross(self):
            for copy in self.p2:
                copy.wait_recv()
            self.c3.start()

        def ready(self):
            for copy in [self.c1] + self.c2 + [self.c3]:
                copy.wait_recv()

        def along_free(self):
            self.z.wait_send()

        def free(self):
            for copy in self.p1 + self.p2 + [self.c1] + self.c2 + [self.c3]:
                copy.wait_send()

    ring = range(1, n_chan)
    gather_v = [Gather(j - 1, j, 0, 2 * nch, True) for j in ring]
    gather_k = [Gather(11 + j, j, 2 * nch, MA0 - 2 * nch, True) for j in ring]
    gather_b = [Gather(2 + j, j, MA0, WO0 - MA0, True) for j in ring]
    gather_o = [Gather(5 + j, j, WO0, WG0 - WO0, True) for j in ring]
    gather_f = [Gather(8 + j, j, WG0, PIECE - WG0, True) for j in ORDER[1:]]

    place_f = [[buf.at[k] for buf in (rb0, rb1, rb2)] for k in range(2)]
    place_m = [[buf.at[k] for buf in (mb0, mb1, mb2)] for k in (0, 1, 2, 0)]

    class Reduce:
        def __init__(self, chunk, place, ref, dist, first, count, slots, late=False):
            chan = None if dist is None else lax.rem(c + dist, n_chan)
            self.ref, self.slots = ref, slots
            send, recv = rs_send.at[chunk], rs_recv.at[chunk]
            q = count // 4
            cut = q // 32 * 16 if chunk % 2 else q - q // 32 * 16
            rest = q - cut
            chans = pl.ds(0, n_chan) if chan is None else pl.ds(chan, 1)
            n = n_chan if chan is None else 1
            far_x = y_bit * 2 + 1 - x_bit
            far_y = (1 - y_bit) * 2 + x_bit

            def item(k, level, at, part, keep, start, size, cols, device):
                buf = place[level].at[:n, at : at + size, :]
                src = ref.at[chans, span(first + part * q + start, size), cols]
                to = chans, span(first + keep * q + start, size)
                return to, buf, size, remote(src, buf, send.at[k], recv.at[k], device)

            whole = place[0].at[:n, :count, :]
            src = ref.at[chans, first : first + count, theirs]
            self.s0 = [(
                (chans, pl.ds(first, count)), whole, count,
                remote(src, whole, send.at[0], recv.at[0], core_dev),
            )]
            self.s1 = []
            for k in range(2):
                self.s1.append(item(
                    1 + k, 1, k * cut, k * 2 + 1 - x_bit, k * 2 + x_bit, 0, cut, mine, x_dev))
                self.s1.append(item(
                    3 + k, 1, 2 * cut + k * rest, (1 - y_bit) * 2 + k, y_bit * 2 + k, cut, rest,
                    mine, y_dev))
            self.s2 = []
            if not (late and dist):
                self.s2 = [
                    item(5, 2, 0, far_y, quarter, 0, cut, mine, y_dev),
                    item(6, 2, cut, far_x, quarter, cut, rest, mine, x_dev),
                ]
            own = span(first + quarter * q, q)
            self.pairs = [(first + (k * 2 + x_bit) * q, cut, k * cut) for k in range(2)]
            self.pairs += [
                (first + (y_bit * 2 + k) * q + cut, rest, 2 * cut + k * rest) for k in range(2)
            ]
            if late and dist:
                self.s3 = [
                    remote(
                        ref.at[chan, span(start, size), mine],
                        slots.at[dist // 2, at : at + size, :],
                        send.at[7 + k], recv.at[7 + k], (b, chan),
                    )
                    for k, (start, size, at) in enumerate(self.pairs)
                ]
            elif dist:
                self.s3 = [remote(
                    ref.at[chan, own, mine], slots, send.at[7], recv.at[7], (b, chan)
                )]
            else:
                self.s3 = [
                    remote(
                        ref.at[lax.rem(c + j, n_chan), own, mine], slots.at[j - 1],
                        send.at[6 + j], recv.at[6 + j], (b, lax.rem(c + j, n_chan)),
                    )
                    for j in range(1, n_chan)
                    if dist is None
                ]
            self.sent = [it[-1] for it in self.s0 + self.s1 + self.s2] + self.s3

        def add(self, items):
            for (chans, rows), buf, size, copy in items:
                copy.wait_recv()
                step = 96 if buf.shape[0] == 1 else 16
                for at in range(0, size, step):
                    n = min(step, size - at)
                    here = self.ref.at[chans, span(rows.start + at, n), mine]
                    here[...] = here[...] + buf[:, at : at + n, :]

        def to_core(self):
            for item in self.s0:
                item[-1].start()

        def to_plane(self):
            self.add(self.s0)
            for item in self.s1:
                item[-1].start()

        def pair(self):
            self.add(self.s1)

        def send_along(self):
            for copy in self.s3:
                copy.start()

        def pair_along(self):
            self.pair()
            self.send_along()

        def collect(self, copies):
            for copy in copies:
                copy.wait_recv()
            for start, size, at in self.pairs:
                for k in range(0, size, 48):
                    here = span(start + k, 48)
                    v = self.ref[c, here, mine].astype(F32)
                    for j in range(self.slots.shape[0]):
                        v = v + self.slots[j, at + k : at + k + 48, :].astype(F32)
                    self.ref[c, here, mine] = v.astype(BF)
            for item in self.s2:
                item[-1].start()

        def turn(self):
            self.add(self.s1)
            for item in self.s2:
                item[-1].start()

        def along(self):
            self.add(self.s2)
            for copy in self.s3:
                copy.start()

        def free(self):
            for copy in self.sent:
                copy.wait_send()

    class Spread:
        def __init__(self, chunk, ref, first, count, slots, recvs, dest, dest_first, ex_at, turns=False):
            self.ref, self.first, self.q = ref, first, count // 4
            self.slots, self.recvs, self.dest = slots, recvs, dest
            send, recv = fin_send.at[chunk], fin_recv.at[chunk]
            self.at = span(dest_first + quarter * self.q, self.q)
            ref = dest.at[self.at, mine]
            self.copies = [
                remote(ref, ref, send.at[k], recv.at[k], device)
                for k, device in enumerate((x_dev, y_dev) if turns else (x_dev, y_dev, diag_dev))
            ]
            self.p2 = []
            if turns:
                cut = self.q // 32 * 16
                parts = (
                    (y_bit * 2 + 1 - x_bit, 0, cut, y_dev),
                    ((1 - y_bit) * 2 + x_bit, cut, self.q - cut, x_dev),
                )
                for k, (part, start, size, device) in enumerate(parts):
                    half_ref = dest.at[span(dest_first + part * self.q + start, size), mine]
                    self.p2.append(remote(
                        half_ref, half_ref, send.at[4 + k], recv.at[4 + k], device
                    ))
            ref_all = dest.at[dest_first : dest_first + count, mine]
            self.last = remote(ref_all, ref_all, send.at[3], recv.at[3], core_dev)
            self.extra = []
            for k, device in enumerate(extra_devs):
                buf = extra.at[k, ex_at : ex_at + self.q, :]
                self.extra.append((buf, remote(
                    ref, buf, ex_send.at[chunk, k], ex_recv.at[chunk, k], device
                )))

        def total(self):
            for copy in self.recvs:
                copy.wait_recv()
            v = self.ref[c, span(self.first + quarter * self.q, self.q), mine].astype(F32)
            for j in range(len(self.recvs)):
                v = v + self.slots[j][...].astype(F32)
            self.dest[self.at, mine] = v.astype(BF)
            for buf, copy in self.extra:
                copy.start()
                copy.wait()
                v = self.dest[self.at, mine].astype(F32) + buf[...].astype(F32)
                self.dest[self.at, mine] = v.astype(BF)
            for copy in self.copies:
                copy.start()

        def turn(self):
            for copy in self.copies:
                copy.wait_recv()
            for copy in self.p2:
                copy.start()

        def cross(self):
            for copy in self.p2 or self.copies:
                copy.wait_recv()
            self.last.start()

        def done(self):
            self.last.wait_recv()
            for copy in self.copies + self.p2 + [self.last]:
                copy.wait_send()

    f_rows = PIECE - WG0
    reduce_f = [
        Reduce(k, place_f[k % 2], w, j, WG0, f_rows, zbf if j != 2 else zbq, j != 2)
        for k, j in enumerate(ORDER)
    ]
    reduce_o = Reduce(n_chan, place_m[0], sd, None, 0, WG0 - WO0, zbm.at[0])
    reduce_g = Reduce(n_chan + 1, place_m[1], w, None, WO0, WO0 - MA0, zbm.at[1])
    reduce_v = Reduce(n_chan + 2, place_m[2], dm, None, 0, 2 * nch, zbm.at[2])
    reduce_k = Reduce(
        n_chan + 3, place_m[3], dm, None, 2 * nch, MA0 - 2 * nch,
        zbm.at[3, :, : (MA0 - 2 * nch) // 4],
    )
    spread_f = Spread(0, w, WG0, f_rows, [zbq], reduce_f[-1].s3, dgu, 0, 0, True)
    at = [f_rows // 4 + k * (nch // 2) for k in range(4)]
    spread_o = Spread(1, sd, 0, WG0 - WO0, zbm.at[0], reduce_o.s3, mixf, WO0, at[0])
    spread_g = Spread(2, w, WO0, WO0 - MA0, zbm.at[1], reduce_g.s3, mixf, MA0, at[1])
    spread_v = Spread(3, dm, 0, 2 * nch, zbm.at[2], reduce_v.s3, mixf, 0, at[2])
    spread_k = Spread(
        4, dm, 2 * nch, MA0 - 2 * nch, zbm.at[3, :, : (MA0 - 2 * nch) // 4], reduce_k.s3, mixf,
        2 * nch, at[3],
    )

    for copy in load_first:
        copy.wait()
    par_copies = exchange(parx, par_send, par_recv)
    for copy in par_copies:
        copy.start()
    for g in gather_v + gather_k:
        g.along()
    for copy in load_second:
        copy.wait()
    hw = hid.shape[1]
    load_gate.wait()
    w[c, WG0 : WG0 + hw, :] = hid[:width, :].T
    load_up.wait()
    w[c, WG0 + hw : WD0, :] = dgu[:width, :hw].T
    load_down.wait()
    lane_r = lax.broadcasted_iota(jnp.int32, (half, half), 0) // HEAD_CH
    lane_c = lax.broadcasted_iota(jnp.int32, (half, half), 1) // HEAD_CH
    ones[...] = jnp.where(lane_r == lane_c, 1.0 / (2 * HEAD_CH), 0.0).astype(BF)
    sgrad[...] = jnp.zeros_like(sgrad)
    row = lax.broadcasted_iota(jnp.int32, (TM, TM), 0)
    col = lax.broadcasted_iota(jnp.int32, (TM, TM), 1)
    swap[...] = jnp.where(row == lax.rem(col, SEGS) * SEGS + col // SEGS, 1.0, 0.0).astype(BF)

    def blocks(i):
        return [span(seg_len * k + SEGS * i, SEGS) for k in range(SEGS)]

    def head_mean(v, exact=False):
        high = v.astype(BF)
        if not exact:
            return dot(high, ones[...], 1, 0)
        low = (v - high.astype(F32)).astype(BF)
        return dot(high, ones[...], 1, 0) + dot(low, ones[...], 1, 0)

    bucket = bucket_ref[0]
    base = c * n_rows
    offset = jnp.bitwise_and(base, bucket - 1)
    slot_limit = len_ref[0, 0]
    for k in range(1, len_ref.shape[1]):
        slot_limit = jnp.where(base >= k * bucket, len_ref[0, k], slot_limit)
    live_rows = slot_limit - offset
    not_start = jnp.where(offset == 0, 0.0, 1.0).astype(F32)

    def section(k):
        return jnp.concatenate(
            [w[cc, SECTION[k] : SECTION[k] + 96, :] for cc in range(n_chan)], axis=0
        )

    def out_rows(k):
        return jnp.concatenate(
            [w[cc, WO0 + 96 * k : WO0 + 96 * k + 96, :] for cc in range(n_chan)], axis=0
        )

    def order_tokens(i):
        part = jnp.concatenate([fin[at, :] for at in blocks(i)], axis=0)
        tok[rows_of(i, TM), :] = dot(swap[...], part, 1, 0).astype(BF)

    def order_seed(i):
        part = jnp.concatenate(
            [
                dm[k, span(seg_len * m + SEGS * i, SEGS), :]
                for k in range(n_chan)
                for m in range(SEGS // n_chan)
            ],
            axis=0,
        ).astype(F32)
        k = lax.broadcasted_iota(jnp.int32, (TM, 1), 0)
        place = k // SEGS * seg_len + lax.rem(k, SEGS) + SEGS * i
        part = (part * jnp.where(place < live_rows, 1.0, 0.0)).astype(BF)
        sd[i] = dot(swap[...], part, 1, 0).astype(BF)

    load_tok.wait()
    tiles(n_tiles, order_tokens)
    for g in gather_v:
        g.plane()
    for copy in load_cot:
        copy.wait()
    tiles(n_tiles, order_seed)
    for g in gather_k:
        g.plane()
    for g in gather_b + gather_o + gather_f[:2]:
        g.along()
    for g in gather_v:
        g.turn()
    for g in gather_k:
        g.turn()
    for g in gather_v:
        g.cross()
    for g in gather_k:
        g.cross()
    for g in gather_v:
        g.ready()

    for copy in par_copies:
        copy.wait()
    par = parx[0] + parx[1] + parx[2] + parx[3]
    bias = par[0:1, :]
    cos1, sin1 = par[1:2, :], par[2:3, :]
    gain_r, gain_i = par[3:4, :], par[4:5, :]
    rms_gain = jnp.concatenate([rms_ref[k : k + 1, :] for k in range(width // 128)], axis=1)
    cos16 = jnp.broadcast_to(cos1, (SEGS, half))
    sin16 = jnp.broadcast_to(sin1, (SEGS, half))

    def power(count):
        rr, ri = cos1, sin1
        while count > 1:
            rr, ri = rr * rr - ri * ri, 2.0 * rr * ri
            count //= 2
        return rr, ri

    seg_cos, seg_sin = power(seg_len)
    all_cos, all_sin = power(n_rows)

    def project(i):
        rows = rows_of(i, TM)
        x = tok[rows, :]
        for k in range(2):
            pre = dot(x, section(k), 1, 1)
            pv[rows, k * half : (k + 1) * half] = pre
            put(out, rows, k * lt, pre * sigmoid(pre))

    def project_forget(i):
        rows = rows_of(i, TM)
        pre = dot(tok[rows, :], section(2), 1, 1) + bias
        put(om, rows, 0, 1.0 / (1.0 + jnp.exp(pre)))

    tiles(n_tiles, project, {1: [g.plane for g in gather_b]})
    for g in gather_k:
        g.ready()
    tiles(n_tiles, project_forget, {1: [g.plane for g in gather_o]})

    def strided(t):
        return span(t * SEGS, SEGS)

    def first(t, carry):
        sr, si, prod = carry
        o = get(om, strided(t), 0, lt)
        f = 1.0 - o
        vr = get(out, strided(t), 0, lt)
        vi = get(out, strided(t), lt, lt)
        tr = cos16 * sr - sin16 * si
        ti = sin16 * sr + cos16 * si
        return f * tr + o * vr, f * ti + o * vi, prod * f

    zero = jnp.zeros((SEGS, half), F32)
    end_r, end_i, prod = lax.fori_loop(
        0, seg_len, first, (zero, zero, jnp.ones((SEGS, half), F32)), unroll=4
    )
    seg[0] = end_r
    seg[1] = end_i
    seg_prod[...] = prod

    def fold_forward(cr, ci, keep):
        total = jnp.ones((1, half), F32)
        for s in range(SEGS):
            if keep:
                seg[2, s : s + 1, :] = cr
                seg[3, s : s + 1, :] = ci
            p = seg_prod[s : s + 1, :]
            ar, ai = p * seg_cos, p * seg_sin
            cr, ci = (
                ar * cr - ai * ci + seg[0, s : s + 1, :],
                ar * ci + ai * cr + seg[1, s : s + 1, :],
            )
            total = total * p
        return cr, ci, total

    zrow = jnp.zeros((1, half), F32)
    er, ei, total = fold_forward(zrow, zrow, False)
    carx[c, 0:1, :] = er
    carx[c, 1:2, :] = ei
    carx[c, 2:3, :] = total * all_cos * not_start
    carx[c, 3:4, :] = total * all_sin * not_start
    to_later, from_earlier = chain(carx, car_send, car_recv, True)
    to_later()
    for g in gather_b:
        g.turn()
    for g in gather_o:
        g.turn()
    gather_f[0].plane()
    for g in gather_b:
        g.cross()
    from_earlier()
    gather_f[2].along()
    cr, ci = zrow, zrow
    for k in range(n_chan - 1):
        ar, ai = carx[k, 2:3, :], carx[k, 3:4, :]
        nr = ar * cr - ai * ci + carx[k, 0:1, :]
        ni = ar * ci + ai * cr + carx[k, 1:2, :]
        cr = jnp.where(k < c, nr, cr)
        ci = jnp.where(k < c, ni, ci)
    fold_forward(cr * not_start, ci * not_start, True)

    def second(t, carry):
        sr, si = carry
        o = get(om, strided(t), 0, lt)
        f = 1.0 - o
        vr = get(out, strided(t), 0, lt)
        vi = get(out, strided(t), lt, lt)
        tr = cos16 * sr - sin16 * si
        ti = sin16 * sr + cos16 * si
        put(ws, strided(t), 0, tr)
        put(ws, strided(t), lt, ti)
        return f * tr + o * vr, f * ti + o * vi

    lax.fori_loop(0, seg_len, second, (seg[2], seg[3]), unroll=4)
    for g in gather_b:
        g.ready()

    def project_gate(i):
        rows = rows_of(i, TM)
        x = tok[rows, :]
        for k in range(2):
            pg[rows, k * half : (k + 1) * half] = dot(x, section(3 + k), 1, 1)

    tiles(n_tiles, project_gate, {2: [g.cross for g in gather_o]})
    for g in gather_o:
        g.ready()

    def mixer_out(i):
        rows = rows_of(i, TM)
        o = get(om, rows, 0, lt)
        f = 1.0 - o
        gr, gi = pg[rows, :half], pg[rows, half:]
        yr = gr * sigmoid(gr) * (f * get(ws, rows, 0, lt) + o * get(out, rows, 0, lt))
        yi = gi * sigmoid(gi) * (f * get(ws, rows, lt, lt) + o * get(out, rows, lt, lt))
        mean = head_mean(yr + yi, True)
        yr, yi = yr - mean, yi - mean
        inv = lax.rsqrt(head_mean(yr * yr + yi * yi) + 1e-5)
        yr, yi = yr * inv, yi * inv
        rstd[rows, :] = inv
        xh[rows, :half] = yr.astype(BF)
        xh[rows, half:] = yi.astype(BF)
        lr, li = (yr * gain_r).astype(BF), (yi * gain_i).astype(BF)
        mix[rows, :half] = lr
        mix[rows, half:] = li
        r = tok[rows, :].astype(F32) + (
            dot(lr, out_rows(0), 1, 0) + dot(li, out_rows(1), 1, 0)
        )
        res[rows, :] = r
        put(out, rows, 0, r)
        rinv = lax.rsqrt(jnp.mean(r * r, axis=1, keepdims=True) + 1e-6)
        fin[rows, :] = (r * rinv * rms_gain).astype(BF)
        dff[rows, :] = jnp.zeros((TM, width), F32)

    tiles(n_tiles, mixer_out, {
        1: [gather_f[0].turn],
        2: [gather_f[1].plane],
    })

    for j in range(n_chan):
        cc = lax.rem(c + ORDER[j], n_chan)

        def feed(i, cc=cc):
            rows = rows_of(i, 2 * TM)
            gate_up = dot(fin[rows, :], w[cc, WG0:WD0, :], 1, 1)
            d_hid = dot(jnp.concatenate([sd[2 * i], sd[2 * i + 1]], axis=0), w[cc, WD0:PIECE, :], 1, 1)
            gate, up = gate_up[:, :hw], gate_up[:, hw:]
            sig = sigmoid(gate)
            act = gate * sig
            h = (act * up).astype(BF)
            hid[rows, :] = h
            dg = (d_hid * up * (sig + act * (1.0 - sig))).astype(BF)
            du = (d_hid * act).astype(BF)
            dgu[rows, :hw] = dg
            dgu[rows, hw:] = du
            put(out, rows, 0, get(out, rows, 0, 2 * lt) + dot(h, w[cc, WD0:PIECE, :], 1, 0))
            dff[rows, :] += dot(dgu[rows, :], w[cc, WG0:WD0, :], 1, 0)

        if j == 0:
            tiles(n_tiles // 2, feed, {1: [gather_f[0].cross]})
            gather_f[1].turn()
            for g in gather_f:
                g.along_free()
            gather_f[0].ready()
        else:
            before = reduce_f[j - 1]
            older = [reduce_f[j - 2]] if j > 1 else []
            if j > 1:
                gather_f[j - 1].ready()
            tiles(n_tiles // 2, feed, {
                1: ([gather_f[1].cross] if j == 1 else [])
                + [r.pair_along for r in older] + [before.to_plane],
            })
            if j == 2:
                gather_f[2].cross()
            gather_f[j - 1].free()
        for k in range(2):
            w[cc, WG0 + hw * k : WG0 + hw * (k + 1), :] = dot(
                dgu[:n_rows, hw * k : hw * (k + 1)], fin[...], 0, 0
            ).astype(BF)
        seeds = jnp.concatenate([sd[k] for k in range(n_tiles)], axis=0)
        if j == 1:
            gather_f[2].turn()
        w[cc, WD0:PIECE, :] = dot(hid[...], seeds, 0, 0).astype(BF)
        reduce_f[j].to_core()
        if j == 0:
            gather_f[2].plane()

    def norm_back(i):
        rows = rows_of(i, TM)
        fin[rows, :] = get(out, rows, 0, 2 * lt).astype(BF)
        r = res[rows, :]
        rinv = lax.rsqrt(jnp.mean(r * r, axis=1, keepdims=True) + 1e-6)
        rhat = r * rinv
        d = dff[rows, :]
        sgrad[2] += fold_rows(d * rhat)
        t = d * rms_gain
        dres = sd[i].astype(F32) + rinv * (
            t - rhat * jnp.mean(t * rhat, axis=1, keepdims=True)
        )
        dff[rows, :] = dres
        dm[i, :TM, :] = dres.astype(BF)

    tiles(n_tiles, norm_back)
    reduce_f[-2].pair()
    d_mixed = jnp.concatenate([dm[k, :TM, :] for k in range(n_tiles)], axis=0)
    for k in range(2):
        grad = dot(mix[:, k * half : (k + 1) * half], d_mixed, 0, 0).astype(BF)
        for cc in range(n_chan):
            sd[cc, 96 * k : 96 * k + 96, :] = grad[96 * cc : 96 * cc + 96, :]
    reduce_o.to_core()
    reduce_f[-1].to_plane()

    def mixer_back(i):
        rows = rows_of(i, TM)
        low = dm[i, :TM, :]
        dr = dot(low, out_rows(0), 1, 1)
        di = dot(low, out_rows(1), 1, 1)
        xr, xi = xh[rows, :half].astype(F32), xh[rows, half:].astype(F32)
        sgrad[1, :, :half] += fold_rows(dr * xr)
        sgrad[1, :, half:] += fold_rows(di * xi)
        dr, di = dr * gain_r, di * gain_i
        m1 = head_mean(dr + di)
        m2 = head_mean(dr * xr + di * xi)
        inv = rstd[rows, :]
        dr = inv * (dr - m1 - xr * m2)
        di = inv * (di - m1 - xi * m2)
        o = get(om, rows, 0, lt)
        f = 1.0 - o
        for k, dy in ((0, dr), (1, di)):
            cols = slice(k * half, (k + 1) * half)
            pre = pv[rows, cols]
            state = f * get(ws, rows, k * lt, lt) + o * (pre * sigmoid(pre))
            g = pg[rows, cols]
            sig = sigmoid(g)
            act = g * sig
            dp[rows, (3 + k) * half : (4 + k) * half] = (
                dy * state * (sig + act * (1.0 - sig))
            ).astype(BF)
            put(out, rows, k * lt, dy * act)
    tiles(n_tiles, mixer_back, {2: [reduce_o.to_plane]})

    def collect_f():
        reduce_f[0].collect([copy for r in reduce_f[1:-1] for copy in r.s3])

    def own_f():
        reduce_f[0].add(reduce_f[0].s2)

    def first_back(k, carry):
        qr, qi = carry
        t = seg_len - 1 - k
        f = 1.0 - get(om, strided(t), 0, lt)
        lr = get(out, strided(t), 0, lt) + qr
        li = get(out, strided(t), lt, lt) + qi
        return f * (cos16 * lr + sin16 * li), f * (cos16 * li - sin16 * lr)

    qr, qi = lax.fori_loop(0, seg_len, first_back, (zero, zero), unroll=4)
    seg[0] = qr
    seg[1] = qi

    def fold_back(cr, ci, keep):
        for s in range(SEGS - 1, -1, -1):
            if keep:
                seg[2, s : s + 1, :] = cr
                seg[3, s : s + 1, :] = ci
            p = seg_prod[s : s + 1, :]
            ar, ai = p * seg_cos, -(p * seg_sin)
            cr, ci = (
                ar * cr - ai * ci + seg[0, s : s + 1, :],
                ar * ci + ai * cr + seg[1, s : s + 1, :],
            )
        return cr, ci

    er, ei = fold_back(zrow, zrow, False)
    carb[c, 0:1, :] = er * not_start
    carb[c, 1:2, :] = ei * not_start
    carb[c, 2:4, :] = carx[c, 2:4, :]
    to_earlier, from_later = chain(carb, cab_send, cab_recv, False)
    to_earlier()
    reduce_f[-2].send_along()

    for g in gather_v + gather_k + gather_b + gather_o:
        g.along_free()
        g.free()
    for k in range(2):
        grad = dot(dp[:, (3 + k) * half : (4 + k) * half], tok[...], 0, 0).astype(BF)
        for cc in range(n_chan):
            at = WO0 + 96 * k
            w[cc, at : at + 96, :] = grad[96 * cc : 96 * cc + 96, :]
    reduce_g.to_core()
    reduce_f[-1].turn()

    from_later()
    cr, ci = zrow, zrow
    for k in range(n_chan - 1, 0, -1):
        ar, ai = carb[k, 2:3, :], -carb[k, 3:4, :]
        nr = ar * cr - ai * ci + carb[k, 0:1, :]
        ni = ar * ci + ai * cr + carb[k, 1:2, :]
        cr = jnp.where(k > c, nr, cr)
        ci = jnp.where(k > c, ni, ci)
    fold_back(cr, ci, True)

    def second_back(k, carry):
        qr, qi = carry
        t = seg_len - 1 - k
        f = 1.0 - get(om, strided(t), 0, lt)
        lr = get(out, strided(t), 0, lt) + qr
        li = get(out, strided(t), lt, lt) + qi
        put(out, strided(t), 0, lr)
        put(out, strided(t), lt, li)
        return f * (cos16 * lr + sin16 * li), f * (cos16 * li - sin16 * lr)

    lax.fori_loop(0, seg_len, second_back, (seg[2], seg[3]), unroll=4)
    def project_back(i):
        rows = rows_of(i, TM)
        o = get(om, rows, 0, lt)
        f = 1.0 - o
        df = jnp.zeros((TM, half), F32)
        for k in range(2):
            cols = slice(k * half, (k + 1) * half)
            pre = pv[rows, cols]
            sig = sigmoid(pre)
            act = pre * sig
            lam = get(out, rows, k * lt, lt)
            df += lam * (get(ws, rows, k * lt, lt) - act)
            dp[rows, cols] = (o * lam * (sig + act * (1.0 - sig))).astype(BF)
        dx = df * f * o
        dp[rows, 2 * half : 3 * half] = dx.astype(BF)
        sgrad[0, :, :half] += fold_rows(dx)
        sgrad[0, :, half:] += fold_rows(
            f
            * (
                get(out, rows, lt, lt) * get(ws, rows, 0, lt)
                - get(out, rows, 0, lt) * get(ws, rows, lt, lt)
            )
        )

    tiles(n_tiles, project_back, {3: [reduce_f[-1].along]})
    reduce_o.turn()
    for k in range(3):
        grad = dot(dp[:, k * half : (k + 1) * half], tok[...], 0, 0).astype(BF)
        for cc in range(n_chan):
            dm[cc, 96 * k : 96 * k + 96, :] = grad[96 * cc : 96 * cc + 96, :]
        if k == 1:
            reduce_v.to_core()
            reduce_g.to_plane()
    small = jnp.concatenate(
        [jnp.sum(sgrad[k], axis=0, keepdims=True) for k in range(3)]
        + [jnp.zeros((29, width), F32)],
        axis=0,
    ).astype(BF)
    for cc in range(n_chan):
        dm[cc, PAD0:MA0, :] = small
    reduce_k.to_core()
    def order_out(i):
        done = dot(swap[...], fin[rows_of(i, TM), :], 1, 0).astype(BF)
        for k, at in enumerate(blocks(i)):
            mix[at, :] = done[SEGS * k : SEGS * (k + 1), :]

    def d_tokens(i):
        rows = rows_of(i, TM)
        acc = dff[rows, :]
        for k in range(5):
            acc += dot(dp[rows, k * half : (k + 1) * half], section(k), 1, 0)
        high = acc.astype(BF)
        low = (acc - high.astype(F32)).astype(BF)
        done = dot(swap[...], high, 1, 0) + dot(swap[...], low, 1, 0)
        for k, at in enumerate(blocks(i)):
            res[at, :] = done[SEGS * k : SEGS * (k + 1), :]

    tiles(n_tiles, d_tokens, {
        0: [reduce_o.along],
        1: [reduce_v.to_plane],
        2: [reduce_k.to_plane],
    })
    gtok_copy = pltpu.make_async_copy(res, gtok_hbm, store_sem.at[1])
    gtok_copy.start()
    reduce_v.turn()
    collect_f()
    reduce_k.turn()
    reduce_g.turn()
    own_f()
    spread_f.total()
    reduce_v.along()
    spread_o.total()
    reduce_k.along()
    tiles(n_tiles, order_out)
    out_copy = pltpu.make_async_copy(mix, out_hbm, store_sem.at[0])
    out_copy.start()
    reduce_g.along()
    spread_f.turn()
    spread_v.total()
    spread_k.total()
    spread_f.cross()
    spread_o.cross()
    spread_g.total()
    for sp in (spread_v, spread_k, spread_g):
        sp.cross()
    g_copies = []

    def leave(sp, src, rows):
        sp.done()
        copy = pltpu.make_async_copy(src, g_hbm.at[rows, :], store_sem.at[2 + len(g_copies)])
        copy.start()
        g_copies.append(copy)

    leave(spread_f, dgu, pl.ds(WG0, PIECE - WG0))
    for sp, lo, hi in (
        (spread_o, WO0, WG0), (spread_v, 0, 2 * nch), (spread_k, 2 * nch, MA0), (spread_g, MA0, WO0)
    ):
        leave(sp, mixf.at[lo:hi, :], pl.ds(lo, hi - lo))
    for r in reduce_f + [reduce_o, reduce_g, reduce_v, reduce_k]:
        r.free()
    for copy in [out_copy, gtok_copy] + g_copies:
        copy.wait()


def post_kernel(
    g_hbm, gtok_hbm, out_hbm,
    win_ref, wf_ref, bf_ref, rot_ref, wg_ref, gn_ref, wout_ref, rms_ref, gate_ref, up_ref,
    down_ref, gtok_ref, out_ref,
    g, t_in, t_f, t_g, t_out, t_gate, t_up, t_down, t_gtok, t_block, rows8, load_sem, store_sem,
):
    nch = bf_ref.shape[1]
    heads = nch // HEAD_CH
    hw = (WD0 - WG0) // 2
    half = g.shape[1] // 2
    c = lax.axis_index("chan")
    cuts = (0, MA0, WG0, WG0 + hw, WD0, PIECE)
    loads = []
    for k in range(5):
        rows = pl.ds(cuts[k], cuts[k + 1] - cuts[k])
        loads.append(pltpu.make_async_copy(g_hbm.at[rows, :], g.at[rows, :], load_sem.at[k]))
        loads[-1].start()
    through = []
    for src, mid, dst in ((gtok_hbm, t_gtok, gtok_ref), (out_hbm, t_block, out_ref)):
        n = mid.shape[0] // 4
        for k in range(4):
            rows = pl.ds(n * k, n)
            sem = load_sem.at[5 + len(through)]
            through.append((
                pltpu.make_async_copy(src.at[rows, :], mid.at[rows, :], sem),
                mid.at[rows, :], dst.at[rows, :],
            ))
            through[-1][0].start()
    stores = []

    def store(src, dst):
        copy = pltpu.make_async_copy(src, dst, store_sem.at[len(stores)])
        copy.start()
        stores.append(copy)

    def pass_on(count):
        for _ in range(count):
            copy, mid, dst = through.pop(0)
            copy.wait()
            store(mid, dst)

    def joined(first):
        return jnp.concatenate(
            [
                g[first + nch * part + HEAD_CH * hh : first + nch * part + HEAD_CH * (hh + 1), :]
                for hh in range(heads)
                for part in range(2)
            ],
            axis=0,
        )

    loads[0].wait()
    t_in[...] = joined(0).astype(F32)
    store(t_in, win_ref)
    t_f[...] = g[2 * nch : 3 * nch, :].astype(F32)
    store(t_f, wf_ref)
    small = g[PAD0 : PAD0 + 16, :].astype(F32)
    turn = lax.rem(4 - c, 4) * nch
    rows8[0:8, :half] = pltpu.roll(small[0:8, :half], turn, 1)
    rows8[0:8, half:] = pltpu.roll(small[0:8, half:], turn, 1)
    bf_ref[...] = rows8[0:1, :nch]
    rot_ref[...] = rows8[0:1, half : half + nch]
    for hh in range(heads):
        for part in range(2):
            at = half * part + HEAD_CH * hh
            to = HEAD_CH * (2 * hh + part)
            gn_ref[:, to : to + HEAD_CH] = rows8[1:2, at : at + HEAD_CH]
    rows8[8:16, :] = pltpu.roll(small[0:8, :], 2 * turn, 1)
    rms_ref[...] = rows8[10:11, : 2 * nch]
    pass_on(1)
    loads[1].wait()
    t_g[...] = joined(MA0).astype(F32)
    store(t_g, wg_ref)
    t_out[...] = joined(WO0).astype(F32)
    store(t_out, wout_ref)
    pass_on(2)
    loads[2].wait()
    t_gate[...] = g[WG0 : WG0 + hw, :].T.astype(F32)
    store(t_gate, gate_ref)
    pass_on(2)
    loads[3].wait()
    t_up[...] = g[WG0 + hw : WD0, :].T.astype(F32)
    store(t_up, up_ref)
    pass_on(2)
    loads[4].wait()
    t_down[...] = g[WD0:PIECE, :].astype(F32)
    store(t_down, down_ref)
    pass_on(1)
    for copy in stores:
        copy.wait()


def post_call(g, grad_tokens, block_out, nch):
    width = g.shape[1]
    hw = (WD0 - WG0) // 2
    any_spec = pl.BlockSpec(memory_space=pl.ANY)
    vmem = pl.BlockSpec(memory_space=pltpu.VMEM)
    big = [(2 * nch, width), (nch, width), (2 * nch, width), (2 * nch, width), (width, hw),
           (width, hw), (hw, width)]
    shapes = [big[0], big[1], (1, nch), (1, nch), big[2], (1, 2 * nch), big[3], (1, 2 * nch),
              big[4], big[5], big[6], grad_tokens.shape]
    return pl.pallas_call(
        post_kernel,
        out_shape=[jax.ShapeDtypeStruct(shape, F32) for shape in shapes]
        + [jax.ShapeDtypeStruct(block_out.shape, BF)],
        in_specs=[any_spec] * 3,
        out_specs=[vmem if shape[0] == 1 else any_spec for shape in shapes] + [any_spec],
        scratch_shapes=[pltpu.VMEM(g.shape, BF)]
        + [pltpu.VMEM(shape, F32) for shape in big + [grad_tokens.shape]]
        + [
            pltpu.VMEM(block_out.shape, BF),
            pltpu.VMEM((16, width), F32),
            pltpu.SemaphoreType.DMA((13,)),
            pltpu.SemaphoreType.DMA((15,)),
        ],
        compiler_params=pltpu.CompilerParams(vmem_limit_bytes=60 * 2**20),
        name="place",
    )(g, grad_tokens, block_out)


def main_call(weights, tokens, cotangent, vectors, bucket, lengths):
    rows, width = tokens.shape
    half = width // 2
    nch = vectors[0].shape[1]
    n_chan, n_batch = lax.axis_size("chan"), lax.axis_size("batch")
    n_extra = max(1, n_batch.bit_length() - 4)
    w_shape = (n_chan, PIECE, width)
    hw = (WD0 - WG0) // 2
    any_spec = pl.BlockSpec(memory_space=pl.ANY)
    vmem = pl.BlockSpec(memory_space=pltpu.VMEM)
    smem = pl.BlockSpec(memory_space=pltpu.SMEM)
    full32 = pltpu.VMEM((rows, width), F32)
    half32 = pltpu.VMEM((rows, half), F32)
    tiles32 = pltpu.VMEM((width // 128, rows, 128), F32)
    full16 = pltpu.VMEM((rows, width), BF)
    return pl.pallas_call(
        functools.partial(main_kernel, n_batch, n_chan),
        out_shape=[
            jax.ShapeDtypeStruct((PIECE, width), BF),
            jax.ShapeDtypeStruct((rows, width), F32),
            jax.ShapeDtypeStruct((rows, width), BF),
        ],
        in_specs=[any_spec] * 9 + [vmem] * 4 + [smem, smem],
        out_specs=[any_spec] * 3,
        scratch_shapes=[
            pltpu.VMEM(w_shape, BF),
            full16, pltpu.VMEM((rows // TM, TM, width), BF), full32,
            pltpu.VMEM((half // 128, rows, 128), F32), full32, tiles32,
            full16, half32, full32, full16, full16, tiles32, full32,
            pltpu.VMEM((rows, hw), BF), pltpu.VMEM((PIECE - WG0, 2 * hw), BF),
            pltpu.VMEM((n_chan, MA0, width), BF), pltpu.VMEM((rows, 5 * half), BF),
            pltpu.VMEM((half, half), BF),
            pltpu.VMEM((TM, TM), BF),
            pltpu.VMEM((n_chan, 8, half), F32),
            pltpu.VMEM((n_chan, 8, half), F32),
            pltpu.VMEM((n_chan, 8, half), F32),
            pltpu.VMEM((4, SEGS, half), F32),
            pltpu.VMEM((3, 8, width), F32),
            pltpu.VMEM((SEGS, half), F32),
            pltpu.VMEM((2, 1, PIECE - WG0, half), BF),
            pltpu.VMEM((2, 1, (PIECE - WG0) // 2, half), BF),
            pltpu.VMEM((2, 1, (PIECE - WG0) // 4, half), BF),
            pltpu.VMEM((3, n_chan, WG0 - WO0, half), BF),
            pltpu.VMEM((3, n_chan, (WG0 - WO0) // 2, half), BF),
            pltpu.VMEM((3, n_chan, (WG0 - WO0) // 4, half), BF),
            pltpu.VMEM((2, (PIECE - WG0) // 2, half), BF),
            pltpu.VMEM(((PIECE - WG0) // 4, half), BF),
            pltpu.VMEM((4, n_chan - 1, (WG0 - WO0) // 4, half), BF),
            pltpu.VMEM((WG0, width), BF),
            pltpu.VMEM((n_extra, (PIECE + 64) // 4, half) if n_batch > 8 else (1, 16, 128), BF),
            pltpu.VMEM((8, half), F32),
            pltpu.SemaphoreType.DMA((5 + n_chan + 6 * nch // HEAD_CH,)),
            pltpu.SemaphoreType.DMA((7,)),
        ]
        + [pltpu.SemaphoreType.DMA((n_chan,))] * 6
        + [pltpu.SemaphoreType.DMA((5 * (n_chan - 1), 9))] * 2
        + [pltpu.SemaphoreType.DMA((n_chan + 4, 11))] * 2
        + [pltpu.SemaphoreType.DMA((5, 6))] * 2
        + [pltpu.SemaphoreType.DMA((5, n_extra))] * 2,
        compiler_params=pltpu.CompilerParams(
            collective_id=0, has_side_effects=True, vmem_limit_bytes=63 * 2**20
        ),
        cost_estimate=pl.CostEstimate(
            flops=34 * 10**9, bytes_accessed=3 * 10**7, transcendentals=0
        ),
        name="block",
    )(*weights, tokens, cotangent, *vectors, bucket, lengths)


def local(
    tokens, w_in, w_forget, b_forget, rotation, w_outgate, gn_gain, w_out, rms_gain,
    w_gate, w_up, w_down, cotangent, buckets, lengths,
):
    g, grad_tokens, block_out = main_call(
        (w_in.T, w_forget.T, w_outgate.T, w_out, w_gate, w_up, w_down), tokens, cotangent,
        (b_forget[None], rotation[None], gn_gain[None], rms_gain.reshape(-1, 128)), buckets, lengths,
    )
    (
        grad_w_in, grad_w_forget, grad_b, grad_rot, grad_w_outgate, grad_gn, grad_w_out, grad_rms,
        grad_w_gate, grad_w_up, grad_w_down, grad_tokens, block_out,
    ) = post_call(g, grad_tokens, block_out, b_forget.shape[0])
    return (
        block_out, grad_tokens, grad_w_in.T, grad_w_forget.T, grad_b[0], grad_rot[0],
        grad_w_outgate.T, grad_gn[0], grad_w_out, grad_rms[0], grad_w_gate, grad_w_up, grad_w_down,
    )


def solution(mesh):
    both = P(("batch", "chan"), None)
    cols, rows, vec = P(None, "chan"), P("chan", None), P("chan")
    return jax.shard_map(
        local,
        mesh=mesh,
        in_specs=(
            both, cols, cols, vec, vec, cols, vec, rows, P(), cols, cols, rows, both,
            P("batch"), P("batch", None),
        ),
        out_specs=(
            both, both, cols, cols, vec, vec, cols, vec, rows, vec, cols, cols, rows,
        ),
        check_vma=False,
    )
```
